32 devices in a mesh: dp: 8 (over y, x, core), fsdp: 4 (over z).
Axes of the slice: x: 2, y: 2, z: 4, core: 2. Of those that a mesh axis runs over, the one named last changes fastest.
Arguments:
- acts: bfloat16 [4096, 4096], P(('dp', 'fsdp')), may hold values from -6 to 6
- cotangent: bfloat16 [4096, 512], P(('dp', 'fsdp')), may hold values from -6 to 6
- tenant: int32 [4096], P(('dp', 'fsdp')), may hold values from 0 to 63, as said below
- advantage: int32 [4096], P(('dp', 'fsdp')), may hold values from -8 to 8
- base_weight: bfloat16 [4096, 512], P('fsdp'), may hold values from -0.25 to 0.25
- a_param: float32 [4096, 2048], P('fsdp', 'dp'), may hold values from -6 to 6
- a_moment: float32 [4096, 2048], P('fsdp', 'dp'), may hold values from -6 to 6
- a_second: float32 [4096, 2048], P('fsdp', 'dp'), may hold values from 0.1 to 10
- b_param: float32 [2048, 512], P(('dp', 'fsdp')), may hold values from -6 to 6
- b_moment: float32 [2048, 512], P(('dp', 'fsdp')), may hold values from -6 to 6
- b_second: float32 [2048, 512], P(('dp', 'fsdp')), may hold values from 0.1 to 10
Outputs:
- grad_input: bfloat16 [4096, 4096], P(('dp', 'fsdp'))
- new_a_param: float32 [4096, 2048], P('fsdp', 'dp')
- new_a_moment: float32 [4096, 2048], P('fsdp', 'dp')
- new_a_second: float32 [4096, 2048], P('fsdp', 'dp')
- new_b_param: float32 [2048, 512], P(('dp', 'fsdp'))
- new_b_moment: float32 [2048, 512], P(('dp', 'fsdp'))
- new_b_second: float32 [2048, 512], P(('dp', 'fsdp'))
The draws below stay inside these ranges and needn't reach their ends.
Inputs may be any that keep to these rules, and one draw needn't show every extreme that they name: `tenant`: tenant t belongs to owner group t // 8. Among the 128 rows of each device, at most 38 belong to the tenants of one owner group; in every draw one owner group has exactly 38 rows on every device.
All inputs are finite; a program needn't handle non-finite values.
Results may differ from the reference program's by a relative error of at most 0.014.
Values may be sent and summed in bfloat16 or wider, within the bound.
No kernel may reach another device: no remote copies, remote signals or barrier semaphores. Data moves between devices by JAX's collectives and lax.ppermute only.
A program may use at most 64 MiB of HBM per device.

```python
import math
import jax
import jax.numpy as jnp
from jax import lax

MODEL_WIDTH = 4096
KEY_FEATURES = 512
ADAPTER_RANK = 32
TEN_DEV = 8
RD = 128
OWNERS = 8
TENANTS = 64
CAP = 38
ROWS = 4096


def draw_tenant(key, part):
    groups = ROWS // RD
    base_key = jax.random.fold_in(key, 11)
    busy_owner = jax.random.randint(jax.random.fold_in(base_key, 1), (), 0, OWNERS)
    dev_keys = jax.random.split(jax.random.fold_in(base_key, 2), groups)
    position = jnp.arange(RD, dtype=jnp.int32)
    rank_of = jnp.where(position < CAP, 0, jnp.where(position < 2 * CAP, 1, 2 + (position - 2 * CAP) % (OWNERS - 2)))

    def one_device(subkey):
        first_key, second_key, third_key = jax.random.split(subkey, 3)
        scores = jax.random.permutation(first_key, OWNERS).astype(jnp.int32)
        scores = jnp.where(jnp.arange(OWNERS, dtype=jnp.int32) == busy_owner, -1, scores)
        ordered = jnp.argsort(scores).astype(jnp.int32)
        owner_rows = ordered[rank_of]
        local_id = jax.random.randint(second_key, (RD,), 0, TEN_DEV)
        labels = owner_rows * TEN_DEV + local_id
        shuffle = jax.random.permutation(third_key, RD)
        return labels[shuffle]
    return jax.vmap(one_device)(dev_keys).reshape(ROWS).astype(jnp.int32)


def touch_ends(drawn, key, least, top_value):
    longest = drawn.shape.index(max(drawn.shape))
    spots = []
    for shift in (0, 1):
        where = [jax.random.randint(jax.random.fold_in(key, axis), (), 0, length) for axis, length in enumerate(drawn.shape)]
        where[longest] = (where[longest] + shift) % drawn.shape[longest]
        spots.append(tuple(where))
    return drawn.at[spots[0]].set(least).at[spots[1]].set(top_value)


def strengthened(entries, key, source, target, blocks, factor):
    owner, partner = [(jnp.arange(entries.shape[dim]) // (entries.shape[dim] // blocks)).reshape([-1 if axis == dim else 1 for axis in range(entries.ndim)]) for dim in (source, target)]
    chosen = jax.random.permutation(key, blocks)[partner]
    strong = (owner == chosen) | (owner == (partner + blocks // 2) % blocks)
    return jnp.where(strong, factor * entries, entries)


def levels(key, extent, shards, smallest, high):
    def one(dim, shards_of):
        heights = jax.random.uniform(jax.random.fold_in(jax.random.fold_in(key, 6), dim), (shards_of,), jnp.float32, smallest / len(shards), high / len(shards))
        return jnp.repeat(jnp.exp(heights), extent[dim] // shards_of).reshape((-1,) + (1,) * (len(extent) - dim - 1))

    loudness = one(*shards[0])
    for cut in shards[1:]:
        loudness = loudness * one(*cut)
    return loudness


def noise(key, extent, spread, most, cuts=(), held_as=jnp.bfloat16):
    values = spread * jax.random.normal(key, extent, jnp.float32)
    if cuts:
        values = values * levels(key, extent, cuts, -0.22, 0.18)
    return jnp.clip(values, -most, most).astype(held_as)


def heavy_noise(own_key, shape, deviation, limit, shards, heavy, kind=jnp.bfloat16):
    array = deviation * jax.random.normal(own_key, shape, jnp.float32)
    if shards:
        array = array * levels(own_key, shape, shards, -0.22, 0.18)
    return jnp.clip(strengthened(array, jax.random.fold_in(own_key, 3), *heavy), -limit, limit).astype(kind)


def setup_inputs(seed: int = 0) -> dict:
    key_of = jax.random.split(jax.random.key(seed), 12)
    acts = heavy_noise(key_of[0], (ROWS, MODEL_WIDTH), 1.0, 6.0, ((0, 32),), (0, 1, 32, 2.75))
    cotangent = noise(key_of[1], (ROWS, KEY_FEATURES), 1.0, 6.0, ((0, 32),))
    tenant = draw_tenant(jax.random.fold_in(key_of[11], 71), 0)
    advantage = touch_ends(jax.random.randint(key_of[3], (ROWS,), -8, 9), jax.random.fold_in(key_of[3], 1), -8, 8).astype(jnp.int32)
    base_weight = noise(key_of[4], (MODEL_WIDTH, KEY_FEATURES), KEY_FEATURES ** -0.5, 0.25, ((0, 4),))
    a_param = noise(key_of[5], (MODEL_WIDTH, TENANTS * ADAPTER_RANK), 1.0, 6.0, ((0, 4), (1, 8)), jnp.float32)
    a_moment = noise(key_of[6], (MODEL_WIDTH, TENANTS * ADAPTER_RANK), 1.0, 6.0, ((0, 4), (1, 8)), jnp.float32)
    a_second = jnp.clip(jnp.exp(math.log(10.0) - 4.6051702 * jax.random.uniform(key_of[7], (MODEL_WIDTH, TENANTS * ADAPTER_RANK), jnp.float32) ** levels(key_of[7], (MODEL_WIDTH, TENANTS * ADAPTER_RANK), ((0, 4), (1, 8)), -0.2, 0.2)), 0.1, 10.0)
    b_param = noise(key_of[8], (TENANTS * ADAPTER_RANK, KEY_FEATURES), 1.0, 6.0, ((0, 32),), jnp.float32)
    b_moment = noise(key_of[9], (TENANTS * ADAPTER_RANK, KEY_FEATURES), 1.0, 6.0, ((0, 32),), jnp.float32)
    b_second = jnp.clip(jnp.exp(math.log(10.0) - 4.6051702 * jax.random.uniform(key_of[10], (TENANTS * ADAPTER_RANK, KEY_FEATURES), jnp.float32) ** levels(key_of[10], (TENANTS * ADAPTER_RANK, KEY_FEATURES), ((0, 32),), -0.2, 0.2)), 0.1, 10.0)
    return dict(acts=acts, cotangent=cotangent, tenant=tenant, advantage=advantage, base_weight=base_weight, a_param=a_param, a_moment=a_moment, a_second=a_second, b_param=b_param, b_moment=b_moment, b_second=b_second)


adapter_scale = 2.0
learn_rate = 0.02
beta_one = 0.9
beta_two = 0.999
adam_eps = 1e-08
bias_one = 1.0 - 0.9 ** 10
bias_two = 1.0 - 0.999 ** 10

def adam_step(param, moment, second, gradient):
    moment = beta_one * moment + (1.0 - beta_one) * gradient
    second = beta_two * second + (1.0 - beta_two) * gradient * gradient
    param = param - learn_rate * (moment / bias_one) / (jnp.sqrt(second / bias_two) + adam_eps)
    return (param, moment, second)

def reference(acts, cotangent, tenant, advantage, base_weight, a_param, a_moment, a_second, b_param, b_moment, b_second):
    tenant_index = TEN_DEV * OWNERS
    scaled = (cotangent.astype(jnp.float32) * (advantage.astype(jnp.float32) * 0.25)[:, None]).astype(jnp.bfloat16)
    a_low = (a_param * MODEL_WIDTH ** (-0.5)).astype(jnp.bfloat16)
    b_low = (b_param * ADAPTER_RANK ** (-0.5)).astype(jnp.bfloat16)
    a_stack = a_low.reshape(MODEL_WIDTH, tenant_index, ADAPTER_RANK).transpose(1, 0, 2)
    b_stack = b_low.reshape(tenant_index, ADAPTER_RANK, KEY_FEATURES)
    blocks = ROWS // RD
    acts_blocks = acts.reshape(blocks, RD, MODEL_WIDTH)
    scaled_blocks = scaled.reshape(blocks, RD, KEY_FEATURES)
    tenant_blocks = tenant.reshape(blocks, RD)

    def one_block(carry, inputs):
        down_gradient_total, up_gradient_total = carry
        x_blk, s_blk, t_blk = inputs
        down_factor_rows = a_stack[t_blk].astype(jnp.float32)
        b_rows = b_stack[t_blk].astype(jnp.float32)
        x_float = x_blk.astype(jnp.float32)
        s_float = s_blk.astype(jnp.float32)
        mid_proj = jnp.einsum('nd,ndr->nr', x_float, down_factor_rows).astype(jnp.bfloat16)
        backward_projection = jnp.einsum('nk,nrk->nr', s_float, b_rows).astype(jnp.bfloat16)
        adapter_branch_term = (adapter_scale * jnp.einsum('wt,wht->wh', backward_projection.astype(jnp.float32), down_factor_rows)).astype(jnp.bfloat16)
        base_term = jnp.dot(s_blk, base_weight.T, preferred_element_type=jnp.float32).astype(jnp.bfloat16)
        out_rows = (base_term.astype(jnp.float32) + adapter_branch_term.astype(jnp.float32)).astype(jnp.bfloat16)
        down_gradient_total = down_gradient_total.at[t_blk].add(x_float[:, :, None] * backward_projection.astype(jnp.float32)[:, None, :])
        up_gradient_total = up_gradient_total.at[t_blk].add(mid_proj.astype(jnp.float32)[:, :, None] * s_float[:, None, :])
        return ((down_gradient_total, up_gradient_total), out_rows)
    start = (jnp.zeros((tenant_index, MODEL_WIDTH, ADAPTER_RANK), jnp.float32), jnp.zeros((tenant_index, ADAPTER_RANK, KEY_FEATURES), jnp.float32))
    (down_gradient_total, up_gradient_total), out_blocks = lax.scan(one_block, start, (acts_blocks, scaled_blocks, tenant_blocks))
    grad_input = out_blocks.reshape(ROWS, MODEL_WIDTH)
    down_factor_gradient = (down_gradient_total * (adapter_scale * MODEL_WIDTH ** (-0.5))).transpose(1, 0, 2).reshape(MODEL_WIDTH, tenant_index * ADAPTER_RANK)
    up_factor_gradient = (up_gradient_total * (adapter_scale * ADAPTER_RANK ** (-0.5))).reshape(tenant_index * ADAPTER_RANK, KEY_FEATURES)
    new_a = adam_step(a_param, a_moment, a_second, down_factor_gradient)
    new_b = adam_step(b_param, b_moment, b_second, up_factor_gradient)
    return (grad_input, new_a[0], new_a[1], new_a[2], new_b[0], new_b[1], new_b[2])
```

```python
import jax
import jax.numpy as jnp
from jax import lax
from jax.sharding import PartitionSpec as P

MODEL_WIDTH = 4096
ADAPTER_RANK = 32
TEN_DEV = 8
GROUP_ELEMENTS = 1 << 20


adapter_scale = 2.0
learn_rate = 0.02
beta_one = 0.9
beta_two = 0.999
adam_eps = 1e-08
bias_one = 1.0 - 0.9**10
bias_two = 1.0 - 0.999**10


def adam_step(param, moment, second, gradient):
    moment = beta_one * moment + (1.0 - beta_one) * gradient
    second = beta_two * second + (1.0 - beta_two) * gradient * gradient
    param = param - learn_rate * (moment / bias_one) / (jnp.sqrt(second / bias_two) + adam_eps)
    return (param, moment, second)


def contract(left, right, left_dim, right_dim):
    return lax.dot_general(
        left, right, (((left_dim,), (right_dim,)), ((), ())), preferred_element_type=jnp.float32
    )


def swap(block, bit):
    size = lax.axis_size("dp")
    return lax.ppermute(block, "dp", [(i, i ^ bit) for i in range(size)])


def cube_gather(block, order):
    held = {0: block}
    for bit in order:
        held.update({k ^ bit: swap(v, bit) for k, v in list(held.items())})
    return held


def sum_scatter(blocks, order):
    for bit in order:
        after = {}
        for k in [k for k in blocks if not k & bit]:
            after[k] = blocks[k].astype(jnp.float32) + swap(blocks[k ^ bit], bit).astype(
                jnp.float32
            )
        if len(after) > 1:
            after = {k: v.astype(jnp.bfloat16) for k, v in after.items()}
        blocks = after
    return blocks[0]


def per_device(
    acts,
    cotangent,
    tenant,
    advantage,
    base_weight,
    a_param,
    a_moment,
    a_second,
    b_param,
    b_moment,
    b_second,
):
    owners = lax.axis_size("dp")
    shards = lax.axis_size("fsdp")
    me = lax.axis_index("dp")
    row_count, keys = cotangent.shape
    features, columns = a_param.shape
    own_rows = b_param.shape[0]
    rows = row_count * shards
    group = min(max(GROUP_ELEMENTS // (rows * columns), 1), owners)
    wires = [1 << i for i in range(1, owners.bit_length() - 1)]
    orders = (wires + [1], wires[::-1] + [1])
    back_orders = ([1] + wires, [1] + wires[::-1])

    scaled = (
        cotangent.astype(jnp.float32) * (advantage.astype(jnp.float32) * 0.25)[:, None]
    ).astype(jnp.bfloat16)
    a_low = (a_param * MODEL_WIDTH ** (-0.5)).astype(jnp.bfloat16)
    b_low = (b_param * ADAPTER_RANK ** (-0.5)).astype(jnp.bfloat16)

    labels = jnp.stack([tenant // TEN_DEV, tenant % TEN_DEV]).astype(jnp.bfloat16)
    labels = jnp.pad(labels, ((0, 14), (0, keys - row_count)))
    packed = jnp.concatenate([scaled, b_low, labels], axis=0)
    shared = lax.all_to_all(
        jnp.broadcast_to(packed[None], (shards,) + packed.shape), "fsdp", 0, 0, tiled=True
    )
    scaled_all = shared[:, :row_count].reshape(rows, keys)
    b_owner = shared[:, row_count : row_count + own_rows].reshape(columns, keys)
    labels = shared[:, row_count + own_rows :, :row_count].astype(jnp.int32)
    label = ((labels[:, 0] ^ me) * TEN_DEV + labels[:, 1]).reshape(rows)

    acts_part = lax.all_to_all(acts, "fsdp", split_axis=1, concat_axis=0, tiled=True)

    half = features // 2
    a_blocks = [
        cube_gather(a_low[i * half : (i + 1) * half], orders[i]) for i in range(2)
    ]
    b_blocks = cube_gather(b_owner, orders[0])

    base_term = contract(scaled_all, base_weight, 1, 1).astype(jnp.bfloat16)

    width = group * columns
    column = jnp.arange(width, dtype=jnp.int32) // ADAPTER_RANK
    fold = (
        jnp.arange(width, dtype=jnp.int32)[:, None] % ADAPTER_RANK
        == jnp.arange(ADAPTER_RANK, dtype=jnp.int32)[None, :]
    ).astype(jnp.bfloat16)
    down_coefficient = adapter_scale * MODEL_WIDTH ** (-0.5)
    up_coefficient = adapter_scale * ADAPTER_RANK ** (-0.5)

    grad_a_blocks = ({}, {})
    side = [None, None]
    mid = None
    for first in range(0, owners, group):
        members = range(first, first + group)
        mask = label[:, None] == (column + first * TEN_DEV)[None, :]
        b_group = jnp.concatenate([b_blocks[k] for k in members], axis=0)
        back = jnp.where(mask, contract(scaled_all, b_group, 1, 1), 0.0).astype(jnp.bfloat16)
        grad_a = (down_coefficient * contract(acts_part, back, 0, 0)).astype(jnp.bfloat16)
        for n, k in enumerate(members):
            for i in range(2):
                grad_a_blocks[i][k] = grad_a[
                    i * half : (i + 1) * half, n * columns : (n + 1) * columns
                ]
        mid_wide = None
        for i in range(2):
            a_group = jnp.concatenate([a_blocks[i][k] for k in members], axis=1)
            term = contract(back, a_group, 1, 1)
            side[i] = term if side[i] is None else side[i] + term
            term = contract(acts_part[:, i * half : (i + 1) * half], a_group, 1, 0)
            mid_wide = term if mid_wide is None else mid_wide + term
        mid_wide = jnp.where(mask, mid_wide, 0.0).astype(jnp.bfloat16)
        term = contract(fold, mid_wide, 0, 1)
        mid = term if mid is None else mid + term

    side_term = (adapter_scale * jnp.concatenate(side, axis=1)).astype(jnp.bfloat16)
    grad_part = (base_term.astype(jnp.float32) + side_term.astype(jnp.float32)).astype(
        jnp.bfloat16
    )
    grad_input = lax.all_to_all(grad_part, "fsdp", split_axis=0, concat_axis=1, tiled=True)

    mid_parts = lax.all_to_all(
        jnp.broadcast_to(mid.astype(jnp.bfloat16)[None], (shards,) + mid.shape),
        "fsdp",
        0,
        0,
        tiled=True,
    )
    mid = jnp.sum(mid_parts.astype(jnp.float32), axis=0).astype(jnp.bfloat16)
    start = lax.axis_index("fsdp") * own_rows
    mid_rows = lax.dynamic_slice_in_dim(jnp.tile(mid, (TEN_DEV, 1)), start, own_rows, 0)
    local = (start + jnp.arange(own_rows, dtype=jnp.int32)) // ADAPTER_RANK
    wanted = jnp.arange(owners, dtype=jnp.int32)[:, None] * TEN_DEV + local[None, :]
    mid_spread = jnp.where(
        wanted[:, :, None] == label[None, None, :], mid_rows[None], jnp.zeros((), jnp.bfloat16)
    ).reshape(owners * own_rows, rows)
    grad_b = (up_coefficient * contract(mid_spread, scaled_all, 1, 0)).astype(jnp.bfloat16)
    grad_b = sum_scatter(
        {k: grad_b[k * own_rows : (k + 1) * own_rows] for k in range(owners)}, back_orders[0]
    )
    grad_a = jnp.concatenate(
        [sum_scatter(grad_a_blocks[i], back_orders[i]) for i in range(2)], axis=0
    )

    new_a = adam_step(a_param, a_moment, a_second, grad_a)
    new_b = adam_step(b_param, b_moment, b_second, grad_b)
    return (grad_input, new_a[0], new_a[1], new_a[2], new_b[0], new_b[1], new_b[2])


def solution(mesh):
    rows = P(("dp", "fsdp"), None)
    labels = P(("dp", "fsdp"))
    first = P("fsdp", "dp")
    return jax.shard_map(
        per_device,
        mesh=mesh,
        in_specs=(rows, rows, labels, labels, P("fsdp", None), first, first, first, rows, rows, rows),
        out_specs=(rows, first, first, first, rows, rows, rows),
        check_vma=False,
    )
```

```python
import functools

import jax
import jax.numpy as jnp
from jax import lax
from jax.experimental import pallas as pl
from jax.experimental.pallas import tpu as pltpu
from jax.sharding import PartitionSpec as P

MODEL_WIDTH = 4096
ADAPTER_RANK = 32
TEN_DEV = 8
LANES = 128
ROW_STEP = 512
LABEL_ROWS = 16

adapter_scale = 2.0
learn_rate = 0.02
beta_one = 0.9
beta_two = 0.999
adam_eps = 1e-08
bias_one = 1.0 - 0.9**10
bias_two = 1.0 - 0.999**10

f32 = jnp.float32
bf16 = jnp.bfloat16
ANY = pl.BlockSpec(memory_space=pl.ANY)
VMEM = pl.BlockSpec(memory_space=pltpu.VMEM)


def shape(dims, kind=bf16):
    return jax.ShapeDtypeStruct(tuple(dims), kind)


def call(body, outs, ins, scratch=(), in_specs=None, cost=0):
    return pl.pallas_call(
        body,
        out_shape=outs,
        in_specs=in_specs or [VMEM] * len(ins),
        out_specs=jax.tree.map(lambda _: VMEM, outs),
        scratch_shapes=list(scratch),
        compiler_params=pltpu.CompilerParams(vmem_limit_bytes=48 << 20),
        cost_estimate=pl.CostEstimate(flops=cost, bytes_accessed=cost, transcendentals=0),
    )(*ins)


def adam_step(param, moment, second, gradient):
    moment = beta_one * moment + (1.0 - beta_one) * gradient
    second = beta_two * second + (1.0 - beta_two) * gradient * gradient
    param = param - learn_rate * (moment / bias_one) / (jnp.sqrt(second / bias_two) + adam_eps)
    return (param, moment, second)


def dot(left, right, left_dim=1, right_dim=0):
    return lax.dot_general(
        left, right, (((left_dim,), (right_dim,)), ((), ())), preferred_element_type=f32
    )


def iota(dims, axis):
    return lax.broadcasted_iota(jnp.int32, dims, axis)


def column_of(row, lanes=LANES):
    n = row.shape[1]
    wide = jnp.broadcast_to(row.astype(f32), (lanes, n))
    return jnp.transpose(wide)


def prep_kernel(cot, tenant, advantage, a_param, b_param, share, a_low, b_low):
    rows, keys = cot.shape
    factor = column_of(advantage[...]) * 0.25
    factor = jnp.concatenate([factor] * (keys // LANES), axis=1)
    share[:rows] = (cot[...].astype(f32) * factor).astype(bf16)
    t = tenant[...]
    line = iota((LABEL_ROWS, rows), 0)
    owner = jnp.broadcast_to(lax.div(t, TEN_DEV), (LABEL_ROWS, rows))
    local = jnp.broadcast_to(lax.rem(t, TEN_DEV), (LABEL_ROWS, rows))
    labels = jnp.where(line == 0, owner, jnp.where(line == 1, local, 0)).astype(f32)
    share[rows:, :rows] = labels.astype(bf16)
    share[rows:, rows:] = jnp.zeros((LABEL_ROWS, keys - rows), bf16)
    a_low[...] = (a_param[...] * MODEL_WIDTH ** (-0.5)).astype(bf16)
    b_low[...] = (b_param[...] * ADAPTER_RANK ** (-0.5)).astype(bf16)


def second_ids(owners, own_rows, rows):
    line = iota((owners * own_rows, rows), 0)
    inner = lax.rem(line, own_rows) + lax.axis_index("fsdp") * own_rows
    return lax.div(line, own_rows) * TEN_DEV + lax.div(inner, ADAPTER_RANK)


def back_kernel(shards, owners, *refs):
    shares, b_blocks = refs[:shards], refs[shards : shards + owners]
    scaled, label, back, b_all = refs[shards + owners :]
    rd = shares[0].shape[0] - LABEL_ROWS
    own_rows = b_blocks[0].shape[0]
    me, place = lax.axis_index("dp"), lax.axis_index("fsdp")
    for j in range(shards):
        at = pl.ds(pl.multiple_of((place ^ j) * rd, rd), rd)
        scaled[at] = shares[j][:rd]
        ids = shares[j][rd:, :rd].astype(f32).astype(jnp.int32)
        tid = (ids[0:1] ^ me) * TEN_DEV + ids[1:2]
        label[:, at] = jnp.broadcast_to(tid, (8, rd))
    for k in range(owners):
        b_all[k * own_rows : (k + 1) * own_rows] = b_blocks[k][...]
    rows = scaled.shape[0]
    step = min(ROW_STEP, rows)
    ids = second_ids(owners, own_rows, step)
    for r in range(0, rows, step):
        wide = dot(b_all[...], scaled[r : r + step], 1, 1)
        wide = jnp.where(ids == label[0:1, r : r + step], wide, 0.0)
        if own_rows >= ADAPTER_RANK:
            low = jnp.sum(wide.reshape(-1, ADAPTER_RANK, step), axis=0)
        else:
            low = jnp.sum(wide.reshape(-1, own_rows, step), axis=0)
            low = jnp.concatenate([low] * (ADAPTER_RANK // own_rows), axis=0)
            part = lax.div(iota(low.shape, 0), own_rows)
            low = jnp.where(part == lax.rem(place, ADAPTER_RANK // own_rows), low, 0.0)
        back[:, r : r + step] = low.astype(bf16)


def total(parts, at):
    value = parts[0][:, at].astype(f32)
    for part in parts[1:]:
        value = value + part[:, at].astype(f32)
    return value


def load_factors(a_blocks, a_all, sems):
    columns = a_blocks[0].shape[1]
    copies = [
        pltpu.make_async_copy(
            block, a_all.at[:, k * columns : (k + 1) * columns], sems.at[k]
        )
        for k, block in enumerate(a_blocks)
    ]
    for copy in copies:
        copy.start()
    return copies


def side_kernel(shards, owners, *refs):
    backs, a_blocks = refs[:shards], refs[shards : shards + owners]
    label, scaled, weight, out, a_all, back_wide, sems = refs[shards + owners :]
    copies = load_factors(a_blocks, a_all, sems)
    rows, features = out.shape
    step = min(ROW_STEP, rows)
    width = a_all.shape[1]
    for r in range(0, rows, step):
        at = slice(r, r + step)
        low = adapter_scale * jnp.transpose(total(backs, at))
        low = jnp.concatenate([low] * (LANES // ADAPTER_RANK), axis=1)
        where = column_of(label[0:1, at]).astype(jnp.int32) - lax.div(
            iota((step, LANES), 1), ADAPTER_RANK
        )
        for q in range(width // LANES):
            hit = where == q * (LANES // ADAPTER_RANK)
            back_wide[:, q * LANES : (q + 1) * LANES] = jnp.where(hit, low, 0.0).astype(bf16)
        if r == 0:
            for copy in copies:
                copy.wait()
        chunk = min(256, features)
        for c in range(0, features, chunk):
            base = dot(scaled[at], weight[c : c + chunk], 1, 1).astype(bf16)
            side = dot(back_wide[...], a_all[c : c + chunk], 1, 1).astype(bf16)
            out[at, c : c + chunk] = (base.astype(f32) + side.astype(f32)).astype(bf16)


def spread(low, label, k, columns):
    rows = low.shape[1]
    ids = lax.div(iota((columns, rows), 0), ADAPTER_RANK) + k * TEN_DEV
    tall = jnp.concatenate([low] * (columns // ADAPTER_RANK), axis=0)
    return jnp.where(ids == label, tall, 0.0).astype(bf16)


def first_kernel(shards, owners, parity, *refs):
    backs = refs[:shards]
    label, acts = refs[shards : shards + 2]
    arrived = refs[shards + 2] if parity == 0 else None
    outs = refs[shards + 2 + (parity == 0) :]
    coefficient = adapter_scale * MODEL_WIDTH ** (-0.5)
    low = total(backs, slice(None))
    for n in range(owners // 2):
        k = 2 * n + parity
        columns = outs[0].shape[-2]
        grad = coefficient * dot(spread(low, label[0:1], k, columns), acts[...])
        if parity:
            outs[0][n] = grad.astype(bf16)
        else:
            outs[n][...] = (grad + arrived[n].astype(f32)).astype(bf16)


def mid_kernel(owners, *refs):
    a_blocks = refs[:owners]
    label, acts, out, a_all, sems = refs[owners:]
    copies = load_factors(a_blocks, a_all, sems)
    rows = acts.shape[0]
    columns = a_blocks[0].shape[1]
    step = min(ROW_STEP, rows)
    for r in range(0, rows, step):
        at = slice(r, r + step)
        where = column_of(label[0:1, at]).astype(jnp.int32) - lax.div(
            iota((step, LANES), 1), ADAPTER_RANK
        )
        low = jnp.zeros((step, LANES), f32)
        for k in range(owners):
            if r == 0:
                copies[k].wait()
            wide = dot(acts[at], a_all[:, k * columns : (k + 1) * columns])
            for q in range(columns // LANES):
                hit = where == k * TEN_DEV + q * (LANES // ADAPTER_RANK)
                low = low + jnp.where(hit, wide[:, q * LANES : (q + 1) * LANES], 0.0)
        low = jnp.transpose(low).reshape(LANES // ADAPTER_RANK, ADAPTER_RANK, step)
        out[:, at] = jnp.sum(low, axis=0).astype(bf16)


def second_kernel(shards, owners, *refs):
    mids = refs[:shards]
    label, scaled, out, held = refs[shards:]
    own_rows, keys = out.shape[1:]
    rows = scaled.shape[0]
    step = min(ROW_STEP, rows)
    coefficient = adapter_scale * ADAPTER_RANK ** (-0.5)
    ids = second_ids(owners, own_rows, step)
    grad = jnp.zeros((owners * own_rows, keys), f32)
    for r in range(0, rows, step):
        at = slice(r, r + step)
        held[...] = total(mids, at)
        if own_rows >= ADAPTER_RANK:
            low = jnp.concatenate([held[...]] * (owners * own_rows // ADAPTER_RANK), axis=0)
        else:
            first = lax.rem(lax.axis_index("fsdp") * own_rows, ADAPTER_RANK)
            low = held[pl.ds(pl.multiple_of(first, own_rows), own_rows)]
            low = jnp.concatenate([low] * owners, axis=0)
        low = jnp.where(ids == label[0:1, at], low, 0.0).astype(bf16)
        grad = grad + dot(low, scaled[at])
    grad = (coefficient * grad).astype(bf16)
    for k in range(owners):
        out[k] = grad[k * own_rows : (k + 1) * own_rows]


def adam_a_kernel(count, *refs):
    grads, (param, moment, second), outs = refs[:count], refs[count : count + 3], refs[count + 3 :]
    grad = grads[0][...].astype(f32)
    for part in grads[1:]:
        grad = grad + part[...].astype(f32)
    new = adam_step(param[...], moment[...], second[...], jnp.transpose(grad))
    for out, value in zip(outs, new):
        out[...] = value


def adam_b_kernel(count, *refs):
    grads, (param, moment, second), outs = refs[:count], refs[count : count + 3], refs[count + 3 :]
    grad = grads[0][...].astype(f32)
    for part in grads[1:]:
        grad = grad + part[...].astype(f32)
    for out, value in zip(outs, adam_step(param[...], moment[...], second[...], grad)):
        out[...] = value


def swap(block, axis, bits):
    size = lax.axis_size(axis)
    return lax.ppermute(block, axis, [(i, i ^ bits) for i in range(size)])


def per_device(
    acts,
    cotangent,
    tenant,
    advantage,
    base_weight,
    a_param,
    a_moment,
    a_second,
    b_param,
    b_moment,
    b_second,
):
    owners = lax.axis_size("dp")
    shards = lax.axis_size("fsdp")
    row_count, keys = cotangent.shape
    features, columns = a_param.shape
    own_rows = b_param.shape[0]
    rows = row_count * shards

    share, a_low, b_low = call(
        prep_kernel,
        (shape((row_count + LABEL_ROWS, keys)), shape((features, columns)), shape((own_rows, keys))),
        (cotangent, tenant[None], advantage[None], a_param, b_param),
    )
    b_blocks = [b_low] + [swap(b_low, "dp", k) for k in range(1, owners)]
    shares = [share] + [swap(share, "fsdp", j) for j in range(1, shards)]
    chips = [a_low] + [swap(a_low, "dp", k) for k in range(2, owners, 2)]
    acts_part = lax.all_to_all(acts, "fsdp", split_axis=1, concat_axis=0, tiled=True)
    a_blocks = []
    for block in chips:
        a_blocks += [block, swap(block, "dp", 1)]

    scaled, label, back = call(
        functools.partial(back_kernel, shards, owners),
        (shape((rows, keys)), shape((8, rows), jnp.int32), shape((ADAPTER_RANK, rows))),
        (*shares, *b_blocks),
        [pltpu.VMEM((owners * own_rows, keys), bf16)],
    )
    backs = [back] + [swap(back, "fsdp", j) for j in range(1, shards)]

    step = min(ROW_STEP, rows)
    factor_scratch = [pltpu.VMEM((features, owners * columns), bf16)]
    sems = [pltpu.SemaphoreType.DMA((owners,))]
    grad_part = call(
        functools.partial(side_kernel, shards, owners),
        shape((rows, features)),
        (*backs, *a_blocks, label, scaled, base_weight),
        factor_scratch + [pltpu.VMEM((step, owners * columns), bf16)] + sems,
        [VMEM] * shards + [ANY] * owners + [VMEM] * 3,
    )
    grad_input = lax.all_to_all(grad_part, "fsdp", split_axis=0, concat_axis=1, tiled=True)

    odd = call(
        functools.partial(first_kernel, shards, owners, 1),
        shape((owners // 2, columns, features)),
        (*backs, label, acts_part),
    )
    even = call(
        functools.partial(first_kernel, shards, owners, 0),
        [shape((columns, features))] * (owners // 2),
        (*backs, label, acts_part, swap(odd, "dp", 1)),
    )
    grad_a = [even[0]] + [swap(even[n], "dp", 2 * n) for n in range(1, owners // 2)]

    mid = call(
        functools.partial(mid_kernel, owners),
        shape((ADAPTER_RANK, rows)),
        (*a_blocks, label, acts_part),
        factor_scratch + sems,
        [ANY] * owners + [VMEM] * 2,
    )
    mids = [mid] + [swap(mid, "fsdp", j) for j in range(1, shards)]
    grad_b = call(
        functools.partial(second_kernel, shards, owners),
        shape((owners, own_rows, keys)),
        (*mids, label, scaled),
        [pltpu.VMEM((ADAPTER_RANK, step), f32)],
    )
    grad_b = [grad_b[0]] + [swap(grad_b[k], "dp", k) for k in range(1, owners)]

    new_b = call(
        functools.partial(adam_b_kernel, owners),
        [shape(b_param.shape, f32)] * 3,
        (*grad_b, b_param, b_moment, b_second),
    )
    block = min(256, features)
    wide = pl.BlockSpec((columns, block), lambda i: (0, i))
    tall = pl.BlockSpec((block, columns), lambda i: (i, 0))
    new_a = pl.pallas_call(
        functools.partial(adam_a_kernel, owners // 2),
        grid=(features // block,),
        out_shape=[shape(a_param.shape, f32)] * 3,
        in_specs=[wide] * (owners // 2) + [tall] * 3,
        out_specs=[tall] * 3,
        compiler_params=pltpu.CompilerParams(vmem_limit_bytes=48 << 20),
    )(*grad_a, a_param, a_moment, a_second)
    return (grad_input, new_a[0], new_a[1], new_a[2], new_b[0], new_b[1], new_b[2])


def solution(mesh):
    rows = P(("dp", "fsdp"), None)
    labels = P(("dp", "fsdp"))
    first = P("fsdp", "dp")
    return jax.shard_map(
        per_device,
        mesh=mesh,
        in_specs=(rows, rows, labels, labels, P("fsdp", None), first, first, first, rows, rows, rows),
        out_specs=(rows, first, first, first, rows, rows, rows),
        check_vma=False,
    )
```

```python
import functools

import jax
import jax.numpy as jnp
from jax import lax
from jax.experimental import pallas as pl
from jax.experimental.pallas import tpu as pltpu
from jax.sharding import PartitionSpec as P

MODEL_WIDTH = 4096
ADAPTER_RANK = 32
TEN_DEV = 8
LANES = 128
ROW_STEP = 512
LABEL_ROWS = 16
PARTS = 1

adapter_scale = 2.0
learn_rate = 0.02
beta_one = 0.9
beta_two = 0.999
adam_eps = 1e-08
bias_one = 1.0 - 0.9**10
bias_two = 1.0 - 0.999**10

f32 = jnp.float32
bf16 = jnp.bfloat16
ANY = pl.BlockSpec(memory_space=pl.ANY)
VMEM = pl.BlockSpec(memory_space=pltpu.VMEM)


def shape(dims, kind=bf16):
    return jax.ShapeDtypeStruct(tuple(dims), kind)


def call(body, outs, ins, scratch=(), in_specs=None, out_specs=None, vmem=16):
    return pl.pallas_call(
        body,
        out_shape=outs,
        in_specs=in_specs or [VMEM] * len(ins),
        out_specs=out_specs or jax.tree.map(lambda _: VMEM, outs),
        scratch_shapes=list(scratch),
        compiler_params=pltpu.CompilerParams(vmem_limit_bytes=vmem << 20),
        cost_estimate=pl.CostEstimate(flops=0, bytes_accessed=0, transcendentals=0),
    )(*ins)


def adam_step(param, moment, second, gradient):
    moment = beta_one * moment + (1.0 - beta_one) * gradient
    second = beta_two * second + (1.0 - beta_two) * gradient * gradient
    step = (learn_rate / bias_one) * moment
    param = param - step / (jnp.sqrt((1.0 / bias_two) * second) + adam_eps)
    return (param, moment, second)


def dot(left, right, left_dim=1, right_dim=0):
    return lax.dot_general(
        left, right, (((left_dim,), (right_dim,)), ((), ())), preferred_element_type=f32
    )


def iota(dims, axis):
    return lax.broadcasted_iota(jnp.int32, dims, axis)


def column_of(row, lanes=LANES):
    n = row.shape[1]
    wide = jnp.broadcast_to(row.astype(f32), (lanes, n))
    return jnp.transpose(wide)


def prep_kernel(parts, *refs):
    acts, cot, tenant, advantage, a_param, b_param, share, low = refs[:8]
    cuts, sems = refs[8 : 8 + parts], refs[-1]
    shards, _, width = cuts[0].shape
    copies = []
    for h in range(parts):
        for j in range(shards):
            at = pl.ds((j * parts + h) * width, width)
            copies.append(
                pltpu.make_async_copy(acts.at[:, at], cuts[h].at[j], sems.at[h * shards + j])
            )
    for copy in copies:
        copy.start()
    rows, keys = cot.shape
    factor = column_of(advantage[...]) * 0.25
    factor = jnp.concatenate([factor] * (keys // LANES), axis=1)
    share[:rows] = (cot[...].astype(f32) * factor).astype(bf16)
    t = tenant[...]
    line = iota((LABEL_ROWS, rows), 0)
    owner = jnp.broadcast_to(lax.div(t, TEN_DEV), (LABEL_ROWS, rows))
    local = jnp.broadcast_to(lax.rem(t, TEN_DEV), (LABEL_ROWS, rows))
    labels = jnp.where(line == 0, owner, jnp.where(line == 1, local, 0)).astype(f32)
    share[rows:, :rows] = labels.astype(bf16)
    share[rows:, rows:] = jnp.zeros((LABEL_ROWS, keys - rows), bf16)
    features, columns = a_param.shape
    low[:features] = (a_param[...] * MODEL_WIDTH ** (-0.5)).astype(bf16)
    own_rows = b_param.shape[0]
    for q in range(keys // columns):
        part = b_param[:, q * columns : (q + 1) * columns] * ADAPTER_RANK ** (-0.5)
        low[features + q * own_rows : features + (q + 1) * own_rows] = part.astype(bf16)
    for copy in copies:
        copy.wait()


def second_ids(owners, own_rows, rows):
    line = iota((owners * own_rows, rows), 0)
    inner = lax.rem(line, own_rows) + lax.axis_index("fsdp") * own_rows
    return lax.div(line, own_rows) * TEN_DEV + lax.div(inner, ADAPTER_RANK)


def base_kernel(shards, *refs):
    shares, weight = refs[:shards], refs[shards]
    scaled, label, base = refs[shards + 1 :]
    rd = shares[0].shape[0] - LABEL_ROWS
    me, place = lax.axis_index("dp"), lax.axis_index("fsdp")
    for j in range(shards):
        at = pl.ds(pl.multiple_of((place ^ j) * rd, rd), rd)
        scaled[at] = shares[j][:rd]
        ids = shares[j][rd:, :rd].astype(f32).astype(jnp.int32)
        tid = (ids[0:1] ^ me) * TEN_DEV + ids[1:2]
        label[:, at] = jnp.broadcast_to(tid, (8, rd))
    rows = scaled.shape[0]
    step = min(ROW_STEP, rows)
    for r in range(0, rows, step):
        base[r : r + step] = dot(scaled[r : r + step], weight[...], 1, 1).astype(bf16)


def back_kernel(owners, own_rows, *refs):
    blocks = refs[:owners]
    scaled, label, back, b_all, sems = refs[owners:]
    features = blocks[0].shape[0] - own_rows * scaled.shape[1] // blocks[0].shape[1]
    columns = blocks[0].shape[1]
    rows, keys = scaled.shape
    copies = []
    for k in range(owners):
        for q in range(keys // columns):
            copies.append(
                pltpu.make_async_copy(
                    blocks[k].at[pl.ds(features + q * own_rows, own_rows)],
                    b_all.at[pl.ds(k * own_rows, own_rows), pl.ds(q * columns, columns)],
                    sems.at[k, q],
                )
            )
    for copy in copies:
        copy.start()
    step = min(ROW_STEP, rows)
    ids = second_ids(owners, own_rows, step)
    for copy in copies:
        copy.wait()
    for r in range(0, rows, step):
        wide = dot(b_all[...], scaled[r : r + step], 1, 1)
        wide = jnp.where(ids == label[0:1, r : r + step], wide, 0.0)
        if own_rows >= ADAPTER_RANK:
            low = jnp.sum(wide.reshape(-1, ADAPTER_RANK, step), axis=0)
        else:
            low = jnp.sum(wide.reshape(-1, own_rows, step), axis=0)
            low = jnp.concatenate([low] * (ADAPTER_RANK // own_rows), axis=0)
            part = lax.div(iota(low.shape, 0), own_rows)
            place = lax.rem(lax.axis_index("fsdp"), ADAPTER_RANK // own_rows)
            low = jnp.where(part == place, low, 0.0)
        back[:, r : r + step] = low.astype(bf16)


def total(parts, at):
    value = parts[0][:, at].astype(f32)
    for part in parts[1:]:
        value = value + part[:, at].astype(f32)
    return value


def load_factors(a_blocks, a_all, sems):
    columns = a_blocks[0].shape[1]
    copies = [
        pltpu.make_async_copy(
            block.at[pl.ds(0, a_all.shape[0])],
            a_all.at[:, pl.ds(k * columns, columns)],
            sems.at[k],
        )
        for k, block in enumerate(a_blocks)
    ]
    for copy in copies:
        copy.start()
    return copies


def side_kernel(shards, owners, *refs):
    backs, a_blocks = refs[:shards], refs[shards : shards + owners]
    label, base, out, a_all, back_wide, sems = refs[shards + owners :]
    copies = load_factors(a_blocks, a_all, sems)
    rows, features = out.shape
    step = min(ROW_STEP, rows)
    width = a_all.shape[1]
    for r in range(0, rows, step):
        at = slice(r, r + step)
        low = adapter_scale * jnp.transpose(total(backs, at))
        low = jnp.concatenate([low] * (LANES // ADAPTER_RANK), axis=1)
        where = column_of(label[0:1, at]).astype(jnp.int32) - lax.div(
            iota((step, LANES), 1), ADAPTER_RANK
        )
        for q in range(width // LANES):
            hit = where == q * (LANES // ADAPTER_RANK)
            back_wide[:, q * LANES : (q + 1) * LANES] = jnp.where(hit, low, 0.0).astype(bf16)
        if r == 0:
            for copy in copies:
                copy.wait()
        chunk = min(256, features)
        for c in range(0, features, chunk):
            side = dot(back_wide[...], a_all[c : c + chunk], 1, 1).astype(bf16)
            whole = base[at, c : c + chunk].astype(f32) + side.astype(f32)
            out[at, c : c + chunk] = whole.astype(bf16)


def spread(low, label, k, columns):
    rows = low.shape[1]
    ids = lax.div(iota((columns, rows), 0), ADAPTER_RANK) + k * TEN_DEV
    tall = jnp.concatenate([low] * (columns // ADAPTER_RANK), axis=0)
    return jnp.where(ids == label, tall, 0.0).astype(bf16)


def first_kernel(shards, owners, parity, *refs):
    backs = refs[:shards]
    label, acts = refs[shards : shards + 2]
    arrived = refs[shards + 2] if parity == 0 else None
    outs = refs[shards + 2 + (parity == 0) :]
    coefficient = adapter_scale * MODEL_WIDTH ** (-0.5)
    low = total(backs, slice(None))
    for n in range(owners // 2):
        k = 2 * n + parity
        columns = outs[0].shape[-2]
        grad = coefficient * dot(spread(low, label[0:1], k, columns), acts[...])
        if parity:
            outs[0][n] = grad.astype(bf16)
        else:
            outs[n][...] = (grad + arrived[n].astype(f32)).astype(bf16)


def mid_kernel(owners, parts, *refs):
    a_blocks = refs[:owners]
    label, acts = refs[owners], refs[owners + 1 : owners + 1 + parts]
    out, a_all, sems = refs[owners + 1 + parts :]
    copies = load_factors(a_blocks, a_all, sems)
    rows, width = acts[0].shape
    columns = a_blocks[0].shape[1]
    step = min(ROW_STEP, rows)
    for r in range(0, rows, step):
        at = slice(r, r + step)
        where = column_of(label[0:1, at]).astype(jnp.int32) - lax.div(
            iota((step, LANES), 1), ADAPTER_RANK
        )
        low = jnp.zeros((step, LANES), f32)
        for k in range(owners):
            if r == 0:
                copies[k].wait()
            wide = None
            for h in range(parts):
                factor = a_all[h * width : (h + 1) * width, k * columns : (k + 1) * columns]
                term = dot(acts[h][at], factor)
                wide = term if wide is None else wide + term
            for q in range(columns // LANES):
                hit = where == k * TEN_DEV + q * (LANES // ADAPTER_RANK)
                low = low + jnp.where(hit, wide[:, q * LANES : (q + 1) * LANES], 0.0)
        low = jnp.transpose(low).reshape(LANES // ADAPTER_RANK, ADAPTER_RANK, step)
        out[:, at] = jnp.sum(low, axis=0).astype(bf16)


def second_kernel(shards, owners, *refs):
    mids = refs[:shards]
    label, scaled, out, held = refs[shards:]
    own_rows, keys = out.shape[1:]
    rows = scaled.shape[0]
    step = min(ROW_STEP, rows)
    coefficient = adapter_scale * ADAPTER_RANK ** (-0.5)
    ids = second_ids(owners, own_rows, step)
    grad = jnp.zeros((owners * own_rows, keys), f32)
    for r in range(0, rows, step):
        at = slice(r, r + step)
        held[...] = total(mids, at)
        if own_rows >= ADAPTER_RANK:
            low = jnp.concatenate([held[...]] * (owners * own_rows // ADAPTER_RANK), axis=0)
        else:
            first = lax.rem(lax.axis_index("fsdp") * own_rows, ADAPTER_RANK)
            low = held[pl.ds(pl.multiple_of(first, own_rows), own_rows)]
            low = jnp.concatenate([low] * owners, axis=0)
        low = jnp.where(ids == label[0:1, at], low, 0.0).astype(bf16)
        grad = grad + dot(low, scaled[at])
    grad = (coefficient * grad).astype(bf16)
    me = lax.axis_index("dp")
    for k in range(owners):
        out[me ^ k] = grad[k * own_rows : (k + 1) * own_rows]


def adam_a_kernel(count, *refs):
    grads, (param, moment, second), outs = refs[:count], refs[count : count + 3], refs[count + 3 :]
    grad = grads[0][...].astype(f32)
    for part in grads[1:]:
        grad = grad + part[...].astype(f32)
    new = adam_step(param[...], moment[...], second[...], jnp.transpose(grad))
    for out, value in zip(outs, new):
        out[...] = value


def adam_b_kernel(grads, param, moment, second, *outs):
    grad = jnp.sum(grads[...].astype(f32), axis=0)
    for out, value in zip(outs, adam_step(param[...], moment[...], second[...], grad)):
        out[...] = value


def lay_kernel(*refs):
    parts, out, sems = refs[:-2], refs[-2], refs[-1]
    shards, _, width = parts[0].shape
    copies = []
    for h, part in enumerate(parts):
        for j in range(shards):
            at = pl.ds((j * len(parts) + h) * width, width)
            copies.append(
                pltpu.make_async_copy(part.at[j], out.at[:, at], sems.at[h * shards + j])
            )
    for copy in copies:
        copy.start()
    for copy in copies:
        copy.wait()


def swap(block, axis, bits):
    size = lax.axis_size(axis)
    return lax.ppermute(block, axis, [(i, i ^ bits) for i in range(size)])


def per_device(
    acts,
    cotangent,
    tenant,
    advantage,
    base_weight,
    a_param,
    a_moment,
    a_second,
    b_param,
    b_moment,
    b_second,
):
    owners = lax.axis_size("dp")
    shards = lax.axis_size("fsdp")
    row_count, keys = cotangent.shape
    features, columns = a_param.shape
    own_rows = b_param.shape[0]
    rows = row_count * shards

    parts = PARTS
    width = features // parts
    b_lines = own_rows * keys // columns
    cut = shape((shards, row_count, width))
    dma = pltpu.SemaphoreType.DMA

    share, low, *cuts = call(
        functools.partial(prep_kernel, parts),
        [shape((row_count + LABEL_ROWS, keys)), shape((features + b_lines, columns))] + [cut] * parts,
        (acts, cotangent, tenant[None], advantage[None], a_param, b_param),
        [dma((parts * shards,))],
        [ANY] + [VMEM] * 5,
        [VMEM] * 2 + [ANY] * parts,
    )
    shares = [share] + [swap(share, "fsdp", j) for j in range(1, shards)]
    chips = [low] + [swap(low, "dp", k) for k in range(2, owners, 2)]
    blocks = []
    for block in chips:
        blocks += [block, swap(block, "dp", 1)]
    shares[1], *cuts = lax.optimization_barrier((shares[1], *cuts))
    acts_parts = [
        lax.all_to_all(c, "fsdp", split_axis=0, concat_axis=0, tiled=True).reshape(rows, width)
        for c in cuts
    ]

    scaled, label, base = call(
        functools.partial(base_kernel, shards),
        (shape((rows, keys)), shape((8, rows), jnp.int32), shape((rows, features))),
        (*shares, base_weight),
    )
    back = call(
        functools.partial(back_kernel, owners, own_rows),
        shape((ADAPTER_RANK, rows)),
        (*blocks, scaled, label),
        [pltpu.VMEM((owners * own_rows, keys), bf16), dma((owners, keys // columns))],
        [ANY] * owners + [VMEM] * 2,
    )
    backs = [back] + [swap(back, "fsdp", j) for j in range(1, shards)]

    step = min(ROW_STEP, rows)
    factor_scratch = [pltpu.VMEM((features, owners * columns), bf16)]
    sems = [dma((owners,))]
    grad_part = call(
        functools.partial(side_kernel, shards, owners),
        shape((rows, features)),
        (*backs, *blocks, label, base),
        factor_scratch + [pltpu.VMEM((step, owners * columns), bf16)] + sems,
        [VMEM] * shards + [ANY] * owners + [VMEM] * 2,
        vmem=24,
    )
    returned = lax.all_to_all(
        grad_part.reshape(shards, row_count, features), "fsdp", 0, 0, tiled=True
    )
    grad_input = call(
        lay_kernel, shape((row_count, shards * features)), (returned,), [dma((shards,))], [ANY], ANY
    )

    grad_a = []
    for acts_part in acts_parts:
        odd = call(
            functools.partial(first_kernel, shards, owners, 1),
            shape((owners // 2, columns, width)),
            (*backs, label, acts_part),
        )
        even = call(
            functools.partial(first_kernel, shards, owners, 0),
            [shape((columns, width))] * (owners // 2),
            (*backs, label, acts_part, swap(odd, "dp", 1)),
        )
        grad_a.append([even[0]] + [swap(even[n], "dp", 2 * n) for n in range(1, owners // 2)])

    mid = call(
        functools.partial(mid_kernel, owners, parts),
        shape((ADAPTER_RANK, rows)),
        (*blocks, label, *acts_parts),
        factor_scratch + sems,
        [ANY] * owners + [VMEM] * (1 + parts),
    )
    mids = [mid] + [swap(mid, "fsdp", j) for j in range(1, shards)]
    grad_b = call(
        functools.partial(second_kernel, shards, owners),
        shape((owners, own_rows, keys)),
        (*mids, label, scaled),
        [pltpu.VMEM((ADAPTER_RANK, step), f32)],
    )
    new_b = call(
        adam_b_kernel,
        [shape(b_param.shape, f32)] * 3,
        (lax.all_to_all(grad_b, "dp", 0, 0, tiled=True), b_param, b_moment, b_second),
    )
    block = min(256, width)
    steps = width // block
    wide = pl.BlockSpec((columns, block), lambda i: (0, i))
    new_a = (a_param, a_moment, a_second)
    for h in range(parts):
        tall = pl.BlockSpec((block, columns), lambda i, h=h: (h * steps + i, 0))
        new_a = pl.pallas_call(
            functools.partial(adam_a_kernel, owners // 2),
            grid=(steps,),
            out_shape=[shape(a_param.shape, f32)] * 3,
            in_specs=[wide] * (owners // 2) + [tall] * 3,
            out_specs=[tall] * 3,
            compiler_params=pltpu.CompilerParams(vmem_limit_bytes=16 << 20),
        )(*grad_a[h], *new_a)
    return (grad_input, new_a[0], new_a[1], new_a[2], new_b[0], new_b[1], new_b[2])


def solution(mesh):
    rows = P(("dp", "fsdp"), None)
    labels = P(("dp", "fsdp"))
    first = P("fsdp", "dp")
    return jax.shard_map(
        per_device,
        mesh=mesh,
        in_specs=(rows, rows, labels, labels, P("fsdp", None), first, first, first, rows, rows, rows),
        out_specs=(rows, first, first, first, rows, rows, rows),
        check_vma=False,
    )
```

```python
import functools

import jax
import jax.numpy as jnp
from jax import lax
from jax.experimental import pallas as pl
from jax.experimental.pallas import tpu as pltpu
from jax.sharding import PartitionSpec as P

MODEL_WIDTH = 4096
ADAPTER_RANK = 32
TEN_DEV = 8
LANES = 128
ROW_STEP = 512
LABEL_ROWS = 16
VMEM_BYTES = 62 << 20
PARTS = 1

adapter_scale = 2.0
learn_rate = 0.02
beta_one = 0.9
beta_two = 0.999
adam_eps = 1e-08
bias_one = 1.0 - 0.9**10
bias_two = 1.0 - 0.999**10

f32 = jnp.float32
bf16 = jnp.bfloat16
VMEM = pl.BlockSpec(memory_space=pltpu.VMEM)
HBM = pl.BlockSpec(memory_space=pltpu.HBM)
DMA = pltpu.SemaphoreType.DMA

def shape(dims, kind=bf16):
    return jax.ShapeDtypeStruct(tuple(dims), kind)

def call(body, outs, ins, kinds, out_kinds, scratch=()):
    single = not isinstance(outs, (list, tuple))
    outs = [outs] if single else list(outs)
    staged = [x for x, kind in zip(ins, kinds) if kind == "h"]
    staged_outs = [x for x, kind in zip(outs, out_kinds) if kind == "h"]
    count = len(staged) + len(staged_outs)
    buffers = [pltpu.VMEM(x.shape, x.dtype) for x in staged + staged_outs]

    def kernel(*refs):
        refs = list(refs)
        given, made = refs[: len(ins)], refs[len(ins) : len(ins) + len(outs)]
        rest = refs[len(ins) + len(outs) :]
        held, own = rest[:count], rest[count : len(rest) - bool(count)]
        sems = rest[-1]
        loads, stores = [], []
        for n, kind in enumerate(kinds):
            if kind == "h":
                at = len(loads)
                loads.append(pltpu.make_async_copy(given[n], held[at], sems.at[at]))
                given[n] = held[at]
        for n, kind in enumerate(out_kinds):
            if kind == "h":
                at = len(loads) + len(stores)
                stores.append(pltpu.make_async_copy(held[at], made[n], sems.at[at]))
                made[n] = held[at]
        for copy in loads:
            copy.start()

        def ready():
            for copy in loads:
                copy.wait()

        body(ready, *given, *made, *own)
        for copy in stores:
            copy.start()
        for copy in stores:
            copy.wait()

    result = pl.pallas_call(
        kernel,
        out_shape=outs,
        in_specs=[VMEM if kind == "v" else HBM for kind in kinds],
        out_specs=[VMEM if kind == "v" else HBM for kind in out_kinds],
        scratch_shapes=buffers + list(scratch) + ([DMA((count,))] if count else []),
        compiler_params=pltpu.CompilerParams(vmem_limit_bytes=VMEM_BYTES),
        cost_estimate=pl.CostEstimate(flops=0, bytes_accessed=0, transcendentals=0),
    )(*ins)
    return result[0] if single else result

def adam_step(param, moment, second, gradient):
    moment = beta_one * moment + (1.0 - beta_one) * gradient
    second = beta_two * second + (1.0 - beta_two) * gradient * gradient
    step = (learn_rate / bias_one) * moment
    param = param - step / (jnp.sqrt((1.0 / bias_two) * second) + adam_eps)
    return (param, moment, second)

def dot(left, right, left_dim=1, right_dim=0):
    return lax.dot_general(
        left, right, (((left_dim,), (right_dim,)), ((), ())), preferred_element_type=f32
    )

def iota(dims, axis):
    return lax.broadcasted_iota(jnp.int32, dims, axis)

def column_of(row, lanes=LANES):
    n = row.shape[1]
    wide = jnp.broadcast_to(row.astype(f32), (lanes, n))
    return jnp.transpose(wide)

def prep_kernel(parts, ready, *refs):
    acts, cot, tenant, advantage, a_param, b_param, share, low = refs[:8]
    cuts, sems = refs[8 : 8 + parts], refs[-1]
    shards, _, width = cuts[0].shape
    copies = []
    for h in range(parts):
        for j in range(shards):
            at = pl.ds((j * parts + h) * width, width)
            copies.append(
                pltpu.make_async_copy(acts.at[:, at], cuts[h].at[j], sems.at[h * shards + j])
            )
    for copy in copies:
        copy.start()
    ready()
    rows, keys = cot.shape
    factor = column_of(advantage[...]) * 0.25
    factor = jnp.concatenate([factor] * (keys // LANES), axis=1)
    scaled = (cot[...].astype(f32) * factor).astype(bf16)
    t = tenant[...]
    line = iota((LABEL_ROWS, rows), 0)
    owner = jnp.broadcast_to(lax.div(t, TEN_DEV), (LABEL_ROWS, rows))
    local = jnp.broadcast_to(lax.rem(t, TEN_DEV), (LABEL_ROWS, rows))
    labels = jnp.where(line == 0, owner, jnp.where(line == 1, local, 0)).astype(f32)
    labels = labels.astype(bf16)
    for j in range(shards):
        share[j, :rows] = scaled
        share[j, rows:, :rows] = labels
        share[j, rows:, rows:] = jnp.zeros((LABEL_ROWS, keys - rows), bf16)
    features, columns = a_param.shape
    low[:features] = (a_param[...] * MODEL_WIDTH ** (-0.5)).astype(bf16)
    own_rows = b_param.shape[0]
    for q in range(keys // columns):
        part = b_param[:, q * columns : (q + 1) * columns] * ADAPTER_RANK ** (-0.5)
        low[features + q * own_rows : features + (q + 1) * own_rows] = part.astype(bf16)
    for copy in copies:
        copy.wait()

def second_ids(owners, own_rows, rows):
    line = iota((owners * own_rows, rows), 0)
    inner = lax.rem(line, own_rows) + lax.axis_index("fsdp") * own_rows
    return lax.div(line, own_rows) * TEN_DEV + lax.div(inner, ADAPTER_RANK)

def base_kernel(ready, shares, weight, scaled, label, base):
    ready()
    shards, lines, _ = shares.shape
    rd = lines - LABEL_ROWS
    me = lax.axis_index("dp")
    for j in range(shards):
        scaled[j * rd : (j + 1) * rd] = shares[j, :rd]
        ids = shares[j, rd:, :rd].astype(f32).astype(jnp.int32)
        tid = (ids[0:1] ^ me) * TEN_DEV + ids[1:2]
        label[:, j * rd : (j + 1) * rd] = jnp.broadcast_to(tid, (8, rd))
    rows = scaled.shape[0]
    step = min(ROW_STEP, rows)
    for r in range(0, rows, step):
        base[r : r + step] = dot(scaled[r : r + step], weight[...], 1, 1).astype(bf16)

def back_kernel(owners, own_rows, ready, *refs):
    blocks = refs[:owners]
    scaled, label, back, b_all, sems = refs[owners:]
    features = blocks[0].shape[0] - own_rows * scaled.shape[1] // blocks[0].shape[1]
    columns = blocks[0].shape[1]
    rows, keys = scaled.shape
    copies = []
    for k in range(owners):
        for q in range(keys // columns):
            copies.append(
                pltpu.make_async_copy(
                    blocks[k].at[pl.ds(features + q * own_rows, own_rows)],
                    b_all.at[pl.ds(k * own_rows, own_rows), pl.ds(q * columns, columns)],
                    sems.at[k, q],
                )
            )
    for copy in copies:
        copy.start()
    step = min(ROW_STEP, rows)
    ids = second_ids(owners, own_rows, step)
    ready()
    for copy in copies:
        copy.wait()
    for r in range(0, rows, step):
        wide = dot(b_all[...], scaled[r : r + step], 1, 1)
        wide = jnp.where(ids == label[0:1, r : r + step], wide, 0.0)
        if own_rows >= ADAPTER_RANK:
            low = jnp.sum(wide.reshape(-1, ADAPTER_RANK, step), axis=0)
        else:
            low = jnp.sum(wide.reshape(-1, own_rows, step), axis=0)
            low = jnp.concatenate([low] * (ADAPTER_RANK // own_rows), axis=0)
            part = lax.div(iota(low.shape, 0), own_rows)
            place = lax.rem(lax.axis_index("fsdp"), ADAPTER_RANK // own_rows)
            low = jnp.where(part == place, low, 0.0)
        for j in range(back.shape[0]):
            back[j, :, r : r + step] = low.astype(bf16)

def total(parts, at):
    return jnp.sum(parts[:, :, at].astype(f32), axis=0)

def load_factors(a_blocks, a_all, sems):
    columns = a_blocks[0].shape[1]
    copies = [
        pltpu.make_async_copy(
            block.at[pl.ds(0, a_all.shape[0])],
            a_all.at[:, pl.ds(k * columns, columns)],
            sems.at[k],
        )
        for k, block in enumerate(a_blocks)
    ]
    for copy in copies:
        copy.start()
    return copies

def side_kernel(owners, ready, *refs):
    backs, a_blocks = refs[0], refs[1 : 1 + owners]
    label, base, out, a_all, back_wide, sems = refs[1 + owners :]
    copies = load_factors(a_blocks, a_all, sems)
    ready()
    rows, features = out.shape
    step = min(ROW_STEP, rows)
    width = a_all.shape[1]
    for r in range(0, rows, step):
        at = slice(r, r + step)
        low = adapter_scale * jnp.transpose(total(backs, at))
        low = jnp.concatenate([low] * (LANES // ADAPTER_RANK), axis=1)
        where = column_of(label[0:1, at]).astype(jnp.int32) - lax.div(
            iota((step, LANES), 1), ADAPTER_RANK
        )
        for q in range(width // LANES):
            hit = where == q * (LANES // ADAPTER_RANK)
            back_wide[:, q * LANES : (q + 1) * LANES] = jnp.where(hit, low, 0.0).astype(bf16)
        if r == 0:
            for copy in copies:
                copy.wait()
        chunk = min(256, features)
        for c in range(0, features, chunk):
            side = dot(back_wide[...], a_all[c : c + chunk], 1, 1).astype(bf16)
            whole = base[at, c : c + chunk].astype(f32) + side.astype(f32)
            out[at, c : c + chunk] = whole.astype(bf16)

def spread(low, label, k, columns):
    rows = low.shape[1]
    ids = lax.div(iota((columns, rows), 0), ADAPTER_RANK) + k * TEN_DEV
    tall = jnp.concatenate([low] * (columns // ADAPTER_RANK), axis=0)
    return jnp.where(ids == label, tall, 0.0).astype(bf16)

def first_kernel(owners, parity, ready, backs, label, acts, *refs):
    arrived = refs[0] if parity == 0 else None
    outs = refs[parity == 0 :]
    ready()
    coefficient = adapter_scale * MODEL_WIDTH ** (-0.5)
    low = total(backs, slice(None))
    for n in range(owners // 2):
        k = 2 * n + parity
        columns = outs[0].shape[-2]
        grad = coefficient * dot(spread(low, label[0:1], k, columns), acts[...])
        if parity:
            outs[0][n] = grad.astype(bf16)
        else:
            outs[n][...] = (grad + arrived[n].astype(f32)).astype(bf16)

def mid_kernel(owners, parts, ready, *refs):
    a_blocks = refs[:owners]
    label, acts = refs[owners], refs[owners + 1 : owners + 1 + parts]
    out, a_all, sems = refs[owners + 1 + parts :]
    copies = load_factors(a_blocks, a_all, sems)
    ready()
    rows, width = acts[0].shape
    columns = a_blocks[0].shape[1]
    step = min(ROW_STEP, rows)
    for r in range(0, rows, step):
        at = slice(r, r + step)
        where = column_of(label[0:1, at]).astype(jnp.int32) - lax.div(
            iota((step, LANES), 1), ADAPTER_RANK
        )
        low = jnp.zeros((step, LANES), f32)
        for k in range(owners):
            if r == 0:
                copies[k].wait()
            wide = None
            for h in range(parts):
                factor = a_all[h * width : (h + 1) * width, k * columns : (k + 1) * columns]
                term = dot(acts[h][at], factor)
                wide = term if wide is None else wide + term
            for q in range(columns // LANES):
                hit = where == k * TEN_DEV + q * (LANES // ADAPTER_RANK)
                low = low + jnp.where(hit, wide[:, q * LANES : (q + 1) * LANES], 0.0)
        low = jnp.transpose(low).reshape(LANES // ADAPTER_RANK, ADAPTER_RANK, step)
        for j in range(out.shape[0]):
            out[j, :, at] = jnp.sum(low, axis=0).astype(bf16)

def second_kernel(owners, ready, mids, label, scaled, out, held):
    ready()
    own_rows, keys = out.shape[1:]
    rows = scaled.shape[0]
    step = min(ROW_STEP, rows)
    coefficient = adapter_scale * ADAPTER_RANK ** (-0.5)
    ids = second_ids(owners, own_rows, step)
    grad = jnp.zeros((owners * own_rows, keys), f32)
    for r in range(0, rows, step):
        at = slice(r, r + step)
        held[...] = total(mids, at)
        if own_rows >= ADAPTER_RANK:
            low = jnp.concatenate([held[...]] * (owners * own_rows // ADAPTER_RANK), axis=0)
        else:
            first = lax.rem(lax.axis_index("fsdp") * own_rows, ADAPTER_RANK)
            low = held[pl.ds(pl.multiple_of(first, own_rows), own_rows)]
            low = jnp.concatenate([low] * owners, axis=0)
        low = jnp.where(ids == label[0:1, at], low, 0.0).astype(bf16)
        grad = grad + dot(low, scaled[at])
    grad = (coefficient * grad).astype(bf16)
    me = lax.axis_index("dp")
    for k in range(owners):
        out[me ^ k] = grad[k * own_rows : (k + 1) * own_rows]

def adam_a_kernel(count, *refs):
    grads, (param, moment, second), outs = refs[:count], refs[count : count + 3], refs[count + 3 :]
    grad = grads[0][...].astype(f32)
    for part in grads[1:]:
        grad = grad + part[...].astype(f32)
    new = adam_step(param[...], moment[...], second[...], jnp.transpose(grad))
    for out, value in zip(outs, new):
        out[...] = value

def adam_b_kernel(ready, grads, param, moment, second, *outs):
    ready()
    grad = jnp.sum(grads[...].astype(f32), axis=0)
    for out, value in zip(outs, adam_step(param[...], moment[...], second[...], grad)):
        out[...] = value

def lay_kernel(ready, *refs):
    parts, out, sems = refs[:-2], refs[-2], refs[-1]
    shards, _, width = parts[0].shape
    copies = []
    for h, part in enumerate(parts):
        for j in range(shards):
            at = pl.ds((j * len(parts) + h) * width, width)
            copies.append(
                pltpu.make_async_copy(part.at[j], out.at[:, at], sems.at[h * shards + j])
            )
    for copy in copies:
        copy.start()
    for copy in copies:
        copy.wait()

def swap(block, axis, bits):
    size = lax.axis_size(axis)
    return lax.ppermute(block, axis, [(i, i ^ bits) for i in range(size)])

def exchange(blocks, axis):
    return lax.all_to_all(blocks, axis, split_axis=0, concat_axis=0, tiled=True)

def per_device(
    acts,
    cotangent,
    tenant,
    advantage,
    base_weight,
    a_param,
    a_moment,
    a_second,
    b_param,
    b_moment,
    b_second,
):
    owners = lax.axis_size("dp")
    shards = lax.axis_size("fsdp")
    row_count, keys = cotangent.shape
    features, columns = a_param.shape
    own_rows = b_param.shape[0]
    rows = row_count * shards

    parts = PARTS
    width = features // parts
    b_lines = own_rows * keys // columns
    cut = shape((shards, row_count, width))

    share, low, *cuts = call(
        functools.partial(prep_kernel, parts),
        [shape((shards, row_count + LABEL_ROWS, keys)), shape((features + b_lines, columns))]
        + [cut] * parts,
        (acts, cotangent, tenant[None], advantage[None], a_param, b_param),
        "rhhhhh",
        "hh" + "r" * parts,
        [DMA((parts * shards,))],
    )
    shares = exchange(share, "fsdp")
    chips = [swap(low, "dp", k) for k in range(2, owners, 2)]
    own = swap(low, "dp", 1)
    shares, *rest = lax.optimization_barrier((shares, *chips, *cuts))
    chips, cuts = rest[: len(chips)], rest[len(chips) :]
    blocks = [low, own]
    for block in chips:
        blocks += [block, swap(block, "dp", 1)]
    acts_parts = [exchange(c, "fsdp").reshape(rows, width) for c in cuts]

    scaled, label, base = call(
        base_kernel,
        (shape((rows, keys)), shape((8, rows), jnp.int32), shape((rows, features))),
        (shares, base_weight),
        "hh",
        "hvh",
    )
    backs = exchange(
        call(
            functools.partial(back_kernel, owners, own_rows),
            shape((shards, ADAPTER_RANK, rows)),
            (*blocks, scaled, label),
            "r" * owners + "hv",
            "h",
            [pltpu.VMEM((owners * own_rows, keys), bf16), DMA((owners, keys // columns))],
        ),
        "fsdp",
    )

    step = min(ROW_STEP, rows)
    factor_scratch = [pltpu.VMEM((features, owners * columns), bf16)]
    sems = [DMA((owners,))]
    grad_part = call(
        functools.partial(side_kernel, owners),
        shape((rows, features)),
        (backs, *blocks, label, base),
        "h" + "r" * owners + "vh",
        "h",
        factor_scratch + [pltpu.VMEM((step, owners * columns), bf16)] + sems,

    )
    grad_part, *acts_parts = lax.optimization_barrier((grad_part, *acts_parts))
    returned = exchange(grad_part.reshape(shards, row_count, features), "fsdp")
    grad_input = call(
        lay_kernel, shape((row_count, shards * features)), (returned,), "r", "r", [DMA((shards,))]
    )

    grad_a = []
    for acts_part in acts_parts:
        odd = call(
            functools.partial(first_kernel, owners, 1),
            shape((owners // 2, columns, width)),
            (backs, label, acts_part),
            "hvh",
            "h",
        )
        even = call(
            functools.partial(first_kernel, owners, 0),
            [shape((columns, width))] * (owners // 2),
            (backs, label, acts_part, swap(odd, "dp", 1)),
            "hvhh",
            "h" * (owners // 2),
        )
        grad_a.append(list(even))
    label, *grads = lax.optimization_barrier((label, *sum(grad_a, [])))
    grad_a = [grads[h * (owners // 2) : (h + 1) * (owners // 2)] for h in range(parts)]
    grad_a = [[g[0]] + [swap(g[n], "dp", 2 * n) for n in range(1, owners // 2)] for g in grad_a]

    mids = exchange(
        call(
            functools.partial(mid_kernel, owners, parts),
            shape((shards, ADAPTER_RANK, rows)),
            (*blocks, label, *acts_parts),
            "r" * owners + "v" + "h" * parts,
            "h",
            factor_scratch + sems,
        ),
        "fsdp",
    )
    grad_b = call(
        functools.partial(second_kernel, owners),
        shape((owners, own_rows, keys)),
        (mids, label, scaled),
        "hvh",
        "h",
        [pltpu.VMEM((ADAPTER_RANK, step), f32)],
    )
    new_b = call(
        adam_b_kernel,
        [shape(b_param.shape, f32)] * 3,
        (exchange(grad_b, "dp"), b_param, b_moment, b_second),
        "hhhh",
        "hhh",
    )
    block = min(256, width)
    steps = width // block
    wide = pl.BlockSpec((columns, block), lambda i: (0, i))
    new_a = (a_param, a_moment, a_second)
    for h in range(parts):
        tall = pl.BlockSpec((block, columns), lambda i, h=h: (h * steps + i, 0))
        new_a = pl.pallas_call(
            functools.partial(adam_a_kernel, owners // 2),
            grid=(steps,),
            out_shape=[shape(a_param.shape, f32)] * 3,
            in_specs=[wide] * (owners // 2) + [tall] * 3,
            out_specs=[tall] * 3,
            compiler_params=pltpu.CompilerParams(vmem_limit_bytes=VMEM_BYTES),
        )(*grad_a[h], *new_a)
    return (grad_input, new_a[0], new_a[1], new_a[2], new_b[0], new_b[1], new_b[2])

def solution(mesh):
    rows = P(("dp", "fsdp"), None)
    labels = P(("dp", "fsdp"))
    first = P("fsdp", "dp")
    return jax.shard_map(
        per_device,
        mesh=mesh,
        in_specs=(rows, rows, labels, labels, P("fsdp", None), first, first, first, rows, rows, rows),
        out_specs=(rows, first, first, first, rows, rows, rows),
        check_vma=False,
    )
```

```python
import functools

import jax
import jax.numpy as jnp
from jax import lax
from jax.experimental import pallas as pl
from jax.experimental.pallas import tpu as pltpu
from jax.sharding import PartitionSpec as P

MODEL_WIDTH = 4096
ADAPTER_RANK = 32
TEN_DEV = 8
LANES = 128
ROW_STEP = 512
LABEL_ROWS = 16
ROOMY = 48
FULL = 62
PARTS = 1

adapter_scale = 2.0
learn_rate = 0.02
beta_one = 0.9
beta_two = 0.999
adam_eps = 1e-08
bias_one = 1.0 - 0.9**10
bias_two = 1.0 - 0.999**10

f32 = jnp.float32
bf16 = jnp.bfloat16
VMEM = pl.BlockSpec(memory_space=pltpu.VMEM)
HBM = pl.BlockSpec(memory_space=pltpu.HBM)
DMA = pltpu.SemaphoreType.DMA

def shape(dims, kind=bf16):
    return jax.ShapeDtypeStruct(tuple(dims), kind)

def call(body, outs, ins, kinds, out_kinds, scratch=(), vmem=ROOMY):
    single = not isinstance(outs, (list, tuple))
    outs = [outs] if single else list(outs)
    staged = [x for x, kind in zip(ins, kinds) if kind == "h"]
    staged_outs = [x for x, kind in zip(outs, out_kinds) if kind == "h"]
    count = len(staged) + len(staged_outs)
    buffers = [pltpu.VMEM(x.shape, x.dtype) for x in staged + staged_outs]

    def kernel(*refs):
        refs = list(refs)
        given, made = refs[: len(ins)], refs[len(ins) : len(ins) + len(outs)]
        rest = refs[len(ins) + len(outs) :]
        held, own = rest[:count], rest[count : len(rest) - bool(count)]
        sems = rest[-1] if count else None
        loads, stores = [], []
        for n, kind in enumerate(kinds):
            if kind == "h":
                at = len(loads)
                loads.append(pltpu.make_async_copy(given[n], held[at], sems.at[at]))
                given[n] = held[at]
        for n, kind in enumerate(out_kinds):
            if kind == "h":
                at = len(loads) + len(stores)
                stores.append(pltpu.make_async_copy(held[at], made[n], sems.at[at]))
                made[n] = held[at]
        for copy in loads:
            copy.start()

        def ready():
            for copy in loads:
                copy.wait()

        body(ready, *given, *made, *own)
        for copy in stores:
            copy.start()
        for copy in stores:
            copy.wait()

    result = pl.pallas_call(
        kernel,
        out_shape=outs,
        in_specs=[VMEM if kind == "v" else HBM for kind in kinds],
        out_specs=[VMEM if kind == "v" else HBM for kind in out_kinds],
        scratch_shapes=buffers + list(scratch) + ([DMA((count,))] if count else []),
        compiler_params=pltpu.CompilerParams(vmem_limit_bytes=vmem << 20),
        cost_estimate=pl.CostEstimate(flops=0, bytes_accessed=0, transcendentals=0),
    )(*ins)
    return result[0] if single else result

def adam_step(param, moment, second, gradient):
    moment = beta_one * moment + (1.0 - beta_one) * gradient
    second = beta_two * second + (1.0 - beta_two) * gradient * gradient
    step = (learn_rate / bias_one) * moment
    param = param - step / (jnp.sqrt((1.0 / bias_two) * second) + adam_eps)
    return (param, moment, second)

def dot(left, right, left_dim=1, right_dim=0):
    return lax.dot_general(
        left, right, (((left_dim,), (right_dim,)), ((), ())), preferred_element_type=f32
    )

def iota(dims, axis):
    return lax.broadcasted_iota(jnp.int32, dims, axis)

def column_of(row, lanes=LANES):
    n = row.shape[1]
    wide = jnp.broadcast_to(row.astype(f32), (lanes, n))
    return jnp.transpose(wide)

def prep_kernel(parts, ready, *refs):
    acts, cot, tenant, advantage, a_param, b_param, share, low = refs[:8]
    cuts = refs[8:]
    shards, _, width = cuts[0].shape
    ready()
    for h in range(parts):
        for j in range(shards):
            at = (j * parts + h) * width
            cuts[h][j] = acts[:, at : at + width]
    rows, keys = cot.shape
    factor = column_of(advantage[...]) * 0.25
    factor = jnp.concatenate([factor] * (keys // LANES), axis=1)
    scaled = (cot[...].astype(f32) * factor).astype(bf16)
    t = tenant[...]
    line = iota((LABEL_ROWS, rows), 0)
    owner = jnp.broadcast_to(lax.div(t, TEN_DEV), (LABEL_ROWS, rows))
    local = jnp.broadcast_to(lax.rem(t, TEN_DEV), (LABEL_ROWS, rows))
    labels = jnp.where(line == 0, owner, jnp.where(line == 1, local, 0)).astype(f32)
    labels = labels.astype(bf16)
    for j in range(shards):
        share[j, :rows] = scaled
        share[j, rows:, :rows] = labels
        share[j, rows:, rows:] = jnp.zeros((LABEL_ROWS, keys - rows), bf16)
    features, columns = a_param.shape
    low[:features] = (a_param[...] * MODEL_WIDTH ** (-0.5)).astype(bf16)
    own_rows = b_param.shape[0]
    for q in range(keys // columns):
        part = b_param[:, q * columns : (q + 1) * columns] * ADAPTER_RANK ** (-0.5)
        low[features + q * own_rows : features + (q + 1) * own_rows] = part.astype(bf16)

def second_ids(owners, own_rows, rows):
    line = iota((owners * own_rows, rows), 0)
    inner = lax.rem(line, own_rows) + lax.axis_index("fsdp") * own_rows
    return lax.div(line, own_rows) * TEN_DEV + lax.div(inner, ADAPTER_RANK)

def base_kernel(ready, shares, weight, scaled, label, base):
    ready()
    shards, lines, _ = shares.shape
    rd = lines - LABEL_ROWS
    me = lax.axis_index("dp")
    for j in range(shards):
        scaled[j * rd : (j + 1) * rd] = shares[j, :rd]
        ids = shares[j, rd:, :rd].astype(f32).astype(jnp.int32)
        tid = (ids[0:1] ^ me) * TEN_DEV + ids[1:2]
        label[:, j * rd : (j + 1) * rd] = jnp.broadcast_to(tid, (8, rd))
    rows = scaled.shape[0]
    step = min(ROW_STEP, rows)
    for r in range(0, rows, step):
        base[r : r + step] = dot(scaled[r : r + step], weight[...], 1, 1).astype(bf16)

def back_kernel(owners, own_rows, ready, *refs):
    blocks = refs[:owners]
    scaled, label, back, b_all, sems = refs[owners:]
    features = blocks[0].shape[0] - own_rows * scaled.shape[1] // blocks[0].shape[1]
    columns = blocks[0].shape[1]
    rows, keys = scaled.shape
    copies = []
    for k in range(owners):
        for q in range(keys // columns):
            copies.append(
                pltpu.make_async_copy(
                    blocks[k].at[pl.ds(features + q * own_rows, own_rows)],
                    b_all.at[pl.ds(k * own_rows, own_rows), pl.ds(q * columns, columns)],
                    sems.at[k, q],
                )
            )
    for copy in copies:
        copy.start()
    step = min(ROW_STEP, rows)
    ids = second_ids(owners, own_rows, step)
    ready()
    for copy in copies:
        copy.wait()
    for r in range(0, rows, step):
        wide = dot(b_all[...], scaled[r : r + step], 1, 1)
        wide = jnp.where(ids == label[0:1, r : r + step], wide, 0.0)
        if own_rows >= ADAPTER_RANK:
            low = jnp.sum(wide.reshape(-1, ADAPTER_RANK, step), axis=0)
        else:
            low = jnp.sum(wide.reshape(-1, own_rows, step), axis=0)
            low = jnp.concatenate([low] * (ADAPTER_RANK // own_rows), axis=0)
            part = lax.div(iota(low.shape, 0), own_rows)
            place = lax.rem(lax.axis_index("fsdp"), ADAPTER_RANK // own_rows)
            low = jnp.where(part == place, low, 0.0)
        back[:, r : r + step] = low.astype(bf16)

def total(parts, at):
    value = parts[0][:, at].astype(f32)
    for part in parts[1:]:
        value = value + part[:, at].astype(f32)
    return value

def load_factors(a_blocks, a_all, sems):
    columns = a_blocks[0].shape[1]
    copies = [
        pltpu.make_async_copy(
            block.at[pl.ds(0, a_all.shape[0])],
            a_all.at[:, pl.ds(k * columns, columns)],
            sems.at[k],
        )
        for k, block in enumerate(a_blocks)
    ]
    for copy in copies:
        copy.start()
    return copies

def side_kernel(shards, owners, ready, *refs):
    backs, a_blocks = refs[:shards], refs[shards : shards + owners]
    label, base, out, a_all, back_wide, sems = refs[shards + owners :]
    copies = load_factors(a_blocks, a_all, sems)
    ready()
    rows, features = out.shape
    step = min(ROW_STEP, rows)
    width = a_all.shape[1]
    for r in range(0, rows, step):
        at = slice(r, r + step)
        low = adapter_scale * jnp.transpose(total(backs, at))
        low = jnp.concatenate([low] * (LANES // ADAPTER_RANK), axis=1)
        where = column_of(label[0:1, at]).astype(jnp.int32) - lax.div(
            iota((step, LANES), 1), ADAPTER_RANK
        )
        for q in range(width // LANES):
            hit = where == q * (LANES // ADAPTER_RANK)
            back_wide[:, q * LANES : (q + 1) * LANES] = jnp.where(hit, low, 0.0).astype(bf16)
        if r == 0:
            for copy in copies:
                copy.wait()
        chunk = min(256, features)
        for c in range(0, features, chunk):
            side = dot(back_wide[...], a_all[c : c + chunk], 1, 1).astype(bf16)
            whole = base[at, c : c + chunk].astype(f32) + side.astype(f32)
            out[at, c : c + chunk] = whole.astype(bf16)

def spread(low, label, k, columns):
    rows = low.shape[1]
    ids = lax.div(iota((columns, rows), 0), ADAPTER_RANK) + k * TEN_DEV
    tall = jnp.concatenate([low] * (columns // ADAPTER_RANK), axis=0)
    return jnp.where(ids == label, tall, 0.0).astype(bf16)

def first_kernel(shards, owners, parity, ready, *refs):
    backs, (label, acts) = refs[:shards], refs[shards : shards + 2]
    arrived = refs[shards + 2] if parity == 0 else None
    outs = refs[shards + 2 + (parity == 0) :]
    ready()
    coefficient = adapter_scale * MODEL_WIDTH ** (-0.5)
    low = total(backs, slice(None))
    for n in range(owners // 2):
        k = 2 * n + parity
        columns = outs[0].shape[-2]
        grad = coefficient * dot(spread(low, label[0:1], k, columns), acts[...])
        if parity:
            outs[0][n] = grad.astype(bf16)
        else:
            outs[n][...] = (grad + arrived[n].astype(f32)).astype(bf16)

def mid_kernel(owners, parts, ready, *refs):
    a_blocks = refs[:owners]
    label, acts = refs[owners], refs[owners + 1 : owners + 1 + parts]
    out, a_all, sems = refs[owners + 1 + parts :]
    copies = load_factors(a_blocks, a_all, sems)
    ready()
    rows, width = acts[0].shape
    columns = a_blocks[0].shape[1]
    step = min(ROW_STEP, rows)
    for r in range(0, rows, step):
        at = slice(r, r + step)
        where = column_of(label[0:1, at]).astype(jnp.int32) - lax.div(
            iota((step, LANES), 1), ADAPTER_RANK
        )
        low = jnp.zeros((step, LANES), f32)
        for k in range(owners):
            if r == 0:
                copies[k].wait()
            wide = None
            for h in range(parts):
                factor = a_all[h * width : (h + 1) * width, k * columns : (k + 1) * columns]
                term = dot(acts[h][at], factor)
                wide = term if wide is None else wide + term
            for q in range(columns // LANES):
                hit = where == k * TEN_DEV + q * (LANES // ADAPTER_RANK)
                low = low + jnp.where(hit, wide[:, q * LANES : (q + 1) * LANES], 0.0)
        low = jnp.transpose(low).reshape(LANES // ADAPTER_RANK, ADAPTER_RANK, step)
        out[:, at] = jnp.sum(low, axis=0).astype(bf16)

def second_kernel(shards, owners, ready, *refs):
    mids, (label, scaled, out, held) = refs[:shards], refs[shards:]
    own_rows, keys = out.shape[1:]
    rows = scaled.shape[0]
    step = min(ROW_STEP, rows)
    coefficient = adapter_scale * ADAPTER_RANK ** (-0.5)
    ids = second_ids(owners, own_rows, step)
    grad = jnp.zeros((owners * own_rows, keys), f32)
    for r in range(0, rows, step):
        at = slice(r, r + step)
        held[...] = total(mids, at)
        if own_rows >= ADAPTER_RANK:
            low = jnp.concatenate([held[...]] * (owners * own_rows // ADAPTER_RANK), axis=0)
        else:
            first = lax.rem(lax.axis_index("fsdp") * own_rows, ADAPTER_RANK)
            low = held[pl.ds(pl.multiple_of(first, own_rows), own_rows)]
            low = jnp.concatenate([low] * owners, axis=0)
        low = jnp.where(ids == label[0:1, at], low, 0.0).astype(bf16)
        grad = grad + dot(low, scaled[at])
    grad = (coefficient * grad).astype(bf16)
    me = lax.axis_index("dp")
    for k in range(owners):
        out[me ^ k] = grad[k * own_rows : (k + 1) * own_rows]

def adam_a_kernel(count, *refs):
    grads, (param, moment, second), outs = refs[:count], refs[count : count + 3], refs[count + 3 :]
    grad = grads[0][...].astype(f32)
    for part in grads[1:]:
        grad = grad + part[...].astype(f32)
    new = adam_step(param[...], moment[...], second[...], jnp.transpose(grad))
    for out, value in zip(outs, new):
        out[...] = value

def adam_b_kernel(ready, grads, param, moment, second, *outs):
    ready()
    grad = jnp.sum(grads[...].astype(f32), axis=0)
    for out, value in zip(outs, adam_step(param[...], moment[...], second[...], grad)):
        out[...] = value

def lay_kernel(ready, *refs):
    parts, out, sems = refs[:-2], refs[-2], refs[-1]
    ready()
    shards, _, width = parts[0].shape
    copies = []
    for h, part in enumerate(parts):
        for j in range(shards):
            at = pl.ds((j * len(parts) + h) * width, width)
            copies.append(
                pltpu.make_async_copy(part.at[j], out.at[:, at], sems.at[h * shards + j])
            )
    for copy in copies:
        copy.start()
    for copy in copies:
        copy.wait()

def swap(block, axis, bits):
    size = lax.axis_size(axis)
    return lax.ppermute(block, axis, [(i, i ^ bits) for i in range(size)])

def exchange(blocks, axis):
    return lax.all_to_all(blocks, axis, split_axis=0, concat_axis=0, tiled=True)

def per_device(
    acts,
    cotangent,
    tenant,
    advantage,
    base_weight,
    a_param,
    a_moment,
    a_second,
    b_param,
    b_moment,
    b_second,
):
    owners = lax.axis_size("dp")
    shards = lax.axis_size("fsdp")
    row_count, keys = cotangent.shape
    features, columns = a_param.shape
    own_rows = b_param.shape[0]
    rows = row_count * shards

    parts = PARTS
    width = features // parts
    b_lines = own_rows * keys // columns
    cut = shape((shards, row_count, width))

    share, low, *cuts = call(
        functools.partial(prep_kernel, parts),
        [shape((shards, row_count + LABEL_ROWS, keys)), shape((features + b_lines, columns))]
        + [cut] * parts,
        (acts, cotangent, tenant[None], advantage[None], a_param, b_param),
        "h" * 6,
        "hh" + "h" * parts,
        vmem=FULL,
    )
    shares = exchange(share, "fsdp")
    chips = [swap(low, "dp", k) for k in range(2, owners, 2)]
    own = swap(low, "dp", 1)
    shares, *rest = lax.optimization_barrier((shares, *chips, *cuts))
    chips, cuts = rest[: len(chips)], rest[len(chips) :]
    blocks = [low, own]
    for block in chips:
        blocks += [block, swap(block, "dp", 1)]
    acts_parts = [exchange(c, "fsdp").reshape(rows, width) for c in cuts]

    scaled, label, base = call(
        base_kernel,
        (shape((rows, keys)), shape((8, rows), jnp.int32), shape((rows, features))),
        (shares, base_weight),
        "vv",
        "vvv",
    )
    back = call(
        functools.partial(back_kernel, owners, own_rows),
        shape((ADAPTER_RANK, rows)),
        (*blocks, scaled, label),
        "r" * owners + "vv",
        "v",
        [pltpu.VMEM((owners * own_rows, keys), bf16), DMA((owners, keys // columns))],
    )
    backs = [back] + [swap(back, "fsdp", j) for j in range(1, shards)]

    step = min(ROW_STEP, rows)
    factor_scratch = [pltpu.VMEM((features, owners * columns), bf16)]
    sems = [DMA((owners,))]
    grad_part = call(
        functools.partial(side_kernel, shards, owners),
        shape((rows, features)),
        (*backs, *blocks, label, base),
        "v" * shards + "r" * owners + "vv",
        "v",
        factor_scratch + [pltpu.VMEM((step, owners * columns), bf16)] + sems,

    )
    grad_part, *acts_parts = lax.optimization_barrier((grad_part, *acts_parts))
    returned = exchange(grad_part.reshape(shards, row_count, features), "fsdp")
    grad_input = call(
        lay_kernel, shape((row_count, shards * features)), (returned,), "h", "r", [DMA((shards,))], FULL
    )

    grad_a = []
    for acts_part in acts_parts:
        odd = call(
            functools.partial(first_kernel, shards, owners, 1),
            shape((owners // 2, columns, width)),
            (*backs, label, acts_part),
            "v" * (shards + 2),
            "v",
        )
        even = call(
            functools.partial(first_kernel, shards, owners, 0),
            [shape((columns, width))] * (owners // 2),
            (*backs, label, acts_part, swap(odd, "dp", 1)),
            "v" * (shards + 3),
            "v" * (owners // 2),
        )
        grad_a.append(list(even))
    label, *grads = lax.optimization_barrier((label, *sum(grad_a, [])))
    grad_a = [grads[h * (owners // 2) : (h + 1) * (owners // 2)] for h in range(parts)]
    grad_a = [[g[0]] + [swap(g[n], "dp", 2 * n) for n in range(1, owners // 2)] for g in grad_a]

    mid = call(
        functools.partial(mid_kernel, owners, parts),
        shape((ADAPTER_RANK, rows)),
        (*blocks, label, *acts_parts),
        "r" * owners + "v" * (1 + parts),
        "v",
        factor_scratch + sems,
    )
    mids = [mid] + [swap(mid, "fsdp", j) for j in range(1, shards)]
    grad_b = call(
        functools.partial(second_kernel, shards, owners),
        shape((owners, own_rows, keys)),
        (*mids, label, scaled),
        "v" * (shards + 2),
        "v",
        [pltpu.VMEM((ADAPTER_RANK, step), f32)],
    )
    new_b = call(
        adam_b_kernel,
        [shape(b_param.shape, f32)] * 3,
        (exchange(grad_b, "dp"), b_param, b_moment, b_second),
        "vvvv",
        "vvv",
    )
    block = min(256, width)
    steps = width // block
    wide = pl.BlockSpec((columns, block), lambda i: (0, i))
    new_a = (a_param, a_moment, a_second)
    for h in range(parts):
        tall = pl.BlockSpec((block, columns), lambda i, h=h: (h * steps + i, 0))
        new_a = pl.pallas_call(
            functools.partial(adam_a_kernel, owners // 2),
            grid=(steps,),
            out_shape=[shape(a_param.shape, f32)] * 3,
            in_specs=[wide] * (owners // 2) + [tall] * 3,
            out_specs=[tall] * 3,
            compiler_params=pltpu.CompilerParams(vmem_limit_bytes=FULL << 20),
        )(*grad_a[h], *new_a)
    return (grad_input, new_a[0], new_a[1], new_a[2], new_b[0], new_b[1], new_b[2])

def solution(mesh):
    rows = P(("dp", "fsdp"), None)
    labels = P(("dp", "fsdp"))
    first = P("fsdp", "dp")
    return jax.shard_map(
        per_device,
        mesh=mesh,
        in_specs=(rows, rows, labels, labels, P("fsdp", None), first, first, first, rows, rows, rows),
        out_specs=(rows, first, first, first, rows, rows, rows),
        check_vma=False,
    )
```

```python
import functools

import jax
import jax.numpy as jnp
from jax import lax
from jax.experimental import pallas as pl
from jax.experimental.pallas import tpu as pltpu
from jax.sharding import PartitionSpec as P

MODEL_WIDTH = 4096
ADAPTER_RANK = 32
TEN_DEV = 8
LANES = 128
ROW_STEP = 512
LABEL_ROWS = 16
ROOMY = 48
FULL = 62
PARTS = 1

adapter_scale = 2.0
learn_rate = 0.02
beta_one = 0.9
beta_two = 0.999
adam_eps = 1e-08
bias_one = 1.0 - 0.9**10
bias_two = 1.0 - 0.999**10

f32 = jnp.float32
bf16 = jnp.bfloat16
VMEM = pl.BlockSpec(memory_space=pltpu.VMEM)
HBM = pl.BlockSpec(memory_space=pltpu.HBM)
DMA = pltpu.SemaphoreType.DMA

def shape(dims, kind=bf16):
    return jax.ShapeDtypeStruct(tuple(dims), kind)

def call(body, outs, ins, kinds, out_kinds, scratch=(), vmem=ROOMY, work=0):
    single = not isinstance(outs, (list, tuple))
    outs = [outs] if single else list(outs)
    staged = [x for x, kind in zip(ins, kinds) if kind == "h"]
    staged_outs = [x for x, kind in zip(outs, out_kinds) if kind == "h"]
    count = len(staged) + len(staged_outs)
    buffers = [pltpu.VMEM(x.shape, x.dtype) for x in staged + staged_outs]

    def kernel(*refs):
        refs = list(refs)
        given, made = refs[: len(ins)], refs[len(ins) : len(ins) + len(outs)]
        rest = refs[len(ins) + len(outs) :]
        held, own = rest[:count], rest[count : len(rest) - bool(count)]
        sems = rest[-1] if count else None
        loads, stores = [], []
        for n, kind in enumerate(kinds):
            if kind == "h":
                at = len(loads)
                loads.append(pltpu.make_async_copy(given[n], held[at], sems.at[at]))
                given[n] = held[at]
        for n, kind in enumerate(out_kinds):
            if kind == "h":
                at = len(loads) + len(stores)
                stores.append(pltpu.make_async_copy(held[at], made[n], sems.at[at]))
                made[n] = held[at]
        for copy in loads:
            copy.start()

        def ready():
            for copy in loads:
                copy.wait()

        body(ready, *given, *made, *own)
        for copy in stores:
            copy.start()
        for copy in stores:
            copy.wait()

    result = pl.pallas_call(
        kernel,
        out_shape=outs,
        in_specs=[VMEM if kind == "v" else HBM for kind in kinds],
        out_specs=[VMEM if kind == "v" else HBM for kind in out_kinds],
        scratch_shapes=buffers + list(scratch) + ([DMA((count,))] if count else []),
        compiler_params=pltpu.CompilerParams(vmem_limit_bytes=vmem << 20),
        cost_estimate=pl.CostEstimate(flops=work, bytes_accessed=0, transcendentals=0),
    )(*ins)
    return result[0] if single else result

def adam_step(param, moment, second, gradient):
    moment = beta_one * moment + (1.0 - beta_one) * gradient
    second = beta_two * second + (1.0 - beta_two) * gradient * gradient
    step = (learn_rate / bias_one) * moment
    param = param - step / (jnp.sqrt((1.0 / bias_two) * second) + adam_eps)
    return (param, moment, second)

def dot(left, right, left_dim=1, right_dim=0):
    return lax.dot_general(
        left, right, (((left_dim,), (right_dim,)), ((), ())), preferred_element_type=f32
    )

def iota(dims, axis):
    return lax.broadcasted_iota(jnp.int32, dims, axis)

def column_of(row, lanes=LANES):
    n = row.shape[1]
    wide = jnp.broadcast_to(row.astype(f32), (lanes, n))
    return jnp.transpose(wide)

def prep_kernel(parts, ready, *refs):
    acts, cot, tenant, advantage, a_param, b_param, share, low = refs[:8]
    cuts = refs[8:]
    shards, _, width = cuts[0].shape
    ready()
    for h in range(parts):
        for j in range(shards):
            at = (j * parts + h) * width
            cuts[h][j] = acts[:, at : at + width]
    rows, keys = cot.shape
    factor = column_of(advantage[...]) * 0.25
    factor = jnp.concatenate([factor] * (keys // LANES), axis=1)
    scaled = (cot[...].astype(f32) * factor).astype(bf16)
    t = tenant[...]
    line = iota((LABEL_ROWS, rows), 0)
    owner = jnp.broadcast_to(lax.div(t, TEN_DEV), (LABEL_ROWS, rows))
    local = jnp.broadcast_to(lax.rem(t, TEN_DEV), (LABEL_ROWS, rows))
    labels = jnp.where(line == 0, owner, jnp.where(line == 1, local, 0)).astype(f32)
    labels = labels.astype(bf16)
    for j in range(shards):
        share[j, :rows] = scaled
        share[j, rows:, :rows] = labels
        share[j, rows:, rows:] = jnp.zeros((LABEL_ROWS, keys - rows), bf16)
    features, columns = a_param.shape
    low[:features] = (a_param[...] * MODEL_WIDTH ** (-0.5)).astype(bf16)
    own_rows = b_param.shape[0]
    for q in range(keys // columns):
        part = b_param[:, q * columns : (q + 1) * columns] * ADAPTER_RANK ** (-0.5)
        low[features + q * own_rows : features + (q + 1) * own_rows] = part.astype(bf16)

def second_ids(owners, own_rows, rows):
    line = iota((owners * own_rows, rows), 0)
    inner = lax.rem(line, own_rows) + lax.axis_index("fsdp") * own_rows
    return lax.div(line, own_rows) * TEN_DEV + lax.div(inner, ADAPTER_RANK)

def base_kernel(ready, shares, weight, scaled, label, base):
    ready()
    shards, lines, _ = shares.shape
    rd = lines - LABEL_ROWS
    me = lax.axis_index("dp")
    for j in range(shards):
        scaled[j * rd : (j + 1) * rd] = shares[j, :rd]
        ids = shares[j, rd:, :rd].astype(f32).astype(jnp.int32)
        tid = (ids[0:1] ^ me) * TEN_DEV + ids[1:2]
        label[:, j * rd : (j + 1) * rd] = jnp.broadcast_to(tid, (8, rd))
    rows = scaled.shape[0]
    step = min(ROW_STEP, rows)
    for r in range(0, rows, step):
        base[r : r + step] = dot(scaled[r : r + step], weight[...], 1, 1).astype(bf16)

def back_kernel(owners, own_rows, ready, *refs):
    blocks = refs[:owners]
    scaled, label, back, b_all, sems = refs[owners:]
    features = blocks[0].shape[0] - own_rows * scaled.shape[1] // blocks[0].shape[1]
    columns = blocks[0].shape[1]
    rows, keys = scaled.shape
    copies = []
    for k in range(owners):
        for q in range(keys // columns):
            copies.append(
                pltpu.make_async_copy(
                    blocks[k].at[pl.ds(features + q * own_rows, own_rows)],
                    b_all.at[pl.ds(k * own_rows, own_rows), pl.ds(q * columns, columns)],
                    sems.at[k, q],
                )
            )
    for copy in copies:
        copy.start()
    step = min(ROW_STEP, rows)
    ids = second_ids(owners, own_rows, step)
    ready()
    for copy in copies:
        copy.wait()
    for r in range(0, rows, step):
        wide = dot(b_all[...], scaled[r : r + step], 1, 1)
        wide = jnp.where(ids == label[0:1, r : r + step], wide, 0.0)
        if own_rows >= ADAPTER_RANK:
            low = jnp.sum(wide.reshape(-1, ADAPTER_RANK, step), axis=0)
        else:
            low = jnp.sum(wide.reshape(-1, own_rows, step), axis=0)
            low = jnp.concatenate([low] * (ADAPTER_RANK // own_rows), axis=0)
            part = lax.div(iota(low.shape, 0), own_rows)
            place = lax.rem(lax.axis_index("fsdp"), ADAPTER_RANK // own_rows)
            low = jnp.where(part == place, low, 0.0)
        back[:, r : r + step] = low.astype(bf16)

def total(parts, at):
    value = parts[0][:, at].astype(f32)
    for part in parts[1:]:
        value = value + part[:, at].astype(f32)
    return value

def load_factors(a_blocks, a_all, sems):
    columns = a_blocks[0].shape[1]
    copies = [
        pltpu.make_async_copy(
            block.at[pl.ds(0, a_all.shape[0])],
            a_all.at[:, pl.ds(k * columns, columns)],
            sems.at[k],
        )
        for k, block in enumerate(a_blocks)
    ]
    for copy in copies:
        copy.start()
    return copies

def side_kernel(shards, owners, ready, *refs):
    backs, a_blocks = refs[:shards], refs[shards : shards + owners]
    label, base, out, a_all, back_wide, sems = refs[shards + owners :]
    copies = load_factors(a_blocks, a_all, sems)
    ready()
    rows, features = out.shape
    step = min(ROW_STEP, rows)
    width = a_all.shape[1]
    for r in range(0, rows, step):
        at = slice(r, r + step)
        low = adapter_scale * jnp.transpose(total(backs, at))
        low = jnp.concatenate([low] * (LANES // ADAPTER_RANK), axis=1)
        where = column_of(label[0:1, at]).astype(jnp.int32) - lax.div(
            iota((step, LANES), 1), ADAPTER_RANK
        )
        for q in range(width // LANES):
            hit = where == q * (LANES // ADAPTER_RANK)
            back_wide[:, q * LANES : (q + 1) * LANES] = jnp.where(hit, low, 0.0).astype(bf16)
        if r == 0:
            for copy in copies:
                copy.wait()
        chunk = min(256, features)
        for c in range(0, features, chunk):
            side = dot(back_wide[...], a_all[c : c + chunk], 1, 1).astype(bf16)
            whole = base[at, c : c + chunk].astype(f32) + side.astype(f32)
            out[at, c : c + chunk] = whole.astype(bf16)

def spread(low, label, k, columns):
    rows = low.shape[1]
    ids = lax.div(iota((columns, rows), 0), ADAPTER_RANK) + k * TEN_DEV
    tall = jnp.concatenate([low] * (columns // ADAPTER_RANK), axis=0)
    return jnp.where(ids == label, tall, 0.0).astype(bf16)

def first_kernel(shards, owners, parity, ready, *refs):
    backs, (label, acts) = refs[:shards], refs[shards : shards + 2]
    arrived = refs[shards + 2] if parity == 0 else None
    out = refs[-1]
    chip = lax.div(lax.axis_index("dp"), 2)
    coefficient = adapter_scale * MODEL_WIDTH ** (-0.5)
    low = total(backs, slice(None))
    for n in range(owners // 2):
        k = 2 * n + parity
        columns = out.shape[1]
        grad = coefficient * dot(spread(low, label[0:1], k, columns), acts[...])
        if parity:
            out[n] = grad.astype(bf16)
        else:
            out[chip ^ n] = (grad + arrived[n].astype(f32)).astype(bf16)

def mid_kernel(owners, parts, ready, *refs):
    a_blocks = refs[:owners]
    label, acts = refs[owners], refs[owners + 1 : owners + 1 + parts]
    out, a_all, sems = refs[owners + 1 + parts :]
    copies = load_factors(a_blocks, a_all, sems)
    ready()
    rows, width = acts[0].shape
    columns = a_blocks[0].shape[1]
    step = min(ROW_STEP, rows)
    for r in range(0, rows, step):
        at = slice(r, r + step)
        where = column_of(label[0:1, at]).astype(jnp.int32) - lax.div(
            iota((step, LANES), 1), ADAPTER_RANK
        )
        low = jnp.zeros((step, LANES), f32)
        for k in range(owners):
            if r == 0:
                copies[k].wait()
            wide = None
            for h in range(parts):
                factor = a_all[h * width : (h + 1) * width, k * columns : (k + 1) * columns]
                term = dot(acts[h][at], factor)
                wide = term if wide is None else wide + term
            for q in range(columns // LANES):
                hit = where == k * TEN_DEV + q * (LANES // ADAPTER_RANK)
                low = low + jnp.where(hit, wide[:, q * LANES : (q + 1) * LANES], 0.0)
        low = jnp.transpose(low).reshape(LANES // ADAPTER_RANK, ADAPTER_RANK, step)
        out[:, at] = jnp.sum(low, axis=0).astype(bf16)

def second_kernel(shards, owners, ready, *refs):
    mids, (label, scaled, out, held) = refs[:shards], refs[shards:]
    own_rows, keys = out.shape[1:]
    rows = scaled.shape[0]
    step = min(ROW_STEP, rows)
    coefficient = adapter_scale * ADAPTER_RANK ** (-0.5)
    ids = second_ids(owners, own_rows, step)
    grad = jnp.zeros((owners * own_rows, keys), f32)
    for r in range(0, rows, step):
        at = slice(r, r + step)
        held[...] = total(mids, at)
        if own_rows >= ADAPTER_RANK:
            low = jnp.concatenate([held[...]] * (owners * own_rows // ADAPTER_RANK), axis=0)
        else:
            first = lax.rem(lax.axis_index("fsdp") * own_rows, ADAPTER_RANK)
            low = held[pl.ds(pl.multiple_of(first, own_rows), own_rows)]
            low = jnp.concatenate([low] * owners, axis=0)
        low = jnp.where(ids == label[0:1, at], low, 0.0).astype(bf16)
        grad = grad + dot(low, scaled[at])
    grad = (coefficient * grad).astype(bf16)
    me = lax.axis_index("dp")
    for k in range(owners):
        out[me ^ k] = grad[k * own_rows : (k + 1) * own_rows]

def adam_a_kernel(grads, param, moment, second, *outs):
    grad = jnp.sum(grads[...].astype(f32), axis=0)
    new = adam_step(param[...], moment[...], second[...], jnp.transpose(grad))
    for out, value in zip(outs, new):
        out[...] = value


def adam_b_kernel(ready, grads, param, moment, second, *outs):
    ready()
    grad = jnp.sum(grads[...].astype(f32), axis=0)
    for out, value in zip(outs, adam_step(param[...], moment[...], second[...], grad)):
        out[...] = value

def lay_kernel(ready, *refs):
    parts, out, sems = refs[:-2], refs[-2], refs[-1]
    ready()
    shards, _, width = parts[0].shape
    copies = []
    for h, part in enumerate(parts):
        for j in range(shards):
            at = pl.ds((j * len(parts) + h) * width, width)
            copies.append(
                pltpu.make_async_copy(part.at[j], out.at[:, at], sems.at[h * shards + j])
            )
    for copy in copies:
        copy.start()
    for copy in copies:
        copy.wait()

def swap(block, axis, bits):
    size = lax.axis_size(axis)
    return lax.ppermute(block, axis, [(i, i ^ bits) for i in range(size)])

def exchange(blocks, axis, groups=None):
    return lax.all_to_all(
        blocks, axis, split_axis=0, concat_axis=0, tiled=True, axis_index_groups=groups
    )

def per_device(
    acts,
    cotangent,
    tenant,
    advantage,
    base_weight,
    a_param,
    a_moment,
    a_second,
    b_param,
    b_moment,
    b_second,
):
    owners = lax.axis_size("dp")
    shards = lax.axis_size("fsdp")
    row_count, keys = cotangent.shape
    features, columns = a_param.shape
    own_rows = b_param.shape[0]
    rows = row_count * shards

    parts = PARTS
    width = features // parts
    b_lines = own_rows * keys // columns
    cut = shape((shards, row_count, width))

    share, low, *cuts = call(
        functools.partial(prep_kernel, parts),
        [shape((shards, row_count + LABEL_ROWS, keys)), shape((features + b_lines, columns))]
        + [cut] * parts,
        (acts, cotangent, tenant[None], advantage[None], a_param, b_param),
        "h" * 6,
        "hh" + "h" * parts,
        vmem=FULL,
    )
    shares = exchange(share, "fsdp")
    chips = [swap(low, "dp", k) for k in range(2, owners, 2)]
    own = swap(low, "dp", 1)
    shares, *cuts = lax.optimization_barrier((shares, *cuts))
    shares, *chips = lax.optimization_barrier((shares, *chips))
    blocks = [low, own]
    for block in chips:
        blocks += [block, swap(block, "dp", 1)]
    acts_parts = [exchange(c, "fsdp").reshape(rows, width) for c in cuts]

    scaled, label, base = call(
        base_kernel,
        (shape((rows, keys)), shape((8, rows), jnp.int32), shape((rows, features))),
        (shares, base_weight),
        "vv",
        "vvv",
    )
    back = call(
        functools.partial(back_kernel, owners, own_rows),
        shape((ADAPTER_RANK, rows)),
        (*blocks, scaled, label),
        "r" * owners + "vv",
        "v",
        [pltpu.VMEM((owners * own_rows, keys), bf16), DMA((owners, keys // columns))],
    )
    backs = [back] + [swap(back, "fsdp", j) for j in range(1, shards)]

    step = min(ROW_STEP, rows)
    factor_scratch = [pltpu.VMEM((features, owners * columns), bf16)]
    sems = [DMA((owners,))]
    odds = [
        call(
            functools.partial(first_kernel, shards, owners, 1),
            shape((owners // 2, columns, width)),
            (*backs, label, acts_part),
            "v" * (shards + 2),
            "v",
        )
        for acts_part in acts_parts
    ]
    base, *odds = lax.optimization_barrier((base, *odds))
    grad_part = call(
        functools.partial(side_kernel, shards, owners),
        shape((rows, features)),
        (*backs, *blocks, label, base),
        "v" * shards + "r" * owners + "vv",
        "v",
        factor_scratch + [pltpu.VMEM((step, owners * columns), bf16)] + sems,

    )
    returned = exchange(grad_part.reshape(shards, row_count, features), "fsdp")
    grad_input = call(
        lay_kernel, shape((row_count, shards * features)), (returned,), "h", "r", [DMA((shards,))], FULL
    )

    evens = [
        call(
            functools.partial(first_kernel, shards, owners, 0),
            shape((owners // 2, columns, width)),
            (*backs, label, acts_part, swap(odd, "dp", 1)),
            "v" * (shards + 3),
            "v",
        )
        for odd, acts_part in zip(odds, acts_parts)
    ]
    label, *evens = lax.optimization_barrier((label, *evens))
    chips = [list(range(core, owners, 2)) for core in range(2)]
    grad_a = [exchange(even, "dp", chips) for even in evens]

    mid = call(
        functools.partial(mid_kernel, owners, parts),
        shape((ADAPTER_RANK, rows)),
        (*blocks, label, *acts_parts),
        "r" * owners + "v" * (1 + parts),
        "v",
        factor_scratch + sems,
        work=12 * rows * features * owners * columns,
    )
    mids = [mid] + [swap(mid, "fsdp", j) for j in range(1, shards)]
    grad_b = call(
        functools.partial(second_kernel, shards, owners),
        shape((owners, own_rows, keys)),
        (*mids, label, scaled),
        "v" * (shards + 2),
        "v",
        [pltpu.VMEM((ADAPTER_RANK, step), f32)],
    )
    new_b = call(
        adam_b_kernel,
        [shape(b_param.shape, f32)] * 3,
        (exchange(grad_b, "dp"), b_param, b_moment, b_second),
        "vvvv",
        "vvv",
    )
    block = min(256, width)
    steps = width // block
    wide = pl.BlockSpec((owners // 2, columns, block), lambda i: (0, 0, i))
    tall = pl.BlockSpec((block, columns), lambda i: (i, 0))
    new_a = pl.pallas_call(
        adam_a_kernel,
        grid=(steps,),
        out_shape=[shape(a_param.shape, f32)] * 3,
        in_specs=[wide] + [tall] * 3,
        out_specs=[tall] * 3,
        compiler_params=pltpu.CompilerParams(vmem_limit_bytes=FULL << 20),
    )(grad_a[0], a_param, a_moment, a_second)
    return (grad_input, new_a[0], new_a[1], new_a[2], new_b[0], new_b[1], new_b[2])

def solution(mesh):
    rows = P(("dp", "fsdp"), None)
    labels = P(("dp", "fsdp"))
    first = P("fsdp", "dp")
    return jax.shard_map(
        per_device,
        mesh=mesh,
        in_specs=(rows, rows, labels, labels, P("fsdp", None), first, first, first, rows, rows, rows),
        out_specs=(rows, first, first, first, rows, rows, rows),
        check_vma=False,
    )
```

```python
import functools

import jax
import jax.numpy as jnp
from jax import lax
from jax.experimental import pallas as pl
from jax.experimental.pallas import tpu as pltpu
from jax.sharding import PartitionSpec as P

MODEL_WIDTH = 4096
ADAPTER_RANK = 32
TEN_DEV = 8
LANES = 128
ROW_STEP = 512
LABEL_ROWS = 16
ROOMY = 48
FULL = 62

adapter_scale = 2.0
learn_rate = 0.02
beta_one = 0.9
beta_two = 0.999
adam_eps = 1e-08
bias_one = 1.0 - 0.9**10
bias_two = 1.0 - 0.999**10

f32 = jnp.float32
bf16 = jnp.bfloat16
VMEM = pl.BlockSpec(memory_space=pltpu.VMEM)
HBM = pl.BlockSpec(memory_space=pltpu.HBM)
DMA = pltpu.SemaphoreType.DMA

def shape(dims, kind=bf16):
    return jax.ShapeDtypeStruct(tuple(dims), kind)

def call(body, outs, ins, kinds, out_kinds, scratch=(), vmem=ROOMY, work=0):
    single = not isinstance(outs, (list, tuple))
    outs = [outs] if single else list(outs)
    staged = [x for x, kind in zip(ins, kinds) if kind == "h"]
    staged_outs = [x for x, kind in zip(outs, out_kinds) if kind == "h"]
    count = len(staged) + len(staged_outs)
    buffers = [pltpu.VMEM(x.shape, x.dtype) for x in staged + staged_outs]

    def kernel(*refs):
        refs = list(refs)
        given, made = refs[: len(ins)], refs[len(ins) : len(ins) + len(outs)]
        rest = refs[len(ins) + len(outs) :]
        held, own = rest[:count], rest[count : len(rest) - bool(count)]
        sems = rest[-1] if count else None
        loads, stores = [], []
        for n, kind in enumerate(kinds):
            if kind == "h":
                at = len(loads)
                loads.append(pltpu.make_async_copy(given[n], held[at], sems.at[at]))
                given[n] = held[at]
        for n, kind in enumerate(out_kinds):
            if kind == "h":
                at = len(loads) + len(stores)
                stores.append(pltpu.make_async_copy(held[at], made[n], sems.at[at]))
                made[n] = held[at]
        for copy in loads:
            copy.start()

        def ready():
            for copy in loads:
                copy.wait()

        body(ready, *given, *made, *own)
        for copy in stores:
            copy.start()
        for copy in stores:
            copy.wait()

    result = pl.pallas_call(
        kernel,
        out_shape=outs,
        in_specs=[VMEM if kind == "v" else HBM for kind in kinds],
        out_specs=[VMEM if kind == "v" else HBM for kind in out_kinds],
        scratch_shapes=buffers + list(scratch) + ([DMA((count,))] if count else []),
        compiler_params=pltpu.CompilerParams(vmem_limit_bytes=vmem << 20),
        cost_estimate=pl.CostEstimate(flops=work, bytes_accessed=0, transcendentals=0),
    )(*ins)
    return result[0] if single else result

def adam_step(param, moment, second, gradient):
    moment = beta_one * moment + (1.0 - beta_one) * gradient
    second = beta_two * second + (1.0 - beta_two) * gradient * gradient
    step = (learn_rate / bias_one) * moment
    param = param - step / (jnp.sqrt((1.0 / bias_two) * second) + adam_eps)
    return (param, moment, second)

def dot(left, right, left_dim=1, right_dim=0):
    return lax.dot_general(
        left, right, (((left_dim,), (right_dim,)), ((), ())), preferred_element_type=f32
    )

def iota(dims, axis):
    return lax.broadcasted_iota(jnp.int32, dims, axis)

def column_of(row, lanes=LANES):
    n = row.shape[1]
    wide = jnp.broadcast_to(row.astype(f32), (lanes, n))
    return jnp.transpose(wide)

def prep_kernel(ready, acts, cot, tenant, advantage, a_param, b_param, packed, low):
    ready()
    rows, keys = cot.shape
    shards, _, unit = packed.shape
    features, columns = a_param.shape
    factor = column_of(advantage[...]) * 0.25
    factor = jnp.concatenate([factor] * (keys // LANES), axis=1)
    scaled = (cot[...].astype(f32) * factor).astype(bf16)
    t = tenant[...]
    line = iota((LABEL_ROWS, rows), 0)
    owner = jnp.broadcast_to(lax.div(t, TEN_DEV), (LABEL_ROWS, rows))
    local = jnp.broadcast_to(lax.rem(t, TEN_DEV), (LABEL_ROWS, rows))
    labels = jnp.where(line == 0, owner, jnp.where(line == 1, local, 0)).astype(f32)
    labels = labels.astype(bf16)
    for j in range(shards):
        for q in range(features // unit):
            at = j * features + q * unit
            packed[j, q * rows : (q + 1) * rows] = acts[:, at : at + unit]
        first = features // unit * rows
        for q in range(keys // unit):
            packed[j, first + q * rows : first + (q + 1) * rows] = scaled[:, q * unit : (q + 1) * unit]
        first += keys // unit * rows
        packed[j, first:, :rows] = labels
        packed[j, first:, rows:] = jnp.zeros((LABEL_ROWS, unit - rows), bf16)
    low[:features] = (a_param[...] * MODEL_WIDTH ** (-0.5)).astype(bf16)
    own_rows = b_param.shape[0]
    for q in range(keys // columns):
        part = b_param[:, q * columns : (q + 1) * columns] * ADAPTER_RANK ** (-0.5)
        low[features + q * own_rows : features + (q + 1) * own_rows] = part.astype(bf16)


def second_ids(count, own_rows, rows):
    line = iota((count * own_rows, rows), 0)
    inner = lax.rem(line, own_rows) + lax.axis_index("fsdp") * own_rows
    return lax.div(line, own_rows) * TEN_DEV + lax.div(inner, ADAPTER_RANK)


def base_kernel(ready, scaled, weight, base):
    rows = scaled.shape[0]
    step = min(ROW_STEP, rows)
    for r in range(0, rows, step):
        base[r : r + step] = dot(scaled[r : r + step], weight[...], 1, 1).astype(bf16)


def load_factors(a_blocks, a_all, sems):
    columns = a_blocks[0].shape[1]
    copies = [
        pltpu.make_async_copy(
            block.at[pl.ds(0, a_all.shape[0])],
            a_all.at[:, pl.ds(k * columns, columns)],
            sems.at[k],
        )
        for k, block in enumerate(a_blocks)
    ]
    for copy in copies:
        copy.start()
    return copies


def open_kernel(owners, own_rows, ready, packed, *refs):
    blocks = refs[:owners]
    acts, scaled, label, both, b_all, a_all, b_sems, sems = refs[owners:]
    rows, features = acts.shape
    keys = scaled.shape[1]
    columns = blocks[0].shape[1]
    shards, _, unit = packed.shape
    rd = rows // shards
    b_copies = []
    for k in range(owners):
        for q in range(keys // columns):
            b_copies.append(
                pltpu.make_async_copy(
                    blocks[k].at[pl.ds(features + q * own_rows, own_rows)],
                    b_all.at[pl.ds(k * own_rows, own_rows), pl.ds(q * columns, columns)],
                    b_sems.at[k, q],
                )
            )
    for copy in b_copies:
        copy.start()
    copies = load_factors(blocks, a_all, sems)
    me = lax.axis_index("dp")
    for j in range(shards):
        at = slice(j * rd, (j + 1) * rd)
        for q in range(features // unit):
            acts[at, q * unit : (q + 1) * unit] = packed[j, q * rd : (q + 1) * rd]
        first = features // unit * rd
        for q in range(keys // unit):
            part = packed[j, first + q * rd : first + (q + 1) * rd]
            scaled[at, q * unit : (q + 1) * unit] = part
        first += keys // unit * rd
        ids = packed[j, first:, :rd].astype(f32).astype(jnp.int32)
        tid = (ids[0:1] ^ me) * TEN_DEV + ids[1:2]
        label[:, at] = jnp.broadcast_to(tid, (8, rd))
    step = min(ROW_STEP, rows)
    ids = second_ids(owners, own_rows, step)
    for copy in b_copies:
        copy.wait()
    for r in range(0, rows, step):
        at = slice(r, r + step)
        wide = dot(b_all[...], scaled[at], 1, 1)
        wide = jnp.where(ids == label[0:1, at], wide, 0.0)
        if own_rows >= ADAPTER_RANK:
            low = jnp.sum(wide.reshape(-1, ADAPTER_RANK, step), axis=0)
        else:
            low = jnp.sum(wide.reshape(-1, own_rows, step), axis=0)
            low = jnp.concatenate([low] * (ADAPTER_RANK // own_rows), axis=0)
            part = lax.div(iota(low.shape, 0), own_rows)
            place = lax.rem(lax.axis_index("fsdp"), ADAPTER_RANK // own_rows)
            low = jnp.where(part == place, low, 0.0)
        both[:ADAPTER_RANK, at] = low.astype(bf16)
        where = column_of(label[0:1, at]).astype(jnp.int32) - lax.div(
            iota((step, LANES), 1), ADAPTER_RANK
        )
        low = jnp.zeros((step, LANES), f32)
        for k in range(owners):
            if r == 0:
                copies[k].wait()
            wide = dot(acts[at], a_all[:, k * columns : (k + 1) * columns])
            for q in range(columns // LANES):
                hit = where == k * TEN_DEV + q * (LANES // ADAPTER_RANK)
                low = low + jnp.where(hit, wide[:, q * LANES : (q + 1) * LANES], 0.0)
        low = jnp.transpose(low).reshape(LANES // ADAPTER_RANK, ADAPTER_RANK, step)
        both[ADAPTER_RANK:, at] = jnp.sum(low, axis=0).astype(bf16)


def total(parts, lines, at):
    value = parts[0][lines, at].astype(f32)
    for part in parts[1:]:
        value = value + part[lines, at].astype(f32)
    return value


BACK = slice(0, ADAPTER_RANK)
MID = slice(ADAPTER_RANK, 2 * ADAPTER_RANK)


def side_kernel(shards, owners, ready, *refs):
    backs, a_blocks = refs[:shards], refs[shards : shards + owners]
    label, base, out, a_all, back_wide, sems = refs[shards + owners :]
    copies = load_factors(a_blocks, a_all, sems)
    ready()
    rows, features = out.shape
    step = min(ROW_STEP, rows)
    width = a_all.shape[1]
    for r in range(0, rows, step):
        at = slice(r, r + step)
        low = adapter_scale * jnp.transpose(total(backs, BACK, at))
        low = jnp.concatenate([low] * (LANES // ADAPTER_RANK), axis=1)
        where = column_of(label[0:1, at]).astype(jnp.int32) - lax.div(
            iota((step, LANES), 1), ADAPTER_RANK
        )
        for q in range(width // LANES):
            hit = where == q * (LANES // ADAPTER_RANK)
            back_wide[:, q * LANES : (q + 1) * LANES] = jnp.where(hit, low, 0.0).astype(bf16)
        if r == 0:
            for copy in copies:
                copy.wait()
        chunk = min(256, features)
        for c in range(0, features, chunk):
            side = dot(back_wide[...], a_all[c : c + chunk], 1, 1).astype(bf16)
            whole = base[at, c : c + chunk].astype(f32) + side.astype(f32)
            out[at, c : c + chunk] = whole.astype(bf16)

def spread(low, label, k, columns):
    rows = low.shape[1]
    ids = lax.div(iota((columns, rows), 0), ADAPTER_RANK) + k * TEN_DEV
    tall = jnp.concatenate([low] * (columns // ADAPTER_RANK), axis=0)
    return jnp.where(ids == label, tall, 0.0).astype(bf16)

def grads_kernel(shards, owners, parity, own_rows, ready, *refs):
    boths, (label, acts, scaled) = refs[:shards], refs[shards : shards + 3]
    refs = refs[shards + 3 :]
    arrived = refs[0] if parity == 0 else None
    outs, held = refs[parity == 0 : -1], refs[-1]
    rows, features = acts.shape
    keys = scaled.shape[1]
    columns = outs[0].shape[-2]
    count = owners // 2
    up = adapter_scale * ADAPTER_RANK ** (-0.5)
    down = adapter_scale * MODEL_WIDTH ** (-0.5)
    step = min(ROW_STEP, rows)
    second = None
    line = iota((count * own_rows, step), 0)
    ids = second_ids(count, own_rows, step)
    ids = ids + (lax.div(line, own_rows) + parity) * TEN_DEV
    for r in range(0, rows, step):
        at = slice(r, r + step)
        held[...] = total(boths, MID, at)
        if own_rows >= ADAPTER_RANK:
            low = jnp.concatenate([held[...]] * (count * own_rows // ADAPTER_RANK), axis=0)
        else:
            first = lax.rem(lax.axis_index("fsdp") * own_rows, ADAPTER_RANK)
            low = held[pl.ds(pl.multiple_of(first, own_rows), own_rows)]
            low = jnp.concatenate([low] * count, axis=0)
        low = jnp.where(ids == label[0:1, at], low, 0.0).astype(bf16)
        term = up * dot(low, scaled[at])
        second = term if second is None else second + term
    low = total(boths, BACK, slice(None))
    for n in range(count):
        out = outs[0].at[n] if parity else outs[n]
        k = 2 * n + parity
        grad = down * dot(spread(low, label[0:1], k, columns), acts[...])
        if parity == 0:
            grad = grad + arrived[n, :, :features].astype(f32)
        out[:, :features] = grad.astype(bf16)
        for q in range(keys // LANES):
            lines = slice(q * own_rows, (q + 1) * own_rows)
            part = second[n * own_rows : (n + 1) * own_rows, q * LANES : (q + 1) * LANES]
            if parity == 0:
                part = part + arrived[n, lines, features:].astype(f32)
            out[lines, features:] = part.astype(bf16)
        used = keys // LANES * own_rows
        if used < columns:
            out[used:, features:] = jnp.zeros((columns - used, LANES), bf16)


def adam_kernel(count, own_rows, *refs):
    grads, ends, refs = refs[:count], refs[count : 2 * count], refs[2 * count :]
    firsts, seconds, outs = refs[:3], refs[3:6], refs[6:]

    def summed(parts):
        value = parts[0][...].astype(f32)
        for part in parts[1:]:
            value = value + part[...].astype(f32)
        return value

    new = adam_step(*[x[...] for x in firsts], jnp.transpose(summed(grads)))
    for out, value in zip(outs[:3], new):
        out[...] = value

    @pl.when(pl.program_id(0) == 0)
    def _():
        grad = summed(ends)
        keys = seconds[0].shape[1]
        for q in range(keys // LANES):
            at = slice(q * LANES, (q + 1) * LANES)
            part = grad[q * own_rows : (q + 1) * own_rows]
            for out, value in zip(outs[3:], adam_step(*[x[:, at] for x in seconds], part)):
                out[:, at] = value


def lay_kernel(ready, blocks, out):
    ready()
    shards, _, width = blocks.shape
    for j in range(shards):
        out[:, j * width : (j + 1) * width] = blocks[j]


def swap(block, axis, bits):
    size = lax.axis_size(axis)
    return lax.ppermute(block, axis, [(i, i ^ bits) for i in range(size)])


def exchange(blocks, axis, groups=None):
    return lax.all_to_all(
        blocks, axis, split_axis=0, concat_axis=0, tiled=True, axis_index_groups=groups
    )

def per_device(
    acts,
    cotangent,
    tenant,
    advantage,
    base_weight,
    a_param,
    a_moment,
    a_second,
    b_param,
    b_moment,
    b_second,
):
    owners = lax.axis_size("dp")
    shards = lax.axis_size("fsdp")
    row_count, keys = cotangent.shape
    features, columns = a_param.shape
    own_rows = b_param.shape[0]
    rows = row_count * shards

    unit = min(features, keys)
    b_lines = own_rows * keys // columns
    lines = (features + keys) // unit * row_count + LABEL_ROWS

    packed, low = call(
        prep_kernel,
        [shape((shards, lines, unit)), shape((features + b_lines, columns))],
        (acts, cotangent, tenant[None], advantage[None], a_param, b_param),
        "h" * 6,
        "hh",
        vmem=FULL,
    )
    packed = exchange(packed, "fsdp")
    chips = [low] + [swap(low, "dp", k) for k in range(2, owners, 2)]
    blocks = []
    for block in chips:
        blocks += [block, swap(block, "dp", 1)]

    step = min(ROW_STEP, rows)
    factors = pltpu.VMEM((features, owners * columns), bf16)
    acts_part, scaled, label, both = call(
        functools.partial(open_kernel, owners, own_rows),
        [
            shape((rows, features)),
            shape((rows, keys)),
            shape((8, rows), jnp.int32),
            shape((2 * ADAPTER_RANK, rows)),
        ],
        (packed, *blocks),
        "v" + "r" * owners,
        "vvvv",
        [
            pltpu.VMEM((owners * own_rows, keys), bf16),
            factors,
            DMA((owners, keys // columns)),
            DMA((owners,)),
        ],
    )
    boths = [both] + [swap(both, "fsdp", j) for j in range(1, shards)]
    base = call(base_kernel, shape((rows, features)), (scaled, base_weight), "vv", "v")

    def grads(parity, outs, *more):
        return call(
            functools.partial(grads_kernel, shards, owners, parity, own_rows),
            outs,
            (*boths, label, acts_part, scaled, *more),
            "v" * (shards + 3 + len(more)),
            "v" * (1 if parity else owners // 2),
            [pltpu.VMEM((ADAPTER_RANK, step), f32)],
        )

    odd = grads(1, shape((owners // 2, columns, features + LANES)))
    base, odd = lax.optimization_barrier((base, odd))
    grad_part = call(
        functools.partial(side_kernel, shards, owners),
        shape((rows, features)),
        (*boths, *blocks, label, base),
        "v" * shards + "r" * owners + "vv",
        "v",
        [factors, pltpu.VMEM((step, owners * columns), bf16), DMA((owners,))],
    )
    returned = exchange(grad_part.reshape(shards, row_count, features), "fsdp")
    grad_input = call(
        lay_kernel, shape((row_count, shards * features)), (returned,), "h", "h", vmem=FULL
    )

    even = grads(0, [shape((columns, features + LANES))] * (owners // 2), swap(odd, "dp", 1))
    sums = [even[0]] + [swap(even[n], "dp", 2 * n) for n in range(1, owners // 2)]

    block = min(256, features)
    wide = pl.BlockSpec((columns, block), lambda i: (0, i))
    end = pl.BlockSpec((columns, LANES), lambda i: (0, features // LANES))
    tall = pl.BlockSpec((block, columns), lambda i: (i, 0))
    flat = pl.BlockSpec((own_rows, keys), lambda i: (0, 0))
    new = pl.pallas_call(
        functools.partial(adam_kernel, owners // 2, own_rows),
        grid=(features // block,),
        out_shape=[shape(a_param.shape, f32)] * 3 + [shape(b_param.shape, f32)] * 3,
        in_specs=[wide] * (owners // 2) + [end] * (owners // 2) + [tall] * 3 + [flat] * 3,
        out_specs=[tall] * 3 + [flat] * 3,
        compiler_params=pltpu.CompilerParams(vmem_limit_bytes=FULL << 20),
    )(*sums, *sums, a_param, a_moment, a_second, b_param, b_moment, b_second)
    return (grad_input, *new)


def solution(mesh):
    rows = P(("dp", "fsdp"), None)
    labels = P(("dp", "fsdp"))
    first = P("fsdp", "dp")
    return jax.shard_map(
        per_device,
        mesh=mesh,
        in_specs=(rows, rows, labels, labels, P("fsdp", None), first, first, first, rows, rows, rows),
        out_specs=(rows, first, first, first, rows, rows, rows),
        check_vma=False,
    )
```

```python
import functools

import jax
import jax.numpy as jnp
from jax import lax
from jax.experimental import pallas as pl
from jax.experimental.pallas import tpu as pltpu
from jax.sharding import PartitionSpec as P

MODEL_WIDTH = 4096
ADAPTER_RANK = 32
TEN_DEV = 8
LANES = 128
ROW_STEP = 512
LABEL_ROWS = 16
FULL = (64 << 20) - (64 << 10)

adapter_scale = 2.0
learn_rate = 0.02
beta_one = 0.9
beta_two = 0.999
adam_eps = 1e-08
bias_one = 1.0 - 0.9**10
bias_two = 1.0 - 0.999**10

f32 = jnp.float32
bf16 = jnp.bfloat16
HBM = pl.BlockSpec(memory_space=pltpu.HBM)
DMA = pltpu.SemaphoreType.DMA

def shape(dims, kind=bf16):
    return jax.ShapeDtypeStruct(tuple(dims), kind)

class Staging:
    def __init__(self, loads, stores):
        self.loads, self.stores, self.gone = loads, stores, set()

    def ready(self):
        for copy in self.loads:
            copy.wait()

    def store(self, n):
        self.stores[n].start()
        self.gone.add(n)

    def finish(self):
        for n in self.stores:
            if n not in self.gone:
                self.store(n)
        for copy in self.stores.values():
            copy.wait()


def call(body, outs, ins, kinds, out_kinds, scratch=()):
    single = not isinstance(outs, (list, tuple))
    outs = [outs] if single else list(outs)
    staged = [x for x, kind in zip(ins, kinds) if kind == "h"]
    staged_outs = [x for x, kind in zip(outs, out_kinds) if kind == "h"]
    count = len(staged) + len(staged_outs)
    buffers = [pltpu.VMEM(x.shape, x.dtype) for x in staged + staged_outs]

    def kernel(*refs):
        refs = list(refs)
        given, made = refs[: len(ins)], refs[len(ins) : len(ins) + len(outs)]
        rest = refs[len(ins) + len(outs) :]
        held, own, sems = rest[:count], rest[count:-1], rest[-1]
        loads, stores = [], {}
        for n, kind in enumerate(kinds):
            if kind == "h":
                at = len(loads)
                loads.append(pltpu.make_async_copy(given[n], held[at], sems.at[at]))
                given[n] = held[at]
        for n, kind in enumerate(out_kinds):
            if kind == "h":
                at = len(loads) + len(stores)
                stores[n] = pltpu.make_async_copy(held[at], made[n], sems.at[at])
                made[n] = held[at]
        for copy in loads:
            copy.start()
        io = Staging(loads, stores)
        body(io, *given, *made, *own)
        io.finish()

    result = pl.pallas_call(
        kernel,
        out_shape=outs,
        in_specs=[HBM] * len(ins),
        out_specs=[HBM] * len(outs),
        scratch_shapes=buffers + list(scratch) + [DMA((count,))],
        compiler_params=pltpu.CompilerParams(vmem_limit_bytes=FULL),
        cost_estimate=pl.CostEstimate(flops=0, bytes_accessed=0, transcendentals=0),
    )(*ins)
    return result[0] if single else result


def adam_step(param, moment, second, gradient):
    moment = beta_one * moment + (1.0 - beta_one) * gradient
    second = beta_two * second + (1.0 - beta_two) * gradient * gradient
    step = (learn_rate / bias_one) * moment
    param = param - step / (jnp.sqrt((1.0 / bias_two) * second) + adam_eps)
    return (param, moment, second)

def dot(left, right, left_dim=1, right_dim=0):
    return lax.dot_general(
        left, right, (((left_dim,), (right_dim,)), ((), ())), preferred_element_type=f32
    )

def iota(dims, axis):
    return lax.broadcasted_iota(jnp.int32, dims, axis)

def column_of(row, lanes=LANES):
    n = row.shape[1]
    wide = jnp.broadcast_to(row.astype(f32), (lanes, n))
    return jnp.transpose(wide)

def prep_kernel(io, acts, cot, tenant, advantage, a_param, b_param, packed, low):
    io.ready()
    rows, keys = cot.shape
    shards, _, unit = packed.shape
    features, columns = a_param.shape
    factor = column_of(advantage[...]) * 0.25
    factor = jnp.concatenate([factor] * (keys // LANES), axis=1)
    scaled = (cot[...].astype(f32) * factor).astype(bf16)
    t = tenant[...]
    line = iota((LABEL_ROWS, rows), 0)
    owner = jnp.broadcast_to(lax.div(t, TEN_DEV), (LABEL_ROWS, rows))
    local = jnp.broadcast_to(lax.rem(t, TEN_DEV), (LABEL_ROWS, rows))
    labels = jnp.where(line == 0, owner, jnp.where(line == 1, local, 0)).astype(f32)
    labels = labels.astype(bf16)
    for j in range(shards):
        for q in range(features // unit):
            at = j * features + q * unit
            packed[j, q * rows : (q + 1) * rows] = acts[:, at : at + unit]
        first = features // unit * rows
        for q in range(keys // unit):
            packed[j, first + q * rows : first + (q + 1) * rows] = scaled[:, q * unit : (q + 1) * unit]
        first += keys // unit * rows
        packed[j, first:, :rows] = labels
        packed[j, first:, rows:] = jnp.zeros((LABEL_ROWS, unit - rows), bf16)
    io.store(0)
    low[:features] = (a_param[...] * MODEL_WIDTH ** (-0.5)).astype(bf16)
    own_rows = b_param.shape[0]
    for q in range(keys // columns):
        part = b_param[:, q * columns : (q + 1) * columns] * ADAPTER_RANK ** (-0.5)
        low[features + q * own_rows : features + (q + 1) * own_rows] = part.astype(bf16)


def second_ids(count, own_rows, rows):
    line = iota((count * own_rows, rows), 0)
    inner = lax.rem(line, own_rows) + lax.axis_index("fsdp") * own_rows
    return lax.div(line, own_rows) * TEN_DEV + lax.div(inner, ADAPTER_RANK)


def load_factors(a_blocks, a_all, sems):
    columns = a_blocks[0].shape[1]
    copies = [
        pltpu.make_async_copy(
            block.at[pl.ds(0, a_all.shape[0])],
            a_all.at[:, pl.ds(k * columns, columns)],
            sems.at[k],
        )
        for k, block in enumerate(a_blocks)
    ]
    for copy in copies:
        copy.start()
    return copies


def open_kernel(owners, own_rows, io, packed, *refs):
    blocks = refs[:owners]
    acts, scaled, label, both, b_all, a_all, b_sems, sems = refs[owners:]
    rows, features = acts.shape
    keys = scaled.shape[1]
    columns = blocks[0].shape[1]
    shards, _, unit = packed.shape
    rd = rows // shards
    b_copies = []
    for k in range(owners):
        for q in range(keys // columns):
            b_copies.append(
                pltpu.make_async_copy(
                    blocks[k].at[pl.ds(features + q * own_rows, own_rows)],
                    b_all.at[pl.ds(k * own_rows, own_rows), pl.ds(q * columns, columns)],
                    b_sems.at[k, q],
                )
            )
    for copy in b_copies:
        copy.start()
    copies = load_factors(blocks, a_all, sems)
    io.ready()
    me = lax.axis_index("dp")
    for j in range(shards):
        at = slice(j * rd, (j + 1) * rd)
        for q in range(features // unit):
            acts[at, q * unit : (q + 1) * unit] = packed[j, q * rd : (q + 1) * rd]
        first = features // unit * rd
        for q in range(keys // unit):
            part = packed[j, first + q * rd : first + (q + 1) * rd]
            scaled[at, q * unit : (q + 1) * unit] = part
        first += keys // unit * rd
        ids = packed[j, first:, :rd].astype(f32).astype(jnp.int32)
        tid = (ids[0:1] ^ me) * TEN_DEV + ids[1:2]
        label[:, at] = jnp.broadcast_to(tid, (8, rd))
    for n in range(3):
        io.store(n)
    step = min(ROW_STEP, rows)
    ids = second_ids(owners, own_rows, step)
    for copy in b_copies:
        copy.wait()
    for r in range(0, rows, step):
        at = slice(r, r + step)
        wide = dot(b_all[...], scaled[at], 1, 1)
        wide = jnp.where(ids == label[0:1, at], wide, 0.0)
        if own_rows >= ADAPTER_RANK:
            low = jnp.sum(wide.reshape(-1, ADAPTER_RANK, step), axis=0)
        else:
            low = jnp.sum(wide.reshape(-1, own_rows, step), axis=0)
            low = jnp.concatenate([low] * (ADAPTER_RANK // own_rows), axis=0)
            part = lax.div(iota(low.shape, 0), own_rows)
            place = lax.rem(lax.axis_index("fsdp"), ADAPTER_RANK // own_rows)
            low = jnp.where(part == place, low, 0.0)
        both[:ADAPTER_RANK, at] = low.astype(bf16)
        where = column_of(label[0:1, at]).astype(jnp.int32) - lax.div(
            iota((step, LANES), 1), ADAPTER_RANK
        )
        low = jnp.zeros((step, LANES), f32)
        for k in range(owners):
            if r == 0:
                copies[k].wait()
            wide = dot(acts[at], a_all[:, k * columns : (k + 1) * columns])
            for q in range(columns // LANES):
                hit = where == k * TEN_DEV + q * (LANES // ADAPTER_RANK)
                low = low + jnp.where(hit, wide[:, q * LANES : (q + 1) * LANES], 0.0)
        low = jnp.transpose(low).reshape(LANES // ADAPTER_RANK, ADAPTER_RANK, step)
        both[ADAPTER_RANK:, at] = jnp.sum(low, axis=0).astype(bf16)


def total(parts, lines, at):
    value = parts[0][lines, at].astype(f32)
    for part in parts[1:]:
        value = value + part[lines, at].astype(f32)
    return value


BACK = slice(0, ADAPTER_RANK)
MID = slice(ADAPTER_RANK, 2 * ADAPTER_RANK)


def spread(low, label, k, columns):
    rows = low.shape[1]
    ids = lax.div(iota((columns, rows), 0), ADAPTER_RANK) + k * TEN_DEV
    tall = jnp.concatenate([low] * (columns // ADAPTER_RANK), axis=0)
    return jnp.where(ids == label, tall, 0.0).astype(bf16)

def second_grads(owners, parity, own_rows, boths, label, scaled, held):
    rows = scaled.shape[0]
    count = owners // 2
    step = min(ROW_STEP, rows)
    second = None
    line = iota((count * own_rows, step), 0)
    ids = second_ids(count, own_rows, step)
    ids = ids + (lax.div(line, own_rows) + parity) * TEN_DEV
    for r in range(0, rows, step):
        at = slice(r, r + step)
        held[...] = total(boths, MID, at)
        if own_rows >= ADAPTER_RANK:
            low = jnp.concatenate([held[...]] * (count * own_rows // ADAPTER_RANK), axis=0)
        else:
            first = lax.rem(lax.axis_index("fsdp") * own_rows, ADAPTER_RANK)
            low = held[pl.ds(pl.multiple_of(first, own_rows), own_rows)]
            low = jnp.concatenate([low] * count, axis=0)
        low = jnp.where(ids == label[0:1, at], low, 0.0).astype(bf16)
        term = dot(low, scaled[at])
        second = term if second is None else second + term
    return adapter_scale * ADAPTER_RANK ** (-0.5) * second


def grads_step(owners, parity, own_rows, boths, label, acts, scaled, held, out, arrived, send):
    features = acts.shape[1]
    keys = scaled.shape[1]
    columns = out.shape[1]
    down = adapter_scale * MODEL_WIDTH ** (-0.5)
    second = second_grads(owners, parity, own_rows, boths, label, scaled, held)
    low = total(boths, BACK, slice(None))
    for n in range(owners // 2):
        grad = down * dot(spread(low, label[0:1], 2 * n + parity, columns), acts[...])
        if arrived is not None:
            grad = grad + arrived[n, :, :features].astype(f32)
        out[n, :, :features] = grad.astype(bf16)
        for q in range(keys // LANES):
            lines = slice(q * own_rows, (q + 1) * own_rows)
            part = second[n * own_rows : (n + 1) * own_rows, q * LANES : (q + 1) * LANES]
            if arrived is not None:
                part = part + arrived[n, lines, features:].astype(f32)
            out[n, lines, features:] = part.astype(bf16)
        used = keys // LANES * own_rows
        if used < columns:
            out[n, used:, features:] = jnp.zeros((columns - used, LANES), bf16)
        send[n].start()


def even_kernel(shards, owners, own_rows, io, *refs):
    boths, (label, acts, scaled, arrived) = refs[:shards], refs[shards : shards + 4]
    outs = refs[shards + 4 : shards + 4 + owners // 2]
    held, made, sems = refs[shards + 4 + owners // 2 :]
    send = [pltpu.make_async_copy(made.at[n], outs[n], sems.at[n]) for n in range(owners // 2)]
    io.ready()
    grads_step(owners, 0, own_rows, boths, label, acts, scaled, held, made, arrived, send)
    for copy in send:
        copy.wait()


def main_kernel(shards, owners, own_rows, io, *refs):
    boths, (label, acts, scaled, weight) = refs[:shards], refs[shards : shards + 4]
    a_blocks = refs[shards + 4 : shards + 4 + owners]
    odd, out, held, made, part, a_all, back_wide, sems, odd_sems, part_sems = refs[
        shards + 4 + owners :
    ]
    copies = load_factors(a_blocks, a_all, sems)
    send = [pltpu.make_async_copy(made.at[n], odd.at[n], odd_sems.at[n]) for n in range(owners // 2)]
    io.ready()
    grads_step(owners, 1, own_rows, boths, label, acts, scaled, held, made, None, send)
    rows, features = part.shape
    step = min(ROW_STEP, rows)
    width = a_all.shape[1]
    chunk = min(256, features)
    for r in range(0, rows, step):
        at = slice(r, r + step)
        low = adapter_scale * jnp.transpose(total(boths, BACK, at))
        low = jnp.concatenate([low] * (LANES // ADAPTER_RANK), axis=1)
        where = column_of(label[0:1, at]).astype(jnp.int32) - lax.div(
            iota((step, LANES), 1), ADAPTER_RANK
        )
        for q in range(width // LANES):
            hit = where == q * (LANES // ADAPTER_RANK)
            back_wide[:, q * LANES : (q + 1) * LANES] = jnp.where(hit, low, 0.0).astype(bf16)
        if r == 0:
            for copy in copies:
                copy.wait()
        for c in range(0, features, chunk):
            base = dot(scaled[at], weight[c : c + chunk], 1, 1).astype(bf16)
            side = dot(back_wide[...], a_all[c : c + chunk], 1, 1).astype(bf16)
            part[at, c : c + chunk] = (base.astype(f32) + side.astype(f32)).astype(bf16)
            copy = pltpu.make_async_copy(
                part.at[pl.ds(r, step), pl.ds(c, chunk)],
                out.at[pl.ds(r, step), pl.ds(c, chunk)],
                part_sems.at[r // step, c // chunk],
            )
            copy.start()
            send.append(copy)
    for copy in send:
        copy.wait()


def adam_kernel(count, own_rows, *refs):
    grads, ends, refs = refs[:count], refs[count : 2 * count], refs[2 * count :]
    firsts, seconds, outs = refs[:3], refs[3:6], refs[6:]

    def summed(parts):
        value = parts[0][...].astype(f32)
        for part in parts[1:]:
            value = value + part[...].astype(f32)
        return value

    new = adam_step(*[x[...] for x in firsts], jnp.transpose(summed(grads)))
    for out, value in zip(outs[:3], new):
        out[...] = value

    @pl.when(pl.program_id(0) == 0)
    def _():
        grad = summed(ends)
        keys = seconds[0].shape[1]
        for q in range(keys // LANES):
            at = slice(q * LANES, (q + 1) * LANES)
            part = grad[q * own_rows : (q + 1) * own_rows]
            for out, value in zip(outs[3:], adam_step(*[x[:, at] for x in seconds], part)):
                out[:, at] = value


def lay_kernel(io, blocks, out):
    io.ready()
    shards, _, width = blocks.shape
    for j in range(shards):
        out[:, j * width : (j + 1) * width] = blocks[j]


def swap(block, axis, bits):
    size = lax.axis_size(axis)
    return lax.ppermute(block, axis, [(i, i ^ bits) for i in range(size)])


def exchange(blocks, axis, groups=None):
    return lax.all_to_all(
        blocks, axis, split_axis=0, concat_axis=0, tiled=True, axis_index_groups=groups
    )

def per_device(
    acts,
    cotangent,
    tenant,
    advantage,
    base_weight,
    a_param,
    a_moment,
    a_second,
    b_param,
    b_moment,
    b_second,
):
    owners = lax.axis_size("dp")
    shards = lax.axis_size("fsdp")
    row_count, keys = cotangent.shape
    features, columns = a_param.shape
    own_rows = b_param.shape[0]
    rows = row_count * shards

    unit = min(features, keys)
    b_lines = own_rows * keys // columns
    lines = (features + keys) // unit * row_count + LABEL_ROWS

    packed, low = call(
        prep_kernel,
        [shape((shards, lines, unit)), shape((features + b_lines, columns))],
        (acts, cotangent, tenant[None], advantage[None], a_param, b_param),
        "h" * 6,
        "hh",
    )
    packed = exchange(packed, "fsdp")
    chips = [low] + [swap(low, "dp", k) for k in range(2, owners, 2)]
    blocks = []
    for block in chips:
        blocks += [block, swap(block, "dp", 1)]

    step = min(ROW_STEP, rows)
    factors = pltpu.VMEM((features, owners * columns), bf16)
    acts_part, scaled, label, both = call(
        functools.partial(open_kernel, owners, own_rows),
        [
            shape((rows, features)),
            shape((rows, keys)),
            shape((8, rows), jnp.int32),
            shape((2 * ADAPTER_RANK, rows)),
        ],
        (packed, *blocks),
        "h" + "r" * owners,
        "hhhh",
        [
            pltpu.VMEM((owners * own_rows, keys), bf16),
            factors,
            DMA((owners, keys // columns)),
            DMA((owners,)),
        ],
    )
    boths = [both] + [swap(both, "fsdp", j) for j in range(1, shards)]

    grads = shape((owners // 2, columns, features + LANES))
    held = [pltpu.VMEM((ADAPTER_RANK, step), f32), pltpu.VMEM(grads.shape, bf16)]
    odd, grad_part = call(
        functools.partial(main_kernel, shards, owners, own_rows),
        [grads, shape((rows, features))],
        (*boths, label, acts_part, scaled, base_weight, *blocks),
        "h" * (shards + 4) + "r" * owners,
        "rr",
        held
        + [
            pltpu.VMEM((rows, features), bf16),
            factors,
            pltpu.VMEM((step, owners * columns), bf16),
            DMA((owners,)),
            DMA((owners // 2,)),
            DMA((rows // step, features // min(256, features))),
        ],
    )
    returned = exchange(grad_part.reshape(shards, row_count, features), "fsdp")
    grad_input = call(
        lay_kernel, shape((row_count, shards * features)), (returned,), "h", "h"
    )
    even = call(
        functools.partial(even_kernel, shards, owners, own_rows),
        [shape((columns, features + LANES))] * (owners // 2),
        (*boths, label, acts_part, scaled, swap(odd, "dp", 1)),
        "h" * (shards + 4),
        "r" * (owners // 2),
        held + [DMA((owners // 2,))],
    )
    sums = [even[0]] + [swap(even[n], "dp", 2 * n) for n in range(1, owners // 2)]

    block = LANES
    wide = pl.BlockSpec((columns, block), lambda i: (0, i))
    end = pl.BlockSpec((columns, LANES), lambda i: (0, features // LANES))
    tall = pl.BlockSpec((block, columns), lambda i: (i, 0))
    flat = pl.BlockSpec((own_rows, keys), lambda i: (0, 0))
    new = pl.pallas_call(
        functools.partial(adam_kernel, owners // 2, own_rows),
        grid=(features // block,),
        out_shape=[shape(a_param.shape, f32)] * 3 + [shape(b_param.shape, f32)] * 3,
        in_specs=[wide] * (owners // 2) + [end] * (owners // 2) + [tall] * 3 + [flat] * 3,
        out_specs=[tall] * 3 + [flat] * 3,
        compiler_params=pltpu.CompilerParams(vmem_limit_bytes=FULL),
    )(*sums, *sums, a_param, a_moment, a_second, b_param, b_moment, b_second)
    return (grad_input, *new)


def solution(mesh):
    rows = P(("dp", "fsdp"), None)
    labels = P(("dp", "fsdp"))
    first = P("fsdp", "dp")
    return jax.shard_map(
        per_device,
        mesh=mesh,
        in_specs=(rows, rows, labels, labels, P("fsdp", None), first, first, first, rows, rows, rows),
        out_specs=(rows, first, first, first, rows, rows, rows),
        check_vma=False,
    )
```

```python
import functools

import jax
import jax.numpy as jnp
from jax import lax
from jax.experimental import pallas as pl
from jax.experimental.pallas import tpu as pltpu
from jax.sharding import PartitionSpec as P

MODEL_WIDTH = 4096
ADAPTER_RANK = 32
TEN_DEV = 8
LANES = 128
ROW_STEP = 512
MID_STEP = 256
LABEL_ROWS = 16
FULL = (64 << 20) - (64 << 10)

adapter_scale = 2.0
learn_rate = 0.02
beta_one = 0.9
beta_two = 0.999
adam_eps = 1e-08
bias_one = 1.0 - 0.9**10
bias_two = 1.0 - 0.999**10

f32 = jnp.float32
bf16 = jnp.bfloat16
HBM = pl.BlockSpec(memory_space=pltpu.HBM)
DMA = pltpu.SemaphoreType.DMA

def shape(dims, kind=bf16):
    return jax.ShapeDtypeStruct(tuple(dims), kind)

class Staging:
    def __init__(self, loads, stores):
        self.loads, self.stores, self.gone = loads, stores, set()

    def ready(self):
        for copy in self.loads:
            copy.wait()

    def store(self, n):
        self.stores[n].start()
        self.gone.add(n)

    def finish(self):
        for n in self.stores:
            if n not in self.gone:
                self.store(n)
        for copy in self.stores.values():
            copy.wait()


def call(body, outs, ins, kinds, out_kinds, scratch=()):
    single = not isinstance(outs, (list, tuple))
    outs = [outs] if single else list(outs)
    staged = [x for x, kind in zip(ins, kinds) if kind == "h"]
    staged_outs = [x for x, kind in zip(outs, out_kinds) if kind == "h"]
    count = len(staged) + len(staged_outs)
    buffers = [pltpu.VMEM(x.shape, x.dtype) for x in staged + staged_outs]

    def kernel(*refs):
        refs = list(refs)
        given, made = refs[: len(ins)], refs[len(ins) : len(ins) + len(outs)]
        rest = refs[len(ins) + len(outs) :]
        held, own, sems = rest[:count], rest[count:-1], rest[-1]
        loads, stores = [], {}
        for n, kind in enumerate(kinds):
            if kind == "h":
                at = len(loads)
                loads.append(pltpu.make_async_copy(given[n], held[at], sems.at[at]))
                given[n] = held[at]
        for n, kind in enumerate(out_kinds):
            if kind == "h":
                at = len(loads) + len(stores)
                stores[n] = pltpu.make_async_copy(held[at], made[n], sems.at[at])
                made[n] = held[at]
        for copy in loads:
            copy.start()
        io = Staging(loads, stores)
        body(io, *given, *made, *own)
        io.finish()

    result = pl.pallas_call(
        kernel,
        out_shape=outs,
        in_specs=[HBM] * len(ins),
        out_specs=[HBM] * len(outs),
        scratch_shapes=buffers + list(scratch) + [DMA((count,))],
        compiler_params=pltpu.CompilerParams(vmem_limit_bytes=FULL),
        cost_estimate=pl.CostEstimate(flops=0, bytes_accessed=0, transcendentals=0),
    )(*ins)
    return result[0] if single else result


def adam_step(param, moment, second, gradient):
    moment = beta_one * moment + (1.0 - beta_one) * gradient
    second = beta_two * second + (1.0 - beta_two) * gradient * gradient
    step = (learn_rate / bias_one) * moment
    param = param - step / (jnp.sqrt((1.0 / bias_two) * second) + adam_eps)
    return (param, moment, second)

def dot(left, right, left_dim=1, right_dim=0):
    return lax.dot_general(
        left, right, (((left_dim,), (right_dim,)), ((), ())), preferred_element_type=f32
    )

def iota(dims, axis):
    return lax.broadcasted_iota(jnp.int32, dims, axis)

def column_of(row, lanes=LANES):
    n = row.shape[1]
    wide = jnp.broadcast_to(row.astype(f32), (lanes, n))
    return jnp.transpose(wide)

def prep_kernel(io, acts, cot, tenant, advantage, a_param, b_param, packed, low):
    io.ready()
    rows, keys = cot.shape
    shards, _, unit = packed.shape
    features, columns = a_param.shape
    factor = column_of(advantage[...]) * 0.25
    factor = jnp.concatenate([factor] * (keys // LANES), axis=1)
    scaled = (cot[...].astype(f32) * factor).astype(bf16)
    t = tenant[...]
    line = iota((LABEL_ROWS, rows), 0)
    owner = jnp.broadcast_to(lax.div(t, TEN_DEV), (LABEL_ROWS, rows))
    local = jnp.broadcast_to(lax.rem(t, TEN_DEV), (LABEL_ROWS, rows))
    labels = jnp.where(line == 0, owner, jnp.where(line == 1, local, 0)).astype(f32)
    labels = labels.astype(bf16)
    for j in range(shards):
        for q in range(features // unit):
            at = j * features + q * unit
            packed[j, q * rows : (q + 1) * rows] = acts[:, at : at + unit]
        first = features // unit * rows
        for q in range(keys // unit):
            packed[j, first + q * rows : first + (q + 1) * rows] = scaled[:, q * unit : (q + 1) * unit]
        first += keys // unit * rows
        packed[j, first:, :rows] = labels
        packed[j, first:, rows:] = jnp.zeros((LABEL_ROWS, unit - rows), bf16)
    io.store(0)
    low[:features] = (a_param[...] * MODEL_WIDTH ** (-0.5)).astype(bf16)
    own_rows = b_param.shape[0]
    for q in range(keys // columns):
        part = b_param[:, q * columns : (q + 1) * columns] * ADAPTER_RANK ** (-0.5)
        low[features + q * own_rows : features + (q + 1) * own_rows] = part.astype(bf16)


def second_ids(count, own_rows, rows):
    line = iota((count * own_rows, rows), 0)
    inner = lax.rem(line, own_rows) + lax.axis_index("fsdp") * own_rows
    return lax.div(line, own_rows) * TEN_DEV + lax.div(inner, ADAPTER_RANK)


def load_factors(a_blocks, a_all, sems):
    columns = a_blocks[0].shape[1]
    copies = [
        pltpu.make_async_copy(
            block.at[pl.ds(0, a_all.shape[0])],
            a_all.at[:, pl.ds(k * columns, columns)],
            sems.at[k],
        )
        for k, block in enumerate(a_blocks)
    ]
    for copy in copies:
        copy.start()
    return copies


def open_kernel(owners, own_rows, io, packed, *refs):
    blocks = refs[:owners]
    acts, scaled, label, both, b_all, a_all, b_sems, sems = refs[owners:]
    rows, features = acts.shape
    keys = scaled.shape[1]
    columns = blocks[0].shape[1]
    shards, _, unit = packed.shape
    rd = rows // shards
    b_copies = []
    for k in range(owners):
        for q in range(keys // columns):
            b_copies.append(
                pltpu.make_async_copy(
                    blocks[k].at[pl.ds(features + q * own_rows, own_rows)],
                    b_all.at[pl.ds(k * own_rows, own_rows), pl.ds(q * columns, columns)],
                    b_sems.at[k, q],
                )
            )
    for copy in b_copies:
        copy.start()
    copies = load_factors(blocks, a_all, sems)
    io.ready()
    me = lax.axis_index("dp")
    for j in range(shards):
        at = slice(j * rd, (j + 1) * rd)
        for q in range(features // unit):
            acts[at, q * unit : (q + 1) * unit] = packed[j, q * rd : (q + 1) * rd]
        first = features // unit * rd
        for q in range(keys // unit):
            part = packed[j, first + q * rd : first + (q + 1) * rd]
            scaled[at, q * unit : (q + 1) * unit] = part
        first += keys // unit * rd
        ids = packed[j, first:, :rd].astype(f32).astype(jnp.int32)
        tid = (ids[0:1] ^ me) * TEN_DEV + ids[1:2]
        label[:, at] = jnp.broadcast_to(tid, (8, rd))
    for n in range(3):
        io.store(n)
    step = min(ROW_STEP, rows)
    ids = second_ids(owners, own_rows, step)
    for copy in b_copies:
        copy.wait()
    for r in range(0, rows, step):
        at = slice(r, r + step)
        wide = dot(b_all[...], scaled[at], 1, 1)
        wide = jnp.where(ids == label[0:1, at], wide, 0.0)
        if own_rows >= ADAPTER_RANK:
            low = jnp.sum(wide.reshape(-1, ADAPTER_RANK, step), axis=0)
        else:
            low = jnp.sum(wide.reshape(-1, own_rows, step), axis=0)
            low = jnp.concatenate([low] * (ADAPTER_RANK // own_rows), axis=0)
            part = lax.div(iota(low.shape, 0), own_rows)
            place = lax.rem(lax.axis_index("fsdp"), ADAPTER_RANK // own_rows)
            low = jnp.where(part == place, low, 0.0)
        both[:ADAPTER_RANK, at] = low.astype(bf16)
    step = min(MID_STEP, rows)
    for r in range(0, rows, step):
        at = slice(r, r + step)
        where = column_of(label[0:1, at]).astype(jnp.int32) - lax.div(
            iota((step, LANES), 1), ADAPTER_RANK
        )
        low = jnp.zeros((step, LANES), f32)
        for k in range(owners):
            if r == 0:
                copies[k].wait()
            wide = dot(acts[at], a_all[:, k * columns : (k + 1) * columns])
            for q in range(columns // LANES):
                hit = where == k * TEN_DEV + q * (LANES // ADAPTER_RANK)
                low = low + jnp.where(hit, wide[:, q * LANES : (q + 1) * LANES], 0.0)
        low = jnp.transpose(low).reshape(LANES // ADAPTER_RANK, ADAPTER_RANK, step)
        both[ADAPTER_RANK:, at] = jnp.sum(low, axis=0).astype(bf16)


def total(parts, lines, at):
    value = parts[0][lines, at].astype(f32)
    for part in parts[1:]:
        value = value + part[lines, at].astype(f32)
    return value


BACK = slice(0, ADAPTER_RANK)
MID = slice(ADAPTER_RANK, 2 * ADAPTER_RANK)


def spread(low, label, k, columns):
    rows = low.shape[1]
    ids = lax.div(iota((columns, rows), 0), ADAPTER_RANK) + k * TEN_DEV
    tall = jnp.concatenate([low] * (columns // ADAPTER_RANK), axis=0)
    return jnp.where(ids == label, tall, 0.0).astype(bf16)

def second_grads(owners, parity, own_rows, boths, label, scaled, held):
    rows = scaled.shape[0]
    count = owners // 2
    step = min(ROW_STEP, rows)
    second = None
    line = iota((count * own_rows, step), 0)
    ids = second_ids(count, own_rows, step)
    ids = ids + (lax.div(line, own_rows) + parity) * TEN_DEV
    for r in range(0, rows, step):
        at = slice(r, r + step)
        held[...] = total(boths, MID, at)
        if own_rows >= ADAPTER_RANK:
            low = jnp.concatenate([held[...]] * (count * own_rows // ADAPTER_RANK), axis=0)
        else:
            first = lax.rem(lax.axis_index("fsdp") * own_rows, ADAPTER_RANK)
            low = held[pl.ds(pl.multiple_of(first, own_rows), own_rows)]
            low = jnp.concatenate([low] * count, axis=0)
        low = jnp.where(ids == label[0:1, at], low, 0.0).astype(bf16)
        term = dot(low, scaled[at])
        second = term if second is None else second + term
    return adapter_scale * ADAPTER_RANK ** (-0.5) * second


def grads_step(owners, parity, own_rows, boths, label, acts, scaled, held, out, arrived, send):
    features = acts.shape[1]
    keys = scaled.shape[1]
    columns = out.shape[1]
    down = adapter_scale * MODEL_WIDTH ** (-0.5)
    second = second_grads(owners, parity, own_rows, boths, label, scaled, held)
    low = total(boths, BACK, slice(None))
    for n in range(owners // 2):
        grad = down * dot(spread(low, label[0:1], 2 * n + parity, columns), acts[...])
        if arrived is not None:
            grad = grad + arrived[n, :, :features].astype(f32)
        out[n, :, :features] = grad.astype(bf16)
        for q in range(keys // LANES):
            lines = slice(q * own_rows, (q + 1) * own_rows)
            part = second[n * own_rows : (n + 1) * own_rows, q * LANES : (q + 1) * LANES]
            if arrived is not None:
                part = part + arrived[n, lines, features:].astype(f32)
            out[n, lines, features:] = part.astype(bf16)
        used = keys // LANES * own_rows
        if used < columns:
            out[n, used:, features:] = jnp.zeros((columns - used, LANES), bf16)
        send[n].start()


def grads_kernel(shards, owners, own_rows, parity, io, *refs):
    boths, (label, acts, scaled) = refs[:shards], refs[shards : shards + 3]
    refs = refs[shards + 3 :]
    arrived = refs[0] if parity == 0 else None
    outs, (held, made, sems) = refs[parity == 0 : -3], refs[-3:]
    send = []
    for n in range(owners // 2):
        out = outs[0].at[n] if parity else outs[n]
        send.append(pltpu.make_async_copy(made.at[n], out, sems.at[n]))
    io.ready()
    grads_step(owners, parity, own_rows, boths, label, acts, scaled, held, made, arrived, send)
    for copy in send:
        copy.wait()


def side_kernel(shards, owners, io, *refs):
    boths, (label, scaled, weight) = refs[:shards], refs[shards : shards + 3]
    a_blocks = refs[shards + 3 : shards + 3 + owners]
    out, part, a_all, back_wide, sems, part_sems = refs[shards + 3 + owners :]
    copies = load_factors(a_blocks, a_all, sems)
    send = []
    io.ready()
    rows, features = part.shape
    step = min(ROW_STEP, rows)
    width = a_all.shape[1]
    chunk = min(256, features)
    for r in range(0, rows, step):
        at = slice(r, r + step)
        low = adapter_scale * jnp.transpose(total(boths, BACK, at))
        low = jnp.concatenate([low] * (LANES // ADAPTER_RANK), axis=1)
        where = column_of(label[0:1, at]).astype(jnp.int32) - lax.div(
            iota((step, LANES), 1), ADAPTER_RANK
        )
        for q in range(width // LANES):
            hit = where == q * (LANES // ADAPTER_RANK)
            back_wide[:, q * LANES : (q + 1) * LANES] = jnp.where(hit, low, 0.0).astype(bf16)
        if r == 0:
            for copy in copies:
                copy.wait()
        for c in range(0, features, chunk):
            base = dot(scaled[at], weight[c : c + chunk], 1, 1).astype(bf16)
            side = dot(back_wide[...], a_all[c : c + chunk], 1, 1).astype(bf16)
            part[at, c : c + chunk] = (base.astype(f32) + side.astype(f32)).astype(bf16)
            copy = pltpu.make_async_copy(
                part.at[pl.ds(r, step), pl.ds(c, chunk)],
                out.at[pl.ds(r, step), pl.ds(c, chunk)],
                part_sems.at[r // step, c // chunk],
            )
            copy.start()
            send.append(copy)
    for copy in send:
        copy.wait()


def adam_kernel(count, own_rows, io, *refs):
    grads, firsts = refs[:count], refs[count : count + 3]
    seconds, outs = refs[count + 3 : count + 6], refs[count + 6 : count + 12]
    made, sems = refs[count + 12 : count + 15], refs[count + 15]
    features, _ = firsts[0].shape
    keys = seconds[0].shape[1]
    io.ready()

    def summed(at):
        value = grads[0][:, at].astype(f32)
        for part in grads[1:]:
            value = value + part[:, at].astype(f32)
        return value

    copies = []
    block = min(256, features)
    for n, c in enumerate(range(0, features, block)):
        at = slice(c, c + block)
        grad = jnp.transpose(summed(at))
        for m, value in enumerate(adam_step(*[x[at] for x in firsts], grad)):
            made[m][at] = value
            rows = pl.ds(c, block)
            copies.append(
                pltpu.make_async_copy(made[m].at[rows], outs[m].at[rows], sems.at[m, n])
            )
            copies[-1].start()
    grad = summed(slice(features, features + LANES))
    for q in range(keys // LANES):
        at = slice(q * LANES, (q + 1) * LANES)
        part = grad[q * own_rows : (q + 1) * own_rows]
        for out, value in zip(outs[3:], adam_step(*[x[:, at] for x in seconds], part)):
            out[:, at] = value
    for copy in copies:
        copy.wait()


def lay_kernel(io, blocks, out):
    io.ready()
    shards, _, width = blocks.shape
    for j in range(shards):
        out[:, j * width : (j + 1) * width] = blocks[j]


def swap(block, axis, bits):
    size = lax.axis_size(axis)
    return lax.ppermute(block, axis, [(i, i ^ bits) for i in range(size)])


def exchange(blocks, axis, groups=None):
    return lax.all_to_all(
        blocks, axis, split_axis=0, concat_axis=0, tiled=True, axis_index_groups=groups
    )

def per_device(
    acts,
    cotangent,
    tenant,
    advantage,
    base_weight,
    a_param,
    a_moment,
    a_second,
    b_param,
    b_moment,
    b_second,
):
    owners = lax.axis_size("dp")
    shards = lax.axis_size("fsdp")
    row_count, keys = cotangent.shape
    features, columns = a_param.shape
    own_rows = b_param.shape[0]
    rows = row_count * shards

    unit = min(features, keys)
    b_lines = own_rows * keys // columns
    lines = (features + keys) // unit * row_count + LABEL_ROWS

    packed, low = call(
        prep_kernel,
        [shape((shards, lines, unit)), shape((features + b_lines, columns))],
        (acts, cotangent, tenant[None], advantage[None], a_param, b_param),
        "h" * 6,
        "hh",
    )
    packed = exchange(packed, "fsdp")
    chips = [low] + [swap(low, "dp", k) for k in range(2, owners, 2)]
    blocks = []
    for block in chips:
        blocks += [block, swap(block, "dp", 1)]

    step = min(ROW_STEP, rows)
    factors = pltpu.VMEM((features, owners * columns), bf16)
    acts_part, scaled, label, both = call(
        functools.partial(open_kernel, owners, own_rows),
        [
            shape((rows, features)),
            shape((rows, keys)),
            shape((8, rows), jnp.int32),
            shape((2 * ADAPTER_RANK, rows)),
        ],
        (packed, *blocks),
        "h" + "r" * owners,
        "hhhh",
        [
            pltpu.VMEM((owners * own_rows, keys), bf16),
            factors,
            DMA((owners, keys // columns)),
            DMA((owners,)),
        ],
    )
    boths = [both] + [swap(both, "fsdp", j) for j in range(1, shards)]

    grads = shape((owners // 2, columns, features + LANES))

    def gradients(parity, outs, *more):
        return call(
            functools.partial(grads_kernel, shards, owners, own_rows, parity),
            outs,
            (*boths, label, acts_part, scaled, *more),
            "h" * (shards + 3 + len(more)),
            "r" * (1 if parity else owners // 2),
            [
                pltpu.VMEM((ADAPTER_RANK, step), f32),
                pltpu.VMEM(grads.shape, bf16),
                DMA((owners // 2,)),
            ],
        )

    odd = gradients(1, grads)
    odd, *own = lax.optimization_barrier((odd, *boths))
    grad_part = call(
        functools.partial(side_kernel, shards, owners),
        shape((rows, features)),
        (*own, label, scaled, base_weight, *blocks),
        "h" * (shards + 3) + "r" * owners,
        "r",
        [
            pltpu.VMEM((rows, features), bf16),
            factors,
            pltpu.VMEM((step, owners * columns), bf16),
            DMA((owners,)),
            DMA((rows // step, features // min(256, features))),
        ],
    )
    even = gradients(0, [shape(grads.shape[1:])] * (owners // 2), swap(odd, "dp", 1))
    grad_part, *even = lax.optimization_barrier((grad_part, *even))
    sums = [even[0]] + [swap(even[n], "dp", 2 * n) for n in range(1, owners // 2)]
    returned = exchange(grad_part.reshape(shards, row_count, features), "fsdp")
    grad_input = call(
        lay_kernel, shape((row_count, shards * features)), (returned,), "h", "h"
    )

    new = call(
        functools.partial(adam_kernel, owners // 2, own_rows),
        [shape(a_param.shape, f32)] * 3 + [shape(b_param.shape, f32)] * 3,
        (*sums, a_param, a_moment, a_second, b_param, b_moment, b_second),
        "h" * (owners // 2 + 6),
        "rrrhhh",
        [pltpu.VMEM(a_param.shape, f32)] * 3 + [DMA((3, features // min(256, features)))],
    )
    return (grad_input, *new)


def solution(mesh):
    rows = P(("dp", "fsdp"), None)
    labels = P(("dp", "fsdp"))
    first = P("fsdp", "dp")
    return jax.shard_map(
        per_device,
        mesh=mesh,
        in_specs=(rows, rows, labels, labels, P("fsdp", None), first, first, first, rows, rows, rows),
        out_specs=(rows, first, first, first, rows, rows, rows),
        check_vma=False,
    )
```

```python
import functools

import jax
import jax.numpy as jnp
from jax import lax
from jax.experimental import pallas as pl
from jax.experimental.pallas import tpu as pltpu
from jax.sharding import PartitionSpec as P

MODEL_WIDTH = 4096
ADAPTER_RANK = 32
TEN_DEV = 8
LANES = 128
ROW_STEP = 512
MID_STEP = 256
LABEL_ROWS = 16
FULL = (64 << 20) - (64 << 10)

adapter_scale = 2.0
learn_rate = 0.02
beta_one = 0.9
beta_two = 0.999
adam_eps = 1e-08
bias_one = 1.0 - 0.9**10
bias_two = 1.0 - 0.999**10

f32 = jnp.float32
bf16 = jnp.bfloat16
HBM = pl.BlockSpec(memory_space=pltpu.HBM)
DMA = pltpu.SemaphoreType.DMA

def shape(dims, kind=bf16):
    return jax.ShapeDtypeStruct(tuple(dims), kind)

class Staging:
    def __init__(self, loads, stores):
        self.loads, self.stores, self.gone = loads, stores, set()

    def ready(self):
        for copy in self.loads:
            copy.wait()

    def store(self, n):
        self.stores[n].start()
        self.gone.add(n)

    def finish(self):
        for n in self.stores:
            if n not in self.gone:
                self.store(n)
        for copy in self.stores.values():
            copy.wait()


def call(body, outs, ins, kinds, out_kinds, scratch=()):
    single = not isinstance(outs, (list, tuple))
    outs = [outs] if single else list(outs)
    staged = [x for x, kind in zip(ins, kinds) if kind == "h"]
    staged_outs = [x for x, kind in zip(outs, out_kinds) if kind == "h"]
    count = len(staged) + len(staged_outs)
    buffers = [pltpu.VMEM(x.shape, x.dtype) for x in staged + staged_outs]

    def kernel(*refs):
        refs = list(refs)
        given, made = refs[: len(ins)], refs[len(ins) : len(ins) + len(outs)]
        rest = refs[len(ins) + len(outs) :]
        held, own, sems = rest[:count], rest[count:-1], rest[-1]
        loads, stores = [], {}
        for n, kind in enumerate(kinds):
            if kind == "h":
                at = len(loads)
                loads.append(pltpu.make_async_copy(given[n], held[at], sems.at[at]))
                given[n] = held[at]
        for n, kind in enumerate(out_kinds):
            if kind == "h":
                at = len(loads) + len(stores)
                stores[n] = pltpu.make_async_copy(held[at], made[n], sems.at[at])
                made[n] = held[at]
        for copy in loads:
            copy.start()
        io = Staging(loads, stores)
        body(io, *given, *made, *own)
        io.finish()

    result = pl.pallas_call(
        kernel,
        out_shape=outs,
        in_specs=[HBM] * len(ins),
        out_specs=[HBM] * len(outs),
        scratch_shapes=buffers + list(scratch) + [DMA((count,))],
        compiler_params=pltpu.CompilerParams(vmem_limit_bytes=FULL),
        cost_estimate=pl.CostEstimate(flops=0, bytes_accessed=0, transcendentals=0),
    )(*ins)
    return result[0] if single else result


def adam_step(param, moment, second, gradient):
    moment = beta_one * moment + (1.0 - beta_one) * gradient
    second = beta_two * second + (1.0 - beta_two) * gradient * gradient
    step = (learn_rate / bias_one) * moment
    param = param - step / (jnp.sqrt((1.0 / bias_two) * second) + adam_eps)
    return (param, moment, second)

def dot(left, right, left_dim=1, right_dim=0):
    return lax.dot_general(
        left, right, (((left_dim,), (right_dim,)), ((), ())), preferred_element_type=f32
    )

def halvings(n):
    return n.bit_length() - 1


def over(x, n):
    return lax.shift_right_logical(x, jnp.full(x.shape, halvings(n), jnp.int32))


def past(x, n):
    return x & (n - 1)


def iota(dims, axis):
    return lax.broadcasted_iota(jnp.int32, dims, axis)

def column_of(row, lanes=LANES):
    n = row.shape[1]
    wide = jnp.broadcast_to(row.astype(f32), (lanes, n))
    return jnp.transpose(wide)

def prep_kernel(io, acts, cot, tenant, advantage, a_param, b_param, packed, low):
    io.ready()
    rows, keys = cot.shape
    shards, _, unit = packed.shape
    features, columns = a_param.shape
    factor = column_of(advantage[...]) * 0.25
    factor = jnp.concatenate([factor] * (keys // LANES), axis=1)
    scaled = (cot[...].astype(f32) * factor).astype(bf16)
    t = tenant[...]
    line = iota((LABEL_ROWS, rows), 0)
    owner = jnp.broadcast_to(lax.div(t, TEN_DEV), (LABEL_ROWS, rows))
    local = jnp.broadcast_to(lax.rem(t, TEN_DEV), (LABEL_ROWS, rows))
    labels = jnp.where(line == 0, owner, jnp.where(line == 1, local, 0)).astype(f32)
    labels = labels.astype(bf16)
    for j in range(shards):
        for q in range(features // unit):
            at = j * features + q * unit
            packed[j, q * rows : (q + 1) * rows] = acts[:, at : at + unit]
        first = features // unit * rows
        for q in range(keys // unit):
            packed[j, first + q * rows : first + (q + 1) * rows] = scaled[:, q * unit : (q + 1) * unit]
        first += keys // unit * rows
        packed[j, first:, :rows] = labels
        packed[j, first:, rows:] = jnp.zeros((LABEL_ROWS, unit - rows), bf16)
    io.store(0)
    low[:features] = (a_param[...] * MODEL_WIDTH ** (-0.5)).astype(bf16)
    own_rows = b_param.shape[0]
    for q in range(keys // columns):
        part = b_param[:, q * columns : (q + 1) * columns] * ADAPTER_RANK ** (-0.5)
        low[features + q * own_rows : features + (q + 1) * own_rows] = part.astype(bf16)


def second_ids(count, own_rows, rows):
    line = iota((count * own_rows, rows), 0)
    inner = past(line, own_rows) + lax.axis_index("fsdp") * own_rows
    return over(line, own_rows) * TEN_DEV + over(inner, ADAPTER_RANK)


def load_factors(a_blocks, a_all, sems):
    columns = a_blocks[0].shape[1]
    copies = [
        pltpu.make_async_copy(
            block.at[pl.ds(0, a_all.shape[0])],
            a_all.at[:, pl.ds(k * columns, columns)],
            sems.at[k],
        )
        for k, block in enumerate(a_blocks)
    ]
    for copy in copies:
        copy.start()
    return copies


def open_kernel(owners, own_rows, io, packed, *refs):
    blocks = refs[:owners]
    acts, scaled, label, both, marks, b_all, a_all, in_sems, b_sems, sems = refs[owners:]
    rows, features = acts.shape
    keys = scaled.shape[1]
    columns = blocks[0].shape[1]
    shards, _, unit = packed.shape
    rd = rows // shards
    first = (features + keys) // unit * rd
    act_copies, row_copies, b_copies = [], [], []
    for j in range(shards):
        at = pl.ds(j * rd, rd)
        for q in range((features + keys) // unit):
            piece = packed.at[j, pl.ds(q * rd, rd)]
            c = q * unit
            if c < features:
                copy = pltpu.make_async_copy(piece, acts.at[at, pl.ds(c, unit)], in_sems.at[j, q])
                act_copies.append(copy)
            else:
                to = scaled.at[at, pl.ds(c - features, unit)]
                row_copies.append(pltpu.make_async_copy(piece, to, in_sems.at[j, q]))
        row_copies.append(
            pltpu.make_async_copy(
                packed.at[j, pl.ds(first, LABEL_ROWS)], marks.at[j], in_sems.at[j, first // rd]
            )
        )
    for k in range(owners):
        for q in range(keys // columns):
            b_copies.append(
                pltpu.make_async_copy(
                    blocks[k].at[pl.ds(features + q * own_rows, own_rows)],
                    b_all.at[pl.ds(k * own_rows, own_rows), pl.ds(q * columns, columns)],
                    b_sems.at[k, q],
                )
            )
    for copy in row_copies + b_copies + act_copies:
        copy.start()
    copies = load_factors(blocks, a_all, sems)
    me = lax.axis_index("dp")
    for copy in row_copies:
        copy.wait()
    for j in range(shards):
        ids = marks[j, :, :rd].astype(f32).astype(jnp.int32)
        tid = (ids[0:1] ^ me) * TEN_DEV + ids[1:2]
        label[:, j * rd : (j + 1) * rd] = jnp.broadcast_to(tid, (8, rd))
    io.store(1)
    io.store(2)
    step = min(ROW_STEP, rows)
    ids = second_ids(owners, own_rows, step)
    for copy in b_copies:
        copy.wait()
    for r in range(0, rows, step):
        at = slice(r, r + step)
        wide = dot(b_all[...], scaled[at], 1, 1)
        wide = jnp.where(ids == label[0:1, at], wide, 0.0)
        if own_rows >= ADAPTER_RANK:
            low = jnp.sum(wide.reshape(-1, ADAPTER_RANK, step), axis=0)
        else:
            low = jnp.sum(wide.reshape(-1, own_rows, step), axis=0)
            low = jnp.concatenate([low] * (ADAPTER_RANK // own_rows), axis=0)
            part = over(iota(low.shape, 0), own_rows)
            place = lax.rem(lax.axis_index("fsdp"), ADAPTER_RANK // own_rows)
            low = jnp.where(part == place, low, 0.0)
        both[:ADAPTER_RANK, at] = low.astype(bf16)
    for copy in act_copies:
        copy.wait()
    io.store(0)
    step = min(MID_STEP, rows)
    for r in range(0, rows, step):
        at = slice(r, r + step)
        where = column_of(label[0:1, at]).astype(jnp.int32) - over(
            iota((step, LANES), 1), ADAPTER_RANK
        )
        low = jnp.zeros((step, LANES), f32)
        for k in range(owners):
            if r == 0:
                copies[k].wait()
            wide = dot(acts[at], a_all[:, k * columns : (k + 1) * columns])
            for q in range(columns // LANES):
                hit = where == k * TEN_DEV + q * (LANES // ADAPTER_RANK)
                low = low + jnp.where(hit, wide[:, q * LANES : (q + 1) * LANES], 0.0)
        low = jnp.transpose(low).reshape(LANES // ADAPTER_RANK, ADAPTER_RANK, step)
        both[ADAPTER_RANK:, at] = jnp.sum(low, axis=0).astype(bf16)


def total(parts, lines, at):
    value = parts[0][lines, at].astype(f32)
    for part in parts[1:]:
        value = value + part[lines, at].astype(f32)
    return value


BACK = slice(0, ADAPTER_RANK)
MID = slice(ADAPTER_RANK, 2 * ADAPTER_RANK)


def spread(tall, ids, label, k):
    return jnp.where(ids == label - k * TEN_DEV, tall, 0.0).astype(bf16)


def second_grads(owners, parity, own_rows, boths, label, scaled, held):
    rows = scaled.shape[0]
    count = owners // 2
    step = min(ROW_STEP, rows)
    second = None
    line = iota((count * own_rows, step), 0)
    ids = second_ids(count, own_rows, step)
    ids = ids + (over(line, own_rows) + parity) * TEN_DEV
    for r in range(0, rows, step):
        at = slice(r, r + step)
        held[...] = total(boths, MID, at)
        if own_rows >= ADAPTER_RANK:
            low = jnp.concatenate([held[...]] * (count * own_rows // ADAPTER_RANK), axis=0)
        else:
            first = lax.rem(lax.axis_index("fsdp") * own_rows, ADAPTER_RANK)
            low = held[pl.ds(pl.multiple_of(first, own_rows), own_rows)]
            low = jnp.concatenate([low] * count, axis=0)
        low = jnp.where(ids == label[0:1, at], low, 0.0).astype(bf16)
        term = dot(low, scaled[at])
        second = term if second is None else second + term
    return adapter_scale * ADAPTER_RANK ** (-0.5) * second


def grads_step(owners, parity, own_rows, boths, label, acts, scaled, held, out, arrived, send, wait=None):
    features = acts.shape[1]
    keys = scaled.shape[1]
    columns = out.shape[1]
    down = adapter_scale * MODEL_WIDTH ** (-0.5)
    second = second_grads(owners, parity, own_rows, boths, label, scaled, held)
    tall = down * total(boths, BACK, slice(None))
    ids = over(iota((columns, tall.shape[1]), 0), ADAPTER_RANK)
    tall = jnp.concatenate([tall] * (columns // ADAPTER_RANK), axis=0)
    for n in range(owners // 2):
        grad = dot(spread(tall, ids, label[0:1], 2 * n + parity), acts[...])
        if n == 0 and wait is not None:
            wait()
        if arrived is not None:
            grad = grad + arrived[n, :, :features].astype(f32)
        out[n, :, :features] = grad.astype(bf16)
        for q in range(keys // LANES):
            lines = slice(q * own_rows, (q + 1) * own_rows)
            part = second[n * own_rows : (n + 1) * own_rows, q * LANES : (q + 1) * LANES]
            if arrived is not None:
                part = part + arrived[n, lines, features:].astype(f32)
            out[n, lines, features:] = part.astype(bf16)
        used = keys // LANES * own_rows
        if used < columns:
            out[n, used:, features:] = jnp.zeros((columns - used, LANES), bf16)
        send[n].start()


def even_kernel(shards, owners, own_rows, io, *refs):
    boths, (label, acts, scaled, arrived) = refs[:shards], refs[shards : shards + 4]
    outs = refs[shards + 4 : shards + 4 + owners // 2]
    held, made, got, sems, got_sem = refs[shards + 4 + owners // 2 :]
    late = pltpu.make_async_copy(arrived, got, got_sem)
    late.start()
    send = [pltpu.make_async_copy(made.at[n], outs[n], sems.at[n]) for n in range(owners // 2)]
    io.ready()
    grads_step(
        owners, 0, own_rows, boths, label, acts, scaled, held, made, got, send, late.wait
    )
    for copy in send:
        copy.wait()


def main_kernel(shards, owners, own_rows, io, *refs):
    boths, (label, acts, scaled, weight) = refs[:shards], refs[shards : shards + 4]
    a_blocks = refs[shards + 4 : shards + 4 + owners]
    odd, out, held, made, part, a_all, back_wide, sems, odd_sems, part_sems = refs[
        shards + 4 + owners :
    ]
    copies = load_factors(a_blocks, a_all, sems)
    send = [pltpu.make_async_copy(made.at[n], odd.at[n], odd_sems.at[n]) for n in range(owners // 2)]
    io.ready()
    grads_step(owners, 1, own_rows, boths, label, acts, scaled, held, made, None, send)
    rows, features = part.shape
    step = min(ROW_STEP, rows)
    width = a_all.shape[1]
    chunk = min(256, features)
    for r in range(0, rows, step):
        at = slice(r, r + step)
        low = adapter_scale * jnp.transpose(total(boths, BACK, at))
        low = jnp.concatenate([low] * (LANES // ADAPTER_RANK), axis=1)
        where = column_of(label[0:1, at]).astype(jnp.int32) - over(
            iota((step, LANES), 1), ADAPTER_RANK
        )
        for q in range(width // LANES):
            hit = where == q * (LANES // ADAPTER_RANK)
            back_wide[:, q * LANES : (q + 1) * LANES] = jnp.where(hit, low, 0.0).astype(bf16)
        if r == 0:
            for copy in copies:
                copy.wait()
        for c in range(0, features, chunk):
            base = dot(scaled[at], weight[c : c + chunk], 1, 1).astype(bf16)
            side = dot(back_wide[...], a_all[c : c + chunk], 1, 1).astype(bf16)
            part[at, c : c + chunk] = (base.astype(f32) + side.astype(f32)).astype(bf16)
            copy = pltpu.make_async_copy(
                part.at[pl.ds(r, step), pl.ds(c, chunk)],
                out.at[pl.ds(r, step), pl.ds(c, chunk)],
                part_sems.at[r // step, c // chunk],
            )
            copy.start()
            send.append(copy)
    for copy in send:
        copy.wait()


def adam_kernel(count, own_rows, io, *refs):
    grads, firsts = refs[:count], refs[count : count + 3]
    seconds, outs = refs[count + 3 : count + 6], refs[count + 6 : count + 12]
    made, sems = refs[count + 12 : count + 15], refs[count + 15]
    features, _ = firsts[0].shape
    keys = seconds[0].shape[1]
    io.ready()

    def summed(at):
        value = grads[0][:, at].astype(f32)
        for part in grads[1:]:
            value = value + part[:, at].astype(f32)
        return value

    copies = []
    block = min(256, features)
    for n, c in enumerate(range(0, features, block)):
        at = slice(c, c + block)
        grad = jnp.transpose(summed(at))
        for m, value in enumerate(adam_step(*[x[at] for x in firsts], grad)):
            made[m][at] = value
            rows = pl.ds(c, block)
            copies.append(
                pltpu.make_async_copy(made[m].at[rows], outs[m].at[rows], sems.at[m, n])
            )
            copies[-1].start()
    grad = summed(slice(features, features + LANES))
    for q in range(keys // LANES):
        at = slice(q * LANES, (q + 1) * LANES)
        part = grad[q * own_rows : (q + 1) * own_rows]
        for out, value in zip(outs[3:], adam_step(*[x[:, at] for x in seconds], part)):
            out[:, at] = value
    for copy in copies:
        copy.wait()


def lay_kernel(io, blocks, out):
    io.ready()
    shards, _, width = blocks.shape
    for j in range(shards):
        out[:, j * width : (j + 1) * width] = blocks[j]


def swap(block, axis, bits):
    size = lax.axis_size(axis)
    return lax.ppermute(block, axis, [(i, i ^ bits) for i in range(size)])


def exchange(blocks, axis, groups=None):
    return lax.all_to_all(
        blocks, axis, split_axis=0, concat_axis=0, tiled=True, axis_index_groups=groups
    )

def per_device(
    acts,
    cotangent,
    tenant,
    advantage,
    base_weight,
    a_param,
    a_moment,
    a_second,
    b_param,
    b_moment,
    b_second,
):
    owners = lax.axis_size("dp")
    shards = lax.axis_size("fsdp")
    row_count, keys = cotangent.shape
    features, columns = a_param.shape
    own_rows = b_param.shape[0]
    rows = row_count * shards

    unit = min(features, keys)
    b_lines = own_rows * keys // columns
    lines = (features + keys) // unit * row_count + LABEL_ROWS

    packed, low = call(
        prep_kernel,
        [shape((shards, lines, unit)), shape((features + b_lines, columns))],
        (acts, cotangent, tenant[None], advantage[None], a_param, b_param),
        "h" * 6,
        "hh",
    )
    packed = exchange(packed, "fsdp")
    chips = [low] + [swap(low, "dp", k) for k in range(2, owners, 2)]
    blocks = []
    for block in chips:
        blocks += [block, swap(block, "dp", 1)]

    step = min(ROW_STEP, rows)
    factors = pltpu.VMEM((features, owners * columns), bf16)
    acts_part, scaled, label, both = call(
        functools.partial(open_kernel, owners, own_rows),
        [
            shape((rows, features)),
            shape((rows, keys)),
            shape((8, rows), jnp.int32),
            shape((2 * ADAPTER_RANK, rows)),
        ],
        (packed, *blocks),
        "r" + "r" * owners,
        "hhhh",
        [
            pltpu.VMEM((shards, LABEL_ROWS, unit), bf16),
            pltpu.VMEM((owners * own_rows, keys), bf16),
            factors,
            DMA((shards, (features + keys) // unit + 1)),
            DMA((owners, keys // columns)),
            DMA((owners,)),
        ],
    )
    boths = [both] + [swap(both, "fsdp", j) for j in range(1, shards)]

    grads = shape((owners // 2, columns, features + LANES))
    held = [pltpu.VMEM((ADAPTER_RANK, step), f32), pltpu.VMEM(grads.shape, bf16)]
    odd, grad_part = call(
        functools.partial(main_kernel, shards, owners, own_rows),
        [grads, shape((rows, features))],
        (*boths, label, acts_part, scaled, base_weight, *blocks),
        "h" * (shards + 4) + "r" * owners,
        "rr",
        held
        + [
            pltpu.VMEM((rows, features), bf16),
            factors,
            pltpu.VMEM((step, owners * columns), bf16),
            DMA((owners,)),
            DMA((owners // 2,)),
            DMA((rows // step, features // min(256, features))),
        ],
    )
    returned = exchange(grad_part.reshape(shards, row_count, features), "fsdp")
    grad_input = call(
        lay_kernel, shape((row_count, shards * features)), (returned,), "h", "h"
    )
    even = call(
        functools.partial(even_kernel, shards, owners, own_rows),
        [shape((columns, features + LANES))] * (owners // 2),
        (*boths, label, acts_part, scaled, swap(odd, "dp", 1)),
        "h" * (shards + 3) + "r",
        "r" * (owners // 2),
        held + [pltpu.VMEM(grads.shape, bf16), DMA((owners // 2,)), DMA],
    )
    sums = [even[0]] + [swap(even[n], "dp", 2 * n) for n in range(1, owners // 2)]

    new = call(
        functools.partial(adam_kernel, owners // 2, own_rows),
        [shape(a_param.shape, f32)] * 3 + [shape(b_param.shape, f32)] * 3,
        (*sums, a_param, a_moment, a_second, b_param, b_moment, b_second),
        "h" * (owners // 2 + 6),
        "rrrhhh",
        [pltpu.VMEM(a_param.shape, f32)] * 3 + [DMA((3, features // min(256, features)))],
    )
    return (grad_input, *new)


def solution(mesh):
    rows = P(("dp", "fsdp"), None)
    labels = P(("dp", "fsdp"))
    first = P("fsdp", "dp")
    return jax.shard_map(
        per_device,
        mesh=mesh,
        in_specs=(rows, rows, labels, labels, P("fsdp", None), first, first, first, rows, rows, rows),
        out_specs=(rows, first, first, first, rows, rows, rows),
        check_vma=False,
    )
```

```python
import functools

import jax
import jax.numpy as jnp
from jax import lax
from jax.experimental import pallas as pl
from jax.experimental.pallas import tpu as pltpu
from jax.sharding import PartitionSpec as P

MODEL_WIDTH = 4096
ADAPTER_RANK = 32
TEN_DEV = 8
LANES = 128
ROW_STEP = 512
MID_STEP = 256
LABEL_ROWS = 16
FULL = (64 << 20) - (64 << 10)

adapter_scale = 2.0
learn_rate = 0.02
beta_one = 0.9
beta_two = 0.999
adam_eps = 1e-08
bias_one = 1.0 - 0.9**10
bias_two = 1.0 - 0.999**10

f32 = jnp.float32
bf16 = jnp.bfloat16
HBM = pl.BlockSpec(memory_space=pltpu.HBM)
DMA = pltpu.SemaphoreType.DMA

def shape(dims, kind=bf16):
    return jax.ShapeDtypeStruct(tuple(dims), kind)

class Staging:
    def __init__(self, loads, stores):
        self.loads, self.stores, self.gone = loads, stores, set()

    def ready(self):
        for copy in self.loads:
            copy.wait()

    def store(self, n):
        self.stores[n].start()
        self.gone.add(n)

    def finish(self):
        for n in self.stores:
            if n not in self.gone:
                self.store(n)
        for copy in self.stores.values():
            copy.wait()


def call(body, outs, ins, kinds, out_kinds, scratch=()):
    single = not isinstance(outs, (list, tuple))
    outs = [outs] if single else list(outs)
    staged = [x for x, kind in zip(ins, kinds) if kind == "h"]
    staged_outs = [x for x, kind in zip(outs, out_kinds) if kind == "h"]
    count = len(staged) + len(staged_outs)
    buffers = [pltpu.VMEM(x.shape, x.dtype) for x in staged + staged_outs]

    def kernel(*refs):
        refs = list(refs)
        given, made = refs[: len(ins)], refs[len(ins) : len(ins) + len(outs)]
        rest = refs[len(ins) + len(outs) :]
        held, own, sems = rest[:count], rest[count:-1], rest[-1]
        loads, stores = [], {}
        for n, kind in enumerate(kinds):
            if kind == "h":
                at = len(loads)
                loads.append(pltpu.make_async_copy(given[n], held[at], sems.at[at]))
                given[n] = held[at]
        for n, kind in enumerate(out_kinds):
            if kind == "h":
                at = len(loads) + len(stores)
                stores[n] = pltpu.make_async_copy(held[at], made[n], sems.at[at])
                made[n] = held[at]
        for copy in loads:
            copy.start()
        io = Staging(loads, stores)
        body(io, *given, *made, *own)
        io.finish()

    result = pl.pallas_call(
        kernel,
        out_shape=outs,
        in_specs=[HBM] * len(ins),
        out_specs=[HBM] * len(outs),
        scratch_shapes=buffers + list(scratch) + [DMA((count,))],
        compiler_params=pltpu.CompilerParams(vmem_limit_bytes=FULL),
        cost_estimate=pl.CostEstimate(flops=0, bytes_accessed=0, transcendentals=0),
    )(*ins)
    return result[0] if single else result


def adam_step(param, moment, second, gradient):
    moment = beta_one * moment + (1.0 - beta_one) * gradient
    second = beta_two * second + (1.0 - beta_two) * gradient * gradient
    step = (learn_rate / bias_one) * moment
    param = param - step / (jnp.sqrt((1.0 / bias_two) * second) + adam_eps)
    return (param, moment, second)

def dot(left, right, left_dim=1, right_dim=0):
    return lax.dot_general(
        left, right, (((left_dim,), (right_dim,)), ((), ())), preferred_element_type=f32
    )

def halvings(n):
    return n.bit_length() - 1


def over(x, n):
    return lax.shift_right_logical(x, jnp.full(x.shape, halvings(n), jnp.int32))


def past(x, n):
    return x & (n - 1)


def iota(dims, axis):
    return lax.broadcasted_iota(jnp.int32, dims, axis)

def column_of(row, lanes=LANES):
    n = row.shape[1]
    wide = jnp.broadcast_to(row.astype(f32), (lanes, n))
    return jnp.transpose(wide)

def prep_kernel(io, acts, cot, tenant, advantage, a_param, b_param, packed, low):
    io.ready()
    rows, keys = cot.shape
    shards, _, unit = packed.shape
    features, columns = a_param.shape
    factor = column_of(advantage[...]) * 0.25
    factor = jnp.concatenate([factor] * (keys // LANES), axis=1)
    scaled = (cot[...].astype(f32) * factor).astype(bf16)
    t = tenant[...]
    line = iota((LABEL_ROWS, rows), 0)
    owner = jnp.broadcast_to(lax.div(t, TEN_DEV), (LABEL_ROWS, rows))
    local = jnp.broadcast_to(lax.rem(t, TEN_DEV), (LABEL_ROWS, rows))
    labels = jnp.where(line == 0, owner, jnp.where(line == 1, local, 0)).astype(f32)
    labels = labels.astype(bf16)
    for j in range(shards):
        for q in range(features // unit):
            at = j * features + q * unit
            packed[j, q * rows : (q + 1) * rows] = acts[:, at : at + unit]
        first = features // unit * rows
        for q in range(keys // unit):
            packed[j, first + q * rows : first + (q + 1) * rows] = scaled[:, q * unit : (q + 1) * unit]
        first += keys // unit * rows
        packed[j, first:, :rows] = labels
        packed[j, first:, rows:] = jnp.zeros((LABEL_ROWS, unit - rows), bf16)
    io.store(0)
    low[:features] = (a_param[...] * MODEL_WIDTH ** (-0.5)).astype(bf16)
    own_rows = b_param.shape[0]
    for q in range(keys // columns):
        part = b_param[:, q * columns : (q + 1) * columns] * ADAPTER_RANK ** (-0.5)
        low[features + q * own_rows : features + (q + 1) * own_rows] = part.astype(bf16)


def second_ids(count, own_rows, rows):
    line = iota((count * own_rows, rows), 0)
    inner = past(line, own_rows) + lax.axis_index("fsdp") * own_rows
    return over(line, own_rows) * TEN_DEV + over(inner, ADAPTER_RANK)


def load_factors(a_blocks, a_all, sems):
    copies = [
        pltpu.make_async_copy(block.at[pl.ds(0, a_all.shape[1])], a_all.at[k], sems.at[k])
        for k, block in enumerate(a_blocks)
    ]
    for copy in copies:
        copy.start()
    return copies


def open_kernel(owners, own_rows, io, packed, *refs):
    blocks = refs[:owners]
    acts, scaled, label, both, marks, b_all, a_all, in_sems, b_sems, sems = refs[owners:]
    rows, features = acts.shape
    keys = scaled.shape[1]
    columns = blocks[0].shape[1]
    shards, _, unit = packed.shape
    rd = rows // shards
    first = (features + keys) // unit * rd
    act_copies, row_copies, b_copies = [], [], []
    for j in range(shards):
        at = pl.ds(j * rd, rd)
        for q in range((features + keys) // unit):
            piece = packed.at[j, pl.ds(q * rd, rd)]
            c = q * unit
            if c < features:
                copy = pltpu.make_async_copy(piece, acts.at[at, pl.ds(c, unit)], in_sems.at[j, q])
                act_copies.append(copy)
            else:
                to = scaled.at[at, pl.ds(c - features, unit)]
                row_copies.append(pltpu.make_async_copy(piece, to, in_sems.at[j, q]))
        row_copies.append(
            pltpu.make_async_copy(
                packed.at[j, pl.ds(first, LABEL_ROWS)], marks.at[j], in_sems.at[j, first // rd]
            )
        )
    for k in range(owners):
        for q in range(keys // columns):
            b_copies.append(
                pltpu.make_async_copy(
                    blocks[k].at[pl.ds(features + q * own_rows, own_rows)],
                    b_all.at[pl.ds(k * own_rows, own_rows), pl.ds(q * columns, columns)],
                    b_sems.at[k, q],
                )
            )
    for copy in row_copies + b_copies + act_copies:
        copy.start()
    copies = load_factors(blocks, a_all, sems)
    me = lax.axis_index("dp")
    for copy in row_copies:
        copy.wait()
    for j in range(shards):
        ids = marks[j, :, :rd].astype(f32).astype(jnp.int32)
        tid = (ids[0:1] ^ me) * TEN_DEV + ids[1:2]
        label[:, j * rd : (j + 1) * rd] = jnp.broadcast_to(tid, (8, rd))
    io.store(1)
    io.store(2)
    step = min(ROW_STEP, rows)
    ids = second_ids(owners, own_rows, step)
    for copy in b_copies:
        copy.wait()
    for r in range(0, rows, step):
        at = slice(r, r + step)
        wide = dot(b_all[...], scaled[at], 1, 1)
        wide = jnp.where(ids == label[0:1, at], wide, 0.0)
        if own_rows >= ADAPTER_RANK:
            low = jnp.sum(wide.reshape(-1, ADAPTER_RANK, step), axis=0)
        else:
            low = jnp.sum(wide.reshape(-1, own_rows, step), axis=0)
            low = jnp.concatenate([low] * (ADAPTER_RANK // own_rows), axis=0)
            part = over(iota(low.shape, 0), own_rows)
            place = lax.rem(lax.axis_index("fsdp"), ADAPTER_RANK // own_rows)
            low = jnp.where(part == place, low, 0.0)
        both[:ADAPTER_RANK, at] = low.astype(bf16)
    for copy in act_copies:
        copy.wait()
    io.store(0)
    step = min(MID_STEP, rows)
    for r in range(0, rows, step):
        at = slice(r, r + step)
        where = column_of(label[0:1, at]).astype(jnp.int32) - over(
            iota((step, LANES), 1), ADAPTER_RANK
        )
        low = jnp.zeros((step, LANES), f32)
        for k in range(owners):
            if r == 0:
                copies[k].wait()
            wide = dot(acts[at], a_all[k])
            for q in range(columns // LANES):
                hit = where == k * TEN_DEV + q * (LANES // ADAPTER_RANK)
                low = low + jnp.where(hit, wide[:, q * LANES : (q + 1) * LANES], 0.0)
        low = jnp.transpose(low).reshape(LANES // ADAPTER_RANK, ADAPTER_RANK, step)
        both[ADAPTER_RANK:, at] = jnp.sum(low, axis=0).astype(bf16)


def total(parts, lines, at):
    value = parts[0][lines, at].astype(f32)
    for part in parts[1:]:
        value = value + part[lines, at].astype(f32)
    return value


BACK = slice(0, ADAPTER_RANK)
MID = slice(ADAPTER_RANK, 2 * ADAPTER_RANK)


def spread(tall, ids, label, k):
    return jnp.where(ids == label - k * TEN_DEV, tall, 0.0).astype(bf16)


def second_grads(owners, parity, own_rows, boths, label, scaled, held):
    rows = scaled.shape[0]
    count = owners // 2
    step = min(ROW_STEP, rows)
    second = None
    line = iota((count * own_rows, step), 0)
    ids = second_ids(count, own_rows, step)
    ids = ids + (over(line, own_rows) + parity) * TEN_DEV
    for r in range(0, rows, step):
        at = slice(r, r + step)
        held[...] = total(boths, MID, at)
        if own_rows >= ADAPTER_RANK:
            low = jnp.concatenate([held[...]] * (count * own_rows // ADAPTER_RANK), axis=0)
        else:
            first = lax.rem(lax.axis_index("fsdp") * own_rows, ADAPTER_RANK)
            low = held[pl.ds(pl.multiple_of(first, own_rows), own_rows)]
            low = jnp.concatenate([low] * count, axis=0)
        low = jnp.where(ids == label[0:1, at], low, 0.0).astype(bf16)
        term = dot(low, scaled[at])
        second = term if second is None else second + term
    return adapter_scale * ADAPTER_RANK ** (-0.5) * second


def grads_step(owners, parity, own_rows, boths, label, acts, scaled, held, out, arrived, send, wait=None):
    features = acts.shape[1]
    keys = scaled.shape[1]
    columns = out.shape[1]
    down = adapter_scale * MODEL_WIDTH ** (-0.5)
    second = second_grads(owners, parity, own_rows, boths, label, scaled, held)
    tall = down * total(boths, BACK, slice(None))
    ids = over(iota((columns, tall.shape[1]), 0), ADAPTER_RANK)
    tall = jnp.concatenate([tall] * (columns // ADAPTER_RANK), axis=0)
    for n in range(owners // 2):
        grad = dot(spread(tall, ids, label[0:1], 2 * n + parity), acts[...])
        if n == 0 and wait is not None:
            wait()
        if arrived is not None:
            grad = grad + arrived[n, :, :features].astype(f32)
        out[n, :, :features] = grad.astype(bf16)
        for q in range(keys // LANES):
            lines = slice(q * own_rows, (q + 1) * own_rows)
            part = second[n * own_rows : (n + 1) * own_rows, q * LANES : (q + 1) * LANES]
            if arrived is not None:
                part = part + arrived[n, lines, features:].astype(f32)
            out[n, lines, features:] = part.astype(bf16)
        used = keys // LANES * own_rows
        if used < columns:
            out[n, used:, features:] = jnp.zeros((columns - used, LANES), bf16)
        send[n].start()


def even_kernel(shards, owners, own_rows, io, *refs):
    boths, (label, acts, scaled, arrived) = refs[:shards], refs[shards : shards + 4]
    outs = refs[shards + 4 : shards + 4 + owners // 2]
    held, made, got, sems, got_sem = refs[shards + 4 + owners // 2 :]
    late = pltpu.make_async_copy(arrived, got, got_sem)
    late.start()
    send = [pltpu.make_async_copy(made.at[n], outs[n], sems.at[n]) for n in range(owners // 2)]
    io.ready()
    grads_step(
        owners, 0, own_rows, boths, label, acts, scaled, held, made, got, send, late.wait
    )
    for copy in send:
        copy.wait()


def main_kernel(shards, owners, own_rows, io, *refs):
    boths, (label, acts, scaled, weight) = refs[:shards], refs[shards : shards + 4]
    a_blocks = refs[shards + 4 : shards + 4 + owners]
    odd, out, held, made, part, a_all, back_wide, sems, odd_sems, part_sems = refs[
        shards + 4 + owners :
    ]
    copies = load_factors(a_blocks, a_all, sems)
    send = [pltpu.make_async_copy(made.at[n], odd.at[n], odd_sems.at[n]) for n in range(owners // 2)]
    io.ready()
    grads_step(owners, 1, own_rows, boths, label, acts, scaled, held, made, None, send)
    rows, features = part.shape
    step = min(ROW_STEP, rows)
    width = back_wide.shape[1]
    chunk = min(256, features)
    for r in range(0, rows, step):
        at = slice(r, r + step)
        low = adapter_scale * jnp.transpose(total(boths, BACK, at))
        low = jnp.concatenate([low] * (LANES // ADAPTER_RANK), axis=1)
        where = column_of(label[0:1, at]).astype(jnp.int32) - over(
            iota((step, LANES), 1), ADAPTER_RANK
        )
        for q in range(width // LANES):
            hit = where == q * (LANES // ADAPTER_RANK)
            back_wide[:, q * LANES : (q + 1) * LANES] = jnp.where(hit, low, 0.0).astype(bf16)
        if r == 0:
            for copy in copies:
                copy.wait()
        for c in range(0, features, chunk):
            base = dot(scaled[at], weight[c : c + chunk], 1, 1).astype(bf16)
            factor = [a_all[k, c : c + chunk] for k in range(owners)]
            side = dot(back_wide[...], jnp.concatenate(factor, axis=1), 1, 1).astype(bf16)
            part[at, c : c + chunk] = (base.astype(f32) + side.astype(f32)).astype(bf16)
            copy = pltpu.make_async_copy(
                part.at[pl.ds(r, step), pl.ds(c, chunk)],
                out.at[pl.ds(r, step), pl.ds(c, chunk)],
                part_sems.at[r // step, c // chunk],
            )
            copy.start()
            send.append(copy)
    for copy in send:
        copy.wait()


def adam_kernel(count, own_rows, io, *refs):
    given, firsts = refs[:count], refs[count : count + 3]
    seconds, outs = refs[count + 3 : count + 6], refs[count + 6 : count + 12]
    grads, (held, made, grad_sems, in_sems, sems) = refs[count + 12], refs[count + 13 :]
    features, _ = firsts[0].shape
    keys = seconds[0].shape[1]
    block = min(256, features)
    starts = list(range(0, features, block))
    grad_loads = [
        pltpu.make_async_copy(given[n], grads.at[n], grad_sems.at[n]) for n in range(count)
    ]
    loads = [
        pltpu.make_async_copy(
            firsts[m].at[pl.ds(c, block)], held.at[m, pl.ds(c, block)], in_sems.at[m, n]
        )
        for n, c in enumerate(starts)
        for m in range(3)
    ]
    for copy in grad_loads + loads:
        copy.start()

    def summed(at):
        value = grads[0, :, at].astype(f32)
        for n in range(1, count):
            value = value + grads[n, :, at].astype(f32)
        return value

    for copy in grad_loads:
        copy.wait()
    copies = []
    for n, c in enumerate(starts):
        at = slice(c, c + block)
        grad = jnp.transpose(summed(at))
        for m in range(3):
            loads[3 * n + m].wait()
        for m, value in enumerate(adam_step(*[held[m, at] for m in range(3)], grad)):
            made[m, at] = value
            rows = pl.ds(c, block)
            copies.append(
                pltpu.make_async_copy(made.at[m, rows], outs[m].at[rows], sems.at[m, n])
            )
            copies[-1].start()
    io.ready()
    grad = summed(slice(features, features + LANES))
    for q in range(keys // LANES):
        at = slice(q * LANES, (q + 1) * LANES)
        part = grad[q * own_rows : (q + 1) * own_rows]
        for out, value in zip(outs[3:], adam_step(*[x[:, at] for x in seconds], part)):
            out[:, at] = value
    for copy in copies:
        copy.wait()


def lay_kernel(io, blocks, out):
    io.ready()
    shards, _, width = blocks.shape
    for j in range(shards):
        out[:, j * width : (j + 1) * width] = blocks[j]


def swap(block, axis, bits):
    size = lax.axis_size(axis)
    return lax.ppermute(block, axis, [(i, i ^ bits) for i in range(size)])


def exchange(blocks, axis, groups=None):
    return lax.all_to_all(
        blocks, axis, split_axis=0, concat_axis=0, tiled=True, axis_index_groups=groups
    )

def per_device(
    acts,
    cotangent,
    tenant,
    advantage,
    base_weight,
    a_param,
    a_moment,
    a_second,
    b_param,
    b_moment,
    b_second,
):
    owners = lax.axis_size("dp")
    shards = lax.axis_size("fsdp")
    row_count, keys = cotangent.shape
    features, columns = a_param.shape
    own_rows = b_param.shape[0]
    rows = row_count * shards

    unit = min(features, keys)
    b_lines = own_rows * keys // columns
    lines = (features + keys) // unit * row_count + LABEL_ROWS

    packed, low = call(
        prep_kernel,
        [shape((shards, lines, unit)), shape((features + b_lines, columns))],
        (acts, cotangent, tenant[None], advantage[None], a_param, b_param),
        "h" * 6,
        "hh",
    )
    packed = exchange(packed, "fsdp")
    chips = [low] + [swap(low, "dp", k) for k in range(2, owners, 2)]
    blocks = []
    for block in chips:
        blocks += [block, swap(block, "dp", 1)]

    step = min(ROW_STEP, rows)
    factors = pltpu.VMEM((owners, features, columns), bf16)
    acts_part, scaled, label, both = call(
        functools.partial(open_kernel, owners, own_rows),
        [
            shape((rows, features)),
            shape((rows, keys)),
            shape((8, rows), jnp.int32),
            shape((2 * ADAPTER_RANK, rows)),
        ],
        (packed, *blocks),
        "r" + "r" * owners,
        "hhhh",
        [
            pltpu.VMEM((shards, LABEL_ROWS, unit), bf16),
            pltpu.VMEM((owners * own_rows, keys), bf16),
            factors,
            DMA((shards, (features + keys) // unit + 1)),
            DMA((owners, keys // columns)),
            DMA((owners,)),
        ],
    )
    boths = [both] + [swap(both, "fsdp", j) for j in range(1, shards)]

    grads = shape((owners // 2, columns, features + LANES))
    held = [pltpu.VMEM((ADAPTER_RANK, step), f32), pltpu.VMEM(grads.shape, bf16)]
    odd, grad_part = call(
        functools.partial(main_kernel, shards, owners, own_rows),
        [grads, shape((rows, features))],
        (*boths, label, acts_part, scaled, base_weight, *blocks),
        "h" * (shards + 4) + "r" * owners,
        "rr",
        held
        + [
            pltpu.VMEM((rows, features), bf16),
            factors,
            pltpu.VMEM((step, owners * columns), bf16),
            DMA((owners,)),
            DMA((owners // 2,)),
            DMA((rows // step, features // min(256, features))),
        ],
    )
    returned = exchange(grad_part.reshape(shards, row_count, features), "fsdp")
    grad_input = call(
        lay_kernel, shape((row_count, shards * features)), (returned,), "h", "h"
    )
    even = call(
        functools.partial(even_kernel, shards, owners, own_rows),
        [shape((columns, features + LANES))] * (owners // 2),
        (*boths, label, acts_part, scaled, swap(odd, "dp", 1)),
        "h" * (shards + 3) + "r",
        "r" * (owners // 2),
        held + [pltpu.VMEM(grads.shape, bf16), DMA((owners // 2,)), DMA],
    )
    sums = [even[0]] + [swap(even[n], "dp", 2 * n) for n in range(1, owners // 2)]

    pieces = features // min(256, features)
    new = call(
        functools.partial(adam_kernel, owners // 2, own_rows),
        [shape(a_param.shape, f32)] * 3 + [shape(b_param.shape, f32)] * 3,
        (*sums, a_param, a_moment, a_second, b_param, b_moment, b_second),
        "r" * (owners // 2 + 3) + "hhh",
        "rrrhhh",
        [
            pltpu.VMEM(grads.shape, bf16),
            pltpu.VMEM((3, features, columns), f32),
            pltpu.VMEM((3, features, columns), f32),
            DMA((owners // 2,)),
            DMA((3, pieces)),
            DMA((3, pieces)),
        ],
    )
    return (grad_input, *new)


def solution(mesh):
    rows = P(("dp", "fsdp"), None)
    labels = P(("dp", "fsdp"))
    first = P("fsdp", "dp")
    return jax.shard_map(
        per_device,
        mesh=mesh,
        in_specs=(rows, rows, labels, labels, P("fsdp", None), first, first, first, rows, rows, rows),
        out_specs=(rows, first, first, first, rows, rows, rows),
        check_vma=False,
    )
```

```python
import functools

import jax
import jax.numpy as jnp
from jax import lax
from jax.experimental import pallas as pl
from jax.experimental.pallas import tpu as pltpu
from jax.sharding import PartitionSpec as P

MODEL_WIDTH = 4096
ADAPTER_RANK = 32
TEN_DEV = 8
LANES = 128
ROW_STEP = 512
MID_STEP = 256
LABEL_ROWS = 16
FULL = (64 << 20) - (64 << 10)

adapter_scale = 2.0
learn_rate = 0.02
beta_one = 0.9
beta_two = 0.999
adam_eps = 1e-08
bias_one = 1.0 - 0.9**10
bias_two = 1.0 - 0.999**10

f32 = jnp.float32
bf16 = jnp.bfloat16
HBM = pl.BlockSpec(memory_space=pltpu.HBM)
DMA = pltpu.SemaphoreType.DMA

def shape(dims, kind=bf16):
    return jax.ShapeDtypeStruct(tuple(dims), kind)

class Staging:
    def __init__(self, loads, stores):
        self.loads, self.stores, self.gone = loads, stores, set()

    def ready(self):
        for copy in self.loads:
            copy.wait()

    def store(self, n):
        self.stores[n].start()
        self.gone.add(n)

    def finish(self):
        for n in self.stores:
            if n not in self.gone:
                self.store(n)
        for copy in self.stores.values():
            copy.wait()


def call(body, outs, ins, kinds, out_kinds, scratch=(), aliases={}):
    single = not isinstance(outs, (list, tuple))
    outs = [outs] if single else list(outs)
    staged = [x for x, kind in zip(ins, kinds) if kind == "h"]
    staged_outs = [x for x, kind in zip(outs, out_kinds) if kind == "h"]
    count = len(staged) + len(staged_outs)
    buffers = [pltpu.VMEM(x.shape, x.dtype) for x in staged + staged_outs]

    def kernel(*refs):
        refs = list(refs)
        given, made = refs[: len(ins)], refs[len(ins) : len(ins) + len(outs)]
        rest = refs[len(ins) + len(outs) :]
        held, own, sems = rest[:count], rest[count:-1], rest[-1]
        loads, stores = [], {}
        for n, kind in enumerate(kinds):
            if kind == "h":
                at = len(loads)
                loads.append(pltpu.make_async_copy(given[n], held[at], sems.at[at]))
                given[n] = held[at]
        for n, kind in enumerate(out_kinds):
            if kind == "h":
                at = len(loads) + len(stores)
                stores[n] = pltpu.make_async_copy(held[at], made[n], sems.at[at])
                made[n] = held[at]
        for copy in loads:
            copy.start()
        io = Staging(loads, stores)
        body(io, *given, *made, *own)
        io.finish()

    result = pl.pallas_call(
        kernel,
        out_shape=outs,
        in_specs=[HBM] * len(ins),
        out_specs=[HBM] * len(outs),
        scratch_shapes=buffers + list(scratch) + [DMA((count,))],
        input_output_aliases=aliases,
        compiler_params=pltpu.CompilerParams(vmem_limit_bytes=FULL),
        cost_estimate=pl.CostEstimate(flops=0, bytes_accessed=0, transcendentals=0),
    )(*ins)
    return result[0] if single else result


def adam_step(param, moment, second, gradient):
    moment = beta_one * moment + (1.0 - beta_one) * gradient
    second = beta_two * second + (1.0 - beta_two) * gradient * gradient
    step = (learn_rate / bias_one) * moment
    param = param - step / (jnp.sqrt((1.0 / bias_two) * second) + adam_eps)
    return (param, moment, second)

def dot(left, right, left_dim=1, right_dim=0):
    return lax.dot_general(
        left, right, (((left_dim,), (right_dim,)), ((), ())), preferred_element_type=f32
    )

def halvings(n):
    return n.bit_length() - 1


def over(x, n):
    return lax.shift_right_logical(x, jnp.full(x.shape, halvings(n), jnp.int32))


def past(x, n):
    return x & (n - 1)


def iota(dims, axis):
    return lax.broadcasted_iota(jnp.int32, dims, axis)

def column_of(row, lanes=LANES):
    n = row.shape[1]
    wide = jnp.broadcast_to(row.astype(f32), (lanes, n))
    return jnp.transpose(wide)

def prep_kernel(io, acts, cot, tenant, advantage, a_param, b_param, packed, low):
    io.ready()
    rows, keys = cot.shape
    shards, _, unit = packed.shape
    features, columns = a_param.shape
    factor = column_of(advantage[...]) * 0.25
    factor = jnp.concatenate([factor] * (keys // LANES), axis=1)
    scaled = (cot[...].astype(f32) * factor).astype(bf16)
    t = tenant[...]
    line = iota((LABEL_ROWS, rows), 0)
    owner = jnp.broadcast_to(lax.div(t, TEN_DEV), (LABEL_ROWS, rows))
    local = jnp.broadcast_to(lax.rem(t, TEN_DEV), (LABEL_ROWS, rows))
    labels = jnp.where(line == 0, owner, jnp.where(line == 1, local, 0)).astype(f32)
    labels = labels.astype(bf16)
    for j in range(shards):
        for q in range(features // unit):
            at = j * features + q * unit
            packed[j, q * rows : (q + 1) * rows] = acts[:, at : at + unit]
        first = features // unit * rows
        for q in range(keys // unit):
            packed[j, first + q * rows : first + (q + 1) * rows] = scaled[:, q * unit : (q + 1) * unit]
        first += keys // unit * rows
        packed[j, first:, :rows] = labels
        packed[j, first:, rows:] = jnp.zeros((LABEL_ROWS, unit - rows), bf16)
    io.store(0)
    low[:features] = (a_param[...] * MODEL_WIDTH ** (-0.5)).astype(bf16)
    own_rows = b_param.shape[0]
    for q in range(keys // columns):
        part = b_param[:, q * columns : (q + 1) * columns] * ADAPTER_RANK ** (-0.5)
        low[features + q * own_rows : features + (q + 1) * own_rows] = part.astype(bf16)


def second_ids(count, own_rows, rows):
    line = iota((count * own_rows, rows), 0)
    inner = past(line, own_rows) + lax.axis_index("fsdp") * own_rows
    return over(line, own_rows) * TEN_DEV + over(inner, ADAPTER_RANK)


def load_factors(a_blocks, a_all, sems):
    copies = [
        pltpu.make_async_copy(block.at[pl.ds(0, a_all.shape[1])], a_all.at[k], sems.at[k])
        for k, block in enumerate(a_blocks)
    ]
    for copy in copies:
        copy.start()
    return copies


def open_kernel(owners, own_rows, io, packed, *refs):
    blocks = refs[:owners]
    acts, scaled, label, both, marks, b_all, a_all, in_sems, b_sems, sems = refs[owners:]
    rows, features = acts.shape
    keys = scaled.shape[1]
    columns = blocks[0].shape[1]
    shards, _, unit = packed.shape
    rd = rows // shards
    first = (features + keys) // unit * rd
    act_copies, row_copies, b_copies = [], [], []
    for j in range(shards):
        at = pl.ds(j * rd, rd)
        for q in range((features + keys) // unit):
            piece = packed.at[j, pl.ds(q * rd, rd)]
            c = q * unit
            if c < features:
                copy = pltpu.make_async_copy(piece, acts.at[at, pl.ds(c, unit)], in_sems.at[j, q])
                act_copies.append(copy)
            else:
                to = scaled.at[at, pl.ds(c - features, unit)]
                row_copies.append(pltpu.make_async_copy(piece, to, in_sems.at[j, q]))
        row_copies.append(
            pltpu.make_async_copy(
                packed.at[j, pl.ds(first, LABEL_ROWS)], marks.at[j], in_sems.at[j, first // rd]
            )
        )
    for k in range(owners):
        for q in range(keys // columns):
            b_copies.append(
                pltpu.make_async_copy(
                    blocks[k].at[pl.ds(features + q * own_rows, own_rows)],
                    b_all.at[pl.ds(k * own_rows, own_rows), pl.ds(q * columns, columns)],
                    b_sems.at[k, q],
                )
            )
    for copy in row_copies + b_copies + act_copies:
        copy.start()
    copies = load_factors(blocks, a_all, sems)
    me = lax.axis_index("dp")
    for copy in row_copies:
        copy.wait()
    for j in range(shards):
        ids = marks[j, :, :rd].astype(f32).astype(jnp.int32)
        tid = (ids[0:1] ^ me) * TEN_DEV + ids[1:2]
        label[:, j * rd : (j + 1) * rd] = jnp.broadcast_to(tid, (8, rd))
    io.store(1)
    io.store(2)
    step = min(ROW_STEP, rows)
    ids = second_ids(owners, own_rows, step)
    for copy in b_copies:
        copy.wait()
    for r in range(0, rows, step):
        at = slice(r, r + step)
        wide = dot(b_all[...], scaled[at], 1, 1)
        wide = jnp.where(ids == label[0:1, at], wide, 0.0)
        if own_rows >= ADAPTER_RANK:
            low = jnp.sum(wide.reshape(-1, ADAPTER_RANK, step), axis=0)
        else:
            low = jnp.sum(wide.reshape(-1, own_rows, step), axis=0)
            low = jnp.concatenate([low] * (ADAPTER_RANK // own_rows), axis=0)
            part = over(iota(low.shape, 0), own_rows)
            place = lax.rem(lax.axis_index("fsdp"), ADAPTER_RANK // own_rows)
            low = jnp.where(part == place, low, 0.0)
        both[:ADAPTER_RANK, at] = low.astype(bf16)
    for copy in act_copies:
        copy.wait()
    io.store(0)
    step = min(MID_STEP, rows)
    for r in range(0, rows, step):
        at = slice(r, r + step)
        where = column_of(label[0:1, at]).astype(jnp.int32) - over(
            iota((step, LANES), 1), ADAPTER_RANK
        )
        low = jnp.zeros((step, LANES), f32)
        for k in range(owners):
            if r == 0:
                copies[k].wait()
            wide = dot(acts[at], a_all[k])
            for q in range(columns // LANES):
                hit = where == k * TEN_DEV + q * (LANES // ADAPTER_RANK)
                low = low + jnp.where(hit, wide[:, q * LANES : (q + 1) * LANES], 0.0)
        low = jnp.transpose(low).reshape(LANES // ADAPTER_RANK, ADAPTER_RANK, step)
        both[ADAPTER_RANK:, at] = jnp.sum(low, axis=0).astype(bf16)


def total(parts, lines, at):
    value = parts[0][lines, at].astype(f32)
    for part in parts[1:]:
        value = value + part[lines, at].astype(f32)
    return value


BACK = slice(0, ADAPTER_RANK)
MID = slice(ADAPTER_RANK, 2 * ADAPTER_RANK)


def spread(tall, ids, label, k):
    return jnp.where(ids == label - k * TEN_DEV, tall, 0.0).astype(bf16)


def second_grads(owners, parity, own_rows, boths, label, scaled, held):
    rows = scaled.shape[0]
    count = owners // 2
    step = min(ROW_STEP, rows)
    second = None
    line = iota((count * own_rows, step), 0)
    ids = second_ids(count, own_rows, step)
    ids = ids + (over(line, own_rows) + parity) * TEN_DEV
    for r in range(0, rows, step):
        at = slice(r, r + step)
        held[...] = total(boths, MID, at)
        if own_rows >= ADAPTER_RANK:
            low = jnp.concatenate([held[...]] * (count * own_rows // ADAPTER_RANK), axis=0)
        else:
            first = lax.rem(lax.axis_index("fsdp") * own_rows, ADAPTER_RANK)
            low = held[pl.ds(pl.multiple_of(first, own_rows), own_rows)]
            low = jnp.concatenate([low] * count, axis=0)
        low = jnp.where(ids == label[0:1, at], low, 0.0).astype(bf16)
        term = dot(low, scaled[at])
        second = term if second is None else second + term
    return adapter_scale * ADAPTER_RANK ** (-0.5) * second


def grads_step(
    owners, parity, own_rows, boths, label, acts, scaled, held, out, arrived, send, span, wait=None
):
    width = span[1] - span[0]
    keys = scaled.shape[1]
    columns = out.shape[1]
    down = adapter_scale * MODEL_WIDTH ** (-0.5)
    ends = out.shape[2] > width
    if ends:
        second = second_grads(owners, parity, own_rows, boths, label, scaled, held)
    tall = down * total(boths, BACK, slice(None))
    ids = over(iota((columns, tall.shape[1]), 0), ADAPTER_RANK)
    tall = jnp.concatenate([tall] * (columns // ADAPTER_RANK), axis=0)
    for n in range(owners // 2):
        rows = spread(tall, ids, label[0:1], 2 * n + parity)
        grad = dot(rows, acts[:, span[0] : span[1]])
        if n == 0 and wait is not None:
            wait()
        if arrived is not None:
            grad = grad + arrived[n, :, :width].astype(f32)
        out[n, :, :width] = grad.astype(bf16)
        if ends:
            for q in range(keys // LANES):
                lines = slice(q * own_rows, (q + 1) * own_rows)
                part = second[n * own_rows : (n + 1) * own_rows, q * LANES : (q + 1) * LANES]
                if arrived is not None:
                    part = part + arrived[n, lines, width:].astype(f32)
                out[n, lines, width:] = part.astype(bf16)
            used = keys // LANES * own_rows
            if used < columns:
                out[n, used:, width:] = jnp.zeros((columns - used, LANES), bf16)
        send[n].start()


def even_kernel(shards, owners, own_rows, span, io, *refs):
    boths, (label, acts, scaled, arrived) = refs[:shards], refs[shards : shards + 4]
    outs = refs[shards + 4 : shards + 4 + owners // 2]
    held, made, got, sems, got_sem = refs[shards + 4 + owners // 2 :]
    lanes = pl.ds(span[0], got.shape[2])
    late = pltpu.make_async_copy(arrived.at[:, :, lanes], got, got_sem)
    late.start()
    send = [pltpu.make_async_copy(made.at[n], outs[n], sems.at[n]) for n in range(owners // 2)]
    io.ready()
    grads_step(
        owners, 0, own_rows, boths, label, acts, scaled, held, made, got, send, span, late.wait
    )
    for copy in send:
        copy.wait()


def main_kernel(shards, owners, own_rows, io, *refs):
    boths, (label, acts, scaled, weight) = refs[:shards], refs[shards : shards + 4]
    a_blocks = refs[shards + 4 : shards + 4 + owners]
    odd, out, held, made, part, a_all, back_wide, sems, odd_sems, part_sems = refs[
        shards + 4 + owners :
    ]
    copies = load_factors(a_blocks, a_all, sems)
    send = [pltpu.make_async_copy(made.at[n], odd.at[n], odd_sems.at[n]) for n in range(owners // 2)]
    io.ready()
    span = (0, acts.shape[1])
    grads_step(owners, 1, own_rows, boths, label, acts, scaled, held, made, None, send, span)
    rows, features = part.shape
    step = min(ROW_STEP, rows)
    width = back_wide.shape[1]
    chunk = min(256, features)
    for r in range(0, rows, step):
        at = slice(r, r + step)
        low = adapter_scale * jnp.transpose(total(boths, BACK, at))
        low = jnp.concatenate([low] * (LANES // ADAPTER_RANK), axis=1)
        where = column_of(label[0:1, at]).astype(jnp.int32) - over(
            iota((step, LANES), 1), ADAPTER_RANK
        )
        for q in range(width // LANES):
            hit = where == q * (LANES // ADAPTER_RANK)
            back_wide[:, q * LANES : (q + 1) * LANES] = jnp.where(hit, low, 0.0).astype(bf16)
        if r == 0:
            for copy in copies:
                copy.wait()
        for c in range(0, features, chunk):
            base = dot(scaled[at], weight[c : c + chunk], 1, 1).astype(bf16)
            factor = [a_all[k, c : c + chunk] for k in range(owners)]
            side = dot(back_wide[...], jnp.concatenate(factor, axis=1), 1, 1).astype(bf16)
            part[at, c : c + chunk] = (base.astype(f32) + side.astype(f32)).astype(bf16)
            copy = pltpu.make_async_copy(
                part.at[pl.ds(r, step), pl.ds(c, chunk)],
                out.at[pl.ds(r, step), pl.ds(c, chunk)],
                part_sems.at[r // step, c // chunk],
            )
            copy.start()
            send.append(copy)
    for copy in send:
        copy.wait()


def adam_kernel(count, own_rows, span, io, *refs):
    grads, firsts, refs = refs[:count], refs[count : count + 3], refs[count + 3 :]
    held, made, in_sems, sems = refs[-4:]
    width = span[1] - span[0]
    ends = grads[0].shape[1] > width
    at = pl.ds(span[0], width)
    seconds = refs[:3] if ends else ()
    outs = refs[:-4][-6:] if ends else refs[:-4]
    loads = [
        pltpu.make_async_copy(firsts[m].at[at], held.at[m], in_sems.at[m]) for m in range(3)
    ]
    for copy in loads:
        copy.start()

    def summed(lanes):
        value = grads[0][:, lanes].astype(f32)
        for part in grads[1:]:
            value = value + part[:, lanes].astype(f32)
        return value

    io.ready()
    for copy in loads:
        copy.wait()
    copies = []
    block = min(256, width)
    for n, c in enumerate(range(0, width, block)):
        rows = slice(c, c + block)
        grad = jnp.transpose(summed(rows))
        for m, value in enumerate(adam_step(*[held[m, rows] for m in range(3)], grad)):
            made[m, rows] = value
            copies.append(
                pltpu.make_async_copy(
                    made.at[m, pl.ds(c, block)],
                    outs[m].at[pl.ds(span[0] + c, block)],
                    sems.at[m, n],
                )
            )
            copies[-1].start()
    if ends:
        grad = summed(slice(width, width + LANES))
        for q in range(seconds[0].shape[1] // LANES):
            lanes = slice(q * LANES, (q + 1) * LANES)
            part = grad[q * own_rows : (q + 1) * own_rows]
            for out, value in zip(outs[3:], adam_step(*[x[:, lanes] for x in seconds], part)):
                out[:, lanes] = value
    for copy in copies:
        copy.wait()


def lay_kernel(io, blocks, out):
    io.ready()
    shards, _, width = blocks.shape
    for j in range(shards):
        out[:, j * width : (j + 1) * width] = blocks[j]


def swap(block, axis, bits):
    size = lax.axis_size(axis)
    return lax.ppermute(block, axis, [(i, i ^ bits) for i in range(size)])


def exchange(blocks, axis, groups=None):
    return lax.all_to_all(
        blocks, axis, split_axis=0, concat_axis=0, tiled=True, axis_index_groups=groups
    )

def per_device(
    acts,
    cotangent,
    tenant,
    advantage,
    base_weight,
    a_param,
    a_moment,
    a_second,
    b_param,
    b_moment,
    b_second,
):
    owners = lax.axis_size("dp")
    shards = lax.axis_size("fsdp")
    row_count, keys = cotangent.shape
    features, columns = a_param.shape
    own_rows = b_param.shape[0]
    rows = row_count * shards

    unit = min(features, keys)
    b_lines = own_rows * keys // columns
    lines = (features + keys) // unit * row_count + LABEL_ROWS

    packed, low = call(
        prep_kernel,
        [shape((shards, lines, unit)), shape((features + b_lines, columns))],
        (acts, cotangent, tenant[None], advantage[None], a_param, b_param),
        "h" * 6,
        "hh",
    )
    packed = exchange(packed, "fsdp")
    chips = [low] + [swap(low, "dp", k) for k in range(2, owners, 2)]
    blocks = []
    for block in chips:
        blocks += [block, swap(block, "dp", 1)]

    step = min(ROW_STEP, rows)
    factors = pltpu.VMEM((owners, features, columns), bf16)
    acts_part, scaled, label, both = call(
        functools.partial(open_kernel, owners, own_rows),
        [
            shape((rows, features)),
            shape((rows, keys)),
            shape((8, rows), jnp.int32),
            shape((2 * ADAPTER_RANK, rows)),
        ],
        (packed, *blocks),
        "r" + "r" * owners,
        "hhhh",
        [
            pltpu.VMEM((shards, LABEL_ROWS, unit), bf16),
            pltpu.VMEM((owners * own_rows, keys), bf16),
            factors,
            DMA((shards, (features + keys) // unit + 1)),
            DMA((owners, keys // columns)),
            DMA((owners,)),
        ],
    )
    boths = [both] + [swap(both, "fsdp", j) for j in range(1, shards)]

    grads = shape((owners // 2, columns, features + LANES))
    held = [pltpu.VMEM((ADAPTER_RANK, step), f32), pltpu.VMEM(grads.shape, bf16)]
    odd, grad_part = call(
        functools.partial(main_kernel, shards, owners, own_rows),
        [grads, shape((rows, features))],
        (*boths, label, acts_part, scaled, base_weight, *blocks),
        "h" * (shards + 4) + "r" * owners,
        "rr",
        held
        + [
            pltpu.VMEM((rows, features), bf16),
            factors,
            pltpu.VMEM((step, owners * columns), bf16),
            DMA((owners,)),
            DMA((owners // 2,)),
            DMA((rows // step, features // min(256, features))),
        ],
    )
    returned = exchange(grad_part.reshape(shards, row_count, features), "fsdp")
    grad_input = call(
        lay_kernel, shape((row_count, shards * features)), (returned,), "h", "h"
    )
    arrived = swap(odd, "dp", 1)
    count = owners // 2
    half = features // 2
    sums = []
    for first in (0, half):
        lanes = half if first == 0 else half + LANES
        even = call(
            functools.partial(even_kernel, shards, owners, own_rows, (first, first + half)),
            [shape((columns, lanes))] * count,
            (*boths, label, acts_part, scaled, arrived),
            "h" * (shards + 3) + "r",
            "r" * count,
            [
                held[0],
                pltpu.VMEM((count, columns, lanes), bf16),
                pltpu.VMEM((count, columns, lanes), bf16),
                DMA((count,)),
                DMA,
            ],
        )
        if first == 0:
            arrived, *even = lax.optimization_barrier((arrived, *even))
        sums.append([even[0]] + [swap(even[n], "dp", 2 * n) for n in range(1, count)])

    firsts = (a_param, a_moment, a_second)
    space = [
        pltpu.VMEM((3, half, columns), f32),
        pltpu.VMEM((3, half, columns), f32),
        DMA((3,)),
        DMA((3, half // min(256, half))),
    ]
    begun = call(
        functools.partial(adam_kernel, count, own_rows, (0, half)),
        [shape(a_param.shape, f32)] * 3,
        (*sums[0], *firsts),
        "h" * count + "rrr",
        "rrr",
        space,
    )
    new = call(
        functools.partial(adam_kernel, count, own_rows, (half, features)),
        [shape(a_param.shape, f32)] * 3 + [shape(b_param.shape, f32)] * 3,
        (*sums[1], *firsts, b_param, b_moment, b_second, *begun),
        "h" * count + "rrr" + "hhh" + "rrr",
        "rrrhhh",
        space,
        {count + 6 + m: m for m in range(3)},
    )
    return (grad_input, *new)


def solution(mesh):
    rows = P(("dp", "fsdp"), None)
    labels = P(("dp", "fsdp"))
    first = P("fsdp", "dp")
    return jax.shard_map(
        per_device,
        mesh=mesh,
        in_specs=(rows, rows, labels, labels, P("fsdp", None), first, first, first, rows, rows, rows),
        out_specs=(rows, first, first, first, rows, rows, rows),
        check_vma=False,
    )
```

```python
import functools

import jax
import jax.numpy as jnp
from jax import lax
from jax.experimental import pallas as pl
from jax.experimental.pallas import tpu as pltpu
from jax.sharding import PartitionSpec as P

MODEL_WIDTH = 4096
ADAPTER_RANK = 32
TEN_DEV = 8
LANES = 128
ROW_STEP = 512
MID_STEP = 256
PIECE = 256
LABEL_ROWS = 16
FULL = (64 << 20) - (64 << 10)

adapter_scale = 2.0
learn_rate = 0.02
beta_one = 0.9
beta_two = 0.999
adam_eps = 1e-08
bias_one = 1.0 - 0.9**10
bias_two = 1.0 - 0.999**10

f32 = jnp.float32
bf16 = jnp.bfloat16
HBM = pl.BlockSpec(memory_space=pltpu.HBM)
DMA = pltpu.SemaphoreType.DMA

def shape(dims, kind=bf16):
    return jax.ShapeDtypeStruct(tuple(dims), kind)

class Staging:
    def __init__(self, loads, stores):
        self.loads, self.stores, self.gone = loads, stores, set()

    def ready(self):
        for copy in self.loads:
            copy.wait()

    def store(self, n):
        self.stores[n].start()
        self.gone.add(n)

    def finish(self):
        for n in self.stores:
            if n not in self.gone:
                self.store(n)
        for copy in self.stores.values():
            copy.wait()


def call(body, outs, ins, kinds, out_kinds, scratch=()):
    single = not isinstance(outs, (list, tuple))
    outs = [outs] if single else list(outs)
    staged = [x for x, kind in zip(ins, kinds) if kind == "h"]
    staged_outs = [x for x, kind in zip(outs, out_kinds) if kind == "h"]
    count = len(staged) + len(staged_outs)
    buffers = [pltpu.VMEM(x.shape, x.dtype) for x in staged + staged_outs]

    def kernel(*refs):
        refs = list(refs)
        given, made = refs[: len(ins)], refs[len(ins) : len(ins) + len(outs)]
        rest = refs[len(ins) + len(outs) :]
        held, own, sems = rest[:count], rest[count:-1], rest[-1]
        loads, stores = [], {}
        for n, kind in enumerate(kinds):
            if kind == "h":
                at = len(loads)
                loads.append(pltpu.make_async_copy(given[n], held[at], sems.at[at]))
                given[n] = held[at]
        for n, kind in enumerate(out_kinds):
            if kind == "h":
                at = len(loads) + len(stores)
                stores[n] = pltpu.make_async_copy(held[at], made[n], sems.at[at])
                made[n] = held[at]
        for copy in loads:
            copy.start()
        io = Staging(loads, stores)
        body(io, *given, *made, *own)
        io.finish()

    result = pl.pallas_call(
        kernel,
        out_shape=outs,
        in_specs=[HBM] * len(ins),
        out_specs=[HBM] * len(outs),
        scratch_shapes=buffers + list(scratch) + [DMA((count,))],
        compiler_params=pltpu.CompilerParams(vmem_limit_bytes=FULL),
        cost_estimate=pl.CostEstimate(flops=0, bytes_accessed=0, transcendentals=0),
    )(*ins)
    return result[0] if single else result


def adam_step(param, moment, second, gradient):
    moment = beta_one * moment + (1.0 - beta_one) * gradient
    second = beta_two * second + (1.0 - beta_two) * gradient * gradient
    step = (learn_rate / bias_one) * moment
    param = param - step / (jnp.sqrt((1.0 / bias_two) * second) + adam_eps)
    return (param, moment, second)

def dot(left, right, left_dim=1, right_dim=0):
    return lax.dot_general(
        left, right, (((left_dim,), (right_dim,)), ((), ())), preferred_element_type=f32
    )

def halvings(n):
    return n.bit_length() - 1


def over(x, n):
    return lax.shift_right_logical(x, jnp.full(x.shape, halvings(n), jnp.int32))


def past(x, n):
    return x & (n - 1)


def iota(dims, axis):
    return lax.broadcasted_iota(jnp.int32, dims, axis)

def column_of(row, lanes=LANES):
    n = row.shape[1]
    wide = jnp.broadcast_to(row.astype(f32), (lanes, n))
    return jnp.transpose(wide)

def prep_kernel(io, acts, cot, tenant, advantage, a_param, b_param, packed, low):
    io.ready()
    rows, keys = cot.shape
    shards, _, unit = packed.shape
    features, columns = a_param.shape
    factor = column_of(advantage[...]) * 0.25
    factor = jnp.concatenate([factor] * (keys // LANES), axis=1)
    scaled = (cot[...].astype(f32) * factor).astype(bf16)
    t = tenant[...]
    line = iota((LABEL_ROWS, rows), 0)
    owner = jnp.broadcast_to(lax.div(t, TEN_DEV), (LABEL_ROWS, rows))
    local = jnp.broadcast_to(lax.rem(t, TEN_DEV), (LABEL_ROWS, rows))
    labels = jnp.where(line == 0, owner, jnp.where(line == 1, local, 0)).astype(f32)
    labels = labels.astype(bf16)
    for j in range(shards):
        for q in range(features // unit):
            at = j * features + q * unit
            packed[j, q * rows : (q + 1) * rows] = acts[:, at : at + unit]
        first = features // unit * rows
        for q in range(keys // unit):
            packed[j, first + q * rows : first + (q + 1) * rows] = scaled[:, q * unit : (q + 1) * unit]
        first += keys // unit * rows
        packed[j, first:, :rows] = labels
        packed[j, first:, rows:] = jnp.zeros((LABEL_ROWS, unit - rows), bf16)
    io.store(0)
    low[:features] = (a_param[...] * MODEL_WIDTH ** (-0.5)).astype(bf16)
    own_rows = b_param.shape[0]
    for q in range(keys // columns):
        part = b_param[:, q * columns : (q + 1) * columns] * ADAPTER_RANK ** (-0.5)
        low[features + q * own_rows : features + (q + 1) * own_rows] = part.astype(bf16)


def second_ids(count, own_rows, rows):
    line = iota((count * own_rows, rows), 0)
    inner = past(line, own_rows) + lax.axis_index("fsdp") * own_rows
    return over(line, own_rows) * TEN_DEV + over(inner, ADAPTER_RANK)


def load_factors(a_blocks, a_all, sems):
    columns = a_blocks[0].shape[1]
    copies = [
        pltpu.make_async_copy(
            block.at[pl.ds(0, a_all.shape[0])],
            a_all.at[:, pl.ds(k * columns, columns)],
            sems.at[k],
        )
        for k, block in enumerate(a_blocks)
    ]
    for copy in copies:
        copy.start()
    return copies


def open_kernel(owners, own_rows, io, packed, *refs):
    blocks = refs[:owners]
    acts, scaled, label, both, marks, b_all, a_all, in_sems, b_sems, sems = refs[owners:]
    rows, features = acts.shape
    keys = scaled.shape[1]
    columns = blocks[0].shape[1]
    shards, _, unit = packed.shape
    rd = rows // shards
    first = (features + keys) // unit * rd
    act_copies, row_copies, b_copies = [], [], []
    for j in range(shards):
        at = pl.ds(j * rd, rd)
        for q in range((features + keys) // unit):
            piece = packed.at[j, pl.ds(q * rd, rd)]
            c = q * unit
            if c < features:
                copy = pltpu.make_async_copy(piece, acts.at[at, pl.ds(c, unit)], in_sems.at[j, q])
                act_copies.append(copy)
            else:
                to = scaled.at[at, pl.ds(c - features, unit)]
                row_copies.append(pltpu.make_async_copy(piece, to, in_sems.at[j, q]))
        row_copies.append(
            pltpu.make_async_copy(
                packed.at[j, pl.ds(first, LABEL_ROWS)], marks.at[j], in_sems.at[j, first // rd]
            )
        )
    for k in range(owners):
        for q in range(keys // columns):
            b_copies.append(
                pltpu.make_async_copy(
                    blocks[k].at[pl.ds(features + q * own_rows, own_rows)],
                    b_all.at[pl.ds(k * own_rows, own_rows), pl.ds(q * columns, columns)],
                    b_sems.at[k, q],
                )
            )
    for copy in row_copies + b_copies + act_copies:
        copy.start()
    copies = load_factors(blocks, a_all, sems)
    me = lax.axis_index("dp")
    for copy in row_copies:
        copy.wait()
    for j in range(shards):
        ids = marks[j, :, :rd].astype(f32).astype(jnp.int32)
        tid = (ids[0:1] ^ me) * TEN_DEV + ids[1:2]
        label[:, j * rd : (j + 1) * rd] = jnp.broadcast_to(tid, (8, rd))
    io.store(1)
    io.store(2)
    step = min(ROW_STEP, rows)
    ids = second_ids(owners, own_rows, step)
    for copy in b_copies:
        copy.wait()
    for r in range(0, rows, step):
        at = slice(r, r + step)
        wide = dot(b_all[...], scaled[at], 1, 1)
        wide = jnp.where(ids == label[0:1, at], wide, 0.0)
        if own_rows >= ADAPTER_RANK:
            low = jnp.sum(wide.reshape(-1, ADAPTER_RANK, step), axis=0)
        else:
            low = jnp.sum(wide.reshape(-1, own_rows, step), axis=0)
            low = jnp.concatenate([low] * (ADAPTER_RANK // own_rows), axis=0)
            part = over(iota(low.shape, 0), own_rows)
            place = lax.rem(lax.axis_index("fsdp"), ADAPTER_RANK // own_rows)
            low = jnp.where(part == place, low, 0.0)
        both[:ADAPTER_RANK, at] = low.astype(bf16)
    for copy in act_copies:
        copy.wait()
    io.store(0)
    step = min(MID_STEP, rows)
    for r in range(0, rows, step):
        at = slice(r, r + step)
        where = column_of(label[0:1, at]).astype(jnp.int32) - over(
            iota((step, LANES), 1), ADAPTER_RANK
        )
        low = jnp.zeros((step, LANES), f32)
        for k in range(owners):
            if r == 0:
                copies[k].wait()
            wide = dot(acts[at], a_all[:, k * columns : (k + 1) * columns])
            for q in range(columns // LANES):
                hit = where == k * TEN_DEV + q * (LANES // ADAPTER_RANK)
                low = low + jnp.where(hit, wide[:, q * LANES : (q + 1) * LANES], 0.0)
        low = jnp.transpose(low).reshape(LANES // ADAPTER_RANK, ADAPTER_RANK, step)
        both[ADAPTER_RANK:, at] = jnp.sum(low, axis=0).astype(bf16)


def total(parts, lines, at):
    value = parts[0][lines, at].astype(f32)
    for part in parts[1:]:
        value = value + part[lines, at].astype(f32)
    return value


BACK = slice(0, ADAPTER_RANK)
MID = slice(ADAPTER_RANK, 2 * ADAPTER_RANK)


def spread(tall, ids, label, k):
    return jnp.where(ids == label - k * TEN_DEV, tall, 0.0).astype(bf16)


def second_grads(owners, parity, own_rows, boths, label, scaled, held):
    rows = scaled.shape[0]
    count = owners // 2
    step = min(ROW_STEP, rows)
    second = None
    line = iota((count * own_rows, step), 0)
    ids = second_ids(count, own_rows, step)
    ids = ids + (over(line, own_rows) + parity) * TEN_DEV
    for r in range(0, rows, step):
        at = slice(r, r + step)
        held[...] = total(boths, MID, at)
        if own_rows >= ADAPTER_RANK:
            low = jnp.concatenate([held[...]] * (count * own_rows // ADAPTER_RANK), axis=0)
        else:
            first = lax.rem(lax.axis_index("fsdp") * own_rows, ADAPTER_RANK)
            low = held[pl.ds(pl.multiple_of(first, own_rows), own_rows)]
            low = jnp.concatenate([low] * count, axis=0)
        low = jnp.where(ids == label[0:1, at], low, 0.0).astype(bf16)
        term = dot(low, scaled[at])
        second = term if second is None else second + term
    return adapter_scale * ADAPTER_RANK ** (-0.5) * second


def grads_step(owners, parity, own_rows, boths, label, acts, scaled, held, out, arrived, send, wait=None):
    features = acts.shape[1]
    keys = scaled.shape[1]
    columns = out.shape[1]
    down = adapter_scale * MODEL_WIDTH ** (-0.5)
    second = second_grads(owners, parity, own_rows, boths, label, scaled, held)
    tall = down * total(boths, BACK, slice(None))
    ids = over(iota((columns, tall.shape[1]), 0), ADAPTER_RANK)
    tall = jnp.concatenate([tall] * (columns // ADAPTER_RANK), axis=0)
    for n in range(owners // 2):
        spread_rows = spread(tall, ids, label[0:1], 2 * n + parity)
        for c in range(0, features, PIECE):
            at = slice(c, min(c + PIECE, features))
            grad = dot(spread_rows, acts[:, at])
            if n == 0 and c == 0 and wait is not None:
                wait()
            if arrived is not None:
                grad = grad + arrived[n, :, at].astype(f32)
            out[n, :, at] = grad.astype(bf16)
        for q in range(keys // LANES):
            lines = slice(q * own_rows, (q + 1) * own_rows)
            part = second[n * own_rows : (n + 1) * own_rows, q * LANES : (q + 1) * LANES]
            if arrived is not None:
                part = part + arrived[n, lines, features:].astype(f32)
            out[n, lines, features:] = part.astype(bf16)
        used = keys // LANES * own_rows
        if used < columns:
            out[n, used:, features:] = jnp.zeros((columns - used, LANES), bf16)
        send[n].start()


def even_kernel(shards, owners, own_rows, io, *refs):
    boths, (label, acts, scaled, arrived) = refs[:shards], refs[shards : shards + 4]
    outs = refs[shards + 4 : shards + 4 + owners // 2]
    held, made, got, sems, got_sem = refs[shards + 4 + owners // 2 :]
    late = pltpu.make_async_copy(arrived, got, got_sem)
    late.start()
    send = [pltpu.make_async_copy(made.at[n], outs[n], sems.at[n]) for n in range(owners // 2)]
    io.ready()
    grads_step(
        owners, 0, own_rows, boths, label, acts, scaled, held, made, got, send, late.wait
    )
    for copy in send:
        copy.wait()


def main_kernel(shards, owners, own_rows, io, *refs):
    boths, (label, acts, scaled, weight) = refs[:shards], refs[shards : shards + 4]
    a_blocks = refs[shards + 4 : shards + 4 + owners]
    odd, out, held, made, part, a_all, back_wide, sems, odd_sems, part_sems = refs[
        shards + 4 + owners :
    ]
    copies = load_factors(a_blocks, a_all, sems)
    send = [pltpu.make_async_copy(made.at[n], odd.at[n], odd_sems.at[n]) for n in range(owners // 2)]
    io.ready()
    grads_step(owners, 1, own_rows, boths, label, acts, scaled, held, made, None, send)
    rows, features = part.shape
    step = min(ROW_STEP, rows)
    width = a_all.shape[1]
    chunk = min(256, features)
    for r in range(0, rows, step):
        at = slice(r, r + step)
        low = adapter_scale * jnp.transpose(total(boths, BACK, at))
        low = jnp.concatenate([low] * (LANES // ADAPTER_RANK), axis=1)
        where = column_of(label[0:1, at]).astype(jnp.int32) - over(
            iota((step, LANES), 1), ADAPTER_RANK
        )
        for q in range(width // LANES):
            hit = where == q * (LANES // ADAPTER_RANK)
            back_wide[:, q * LANES : (q + 1) * LANES] = jnp.where(hit, low, 0.0).astype(bf16)
        if r == 0:
            for copy in copies:
                copy.wait()
        for c in range(0, features, chunk):
            for h in range(0, step, PIECE):
                rows_at = slice(r + h, r + min(h + PIECE, step))
                base = dot(scaled[rows_at], weight[c : c + chunk], 1, 1).astype(bf16)
                wide = back_wide[h : min(h + PIECE, step)]
                side = dot(wide, a_all[c : c + chunk], 1, 1).astype(bf16)
                whole = base.astype(f32) + side.astype(f32)
                part[rows_at, c : c + chunk] = whole.astype(bf16)
            copy = pltpu.make_async_copy(
                part.at[pl.ds(r, step), pl.ds(c, chunk)],
                out.at[pl.ds(r, step), pl.ds(c, chunk)],
                part_sems.at[r // step, c // chunk],
            )
            copy.start()
            send.append(copy)
    for copy in send:
        copy.wait()


def adam_kernel(count, own_rows, io, *refs):
    grads, firsts = refs[:count], refs[count : count + 3]
    seconds, outs = refs[count + 3 : count + 6], refs[count + 6 : count + 12]
    made, sems = refs[count + 12 : count + 15], refs[count + 15]
    features, _ = firsts[0].shape
    keys = seconds[0].shape[1]
    io.ready()

    def summed(at):
        value = grads[0][:, at].astype(f32)
        for part in grads[1:]:
            value = value + part[:, at].astype(f32)
        return value

    copies = []
    block = min(256, features)
    for n, c in enumerate(range(0, features, block)):
        at = slice(c, c + block)
        grad = jnp.transpose(summed(at))
        for m, value in enumerate(adam_step(*[x[at] for x in firsts], grad)):
            made[m][at] = value
            rows = pl.ds(c, block)
            copies.append(
                pltpu.make_async_copy(made[m].at[rows], outs[m].at[rows], sems.at[m, n])
            )
            copies[-1].start()
    grad = summed(slice(features, features + LANES))
    for q in range(keys // LANES):
        at = slice(q * LANES, (q + 1) * LANES)
        part = grad[q * own_rows : (q + 1) * own_rows]
        for out, value in zip(outs[3:], adam_step(*[x[:, at] for x in seconds], part)):
            out[:, at] = value
    for copy in copies:
        copy.wait()


def lay_kernel(io, blocks, out):
    io.ready()
    shards, _, width = blocks.shape
    for j in range(shards):
        out[:, j * width : (j + 1) * width] = blocks[j]


def swap(block, axis, bits):
    size = lax.axis_size(axis)
    return lax.ppermute(block, axis, [(i, i ^ bits) for i in range(size)])


def exchange(blocks, axis, groups=None):
    return lax.all_to_all(
        blocks, axis, split_axis=0, concat_axis=0, tiled=True, axis_index_groups=groups
    )

def per_device(
    acts,
    cotangent,
    tenant,
    advantage,
    base_weight,
    a_param,
    a_moment,
    a_second,
    b_param,
    b_moment,
    b_second,
):
    owners = lax.axis_size("dp")
    shards = lax.axis_size("fsdp")
    row_count, keys = cotangent.shape
    features, columns = a_param.shape
    own_rows = b_param.shape[0]
    rows = row_count * shards

    unit = min(features, keys)
    b_lines = own_rows * keys // columns
    lines = (features + keys) // unit * row_count + LABEL_ROWS

    packed, low = call(
        prep_kernel,
        [shape((shards, lines, unit)), shape((features + b_lines, columns))],
        (acts, cotangent, tenant[None], advantage[None], a_param, b_param),
        "h" * 6,
        "hh",
    )
    packed = exchange(packed, "fsdp")
    chips = [low] + [swap(low, "dp", k) for k in range(2, owners, 2)]
    blocks = []
    for block in chips:
        blocks += [block, swap(block, "dp", 1)]

    step = min(ROW_STEP, rows)
    factors = pltpu.VMEM((features, owners * columns), bf16)
    acts_part, scaled, label, both = call(
        functools.partial(open_kernel, owners, own_rows),
        [
            shape((rows, features)),
            shape((rows, keys)),
            shape((8, rows), jnp.int32),
            shape((2 * ADAPTER_RANK, rows)),
        ],
        (packed, *blocks),
        "r" + "r" * owners,
        "hhhh",
        [
            pltpu.VMEM((shards, LABEL_ROWS, unit), bf16),
            pltpu.VMEM((owners * own_rows, keys), bf16),
            factors,
            DMA((shards, (features + keys) // unit + 1)),
            DMA((owners, keys // columns)),
            DMA((owners,)),
        ],
    )
    boths = [both] + [swap(both, "fsdp", j) for j in range(1, shards)]

    grads = shape((owners // 2, columns, features + LANES))
    held = [pltpu.VMEM((ADAPTER_RANK, step), f32), pltpu.VMEM(grads.shape, bf16)]
    odd, grad_part = call(
        functools.partial(main_kernel, shards, owners, own_rows),
        [grads, shape((rows, features))],
        (*boths, label, acts_part, scaled, base_weight, *blocks),
        "h" * (shards + 4) + "r" * owners,
        "rr",
        held
        + [
            pltpu.VMEM((rows, features), bf16),
            factors,
            pltpu.VMEM((step, owners * columns), bf16),
            DMA((owners,)),
            DMA((owners // 2,)),
            DMA((rows // step, features // min(256, features))),
        ],
    )
    returned = exchange(grad_part.reshape(shards, row_count, features), "fsdp")
    grad_input = call(
        lay_kernel, shape((row_count, shards * features)), (returned,), "h", "h"
    )
    even = call(
        functools.partial(even_kernel, shards, owners, own_rows),
        [shape((columns, features + LANES))] * (owners // 2),
        (*boths, label, acts_part, scaled, swap(odd, "dp", 1)),
        "h" * (shards + 3) + "r",
        "r" * (owners // 2),
        held + [pltpu.VMEM(grads.shape, bf16), DMA((owners // 2,)), DMA],
    )
    sums = [even[0]] + [swap(even[n], "dp", 2 * n) for n in range(1, owners // 2)]

    new = call(
        functools.partial(adam_kernel, owners // 2, own_rows),
        [shape(a_param.shape, f32)] * 3 + [shape(b_param.shape, f32)] * 3,
        (*sums, a_param, a_moment, a_second, b_param, b_moment, b_second),
        "h" * (owners // 2 + 6),
        "rrrhhh",
        [pltpu.VMEM(a_param.shape, f32)] * 3 + [DMA((3, features // min(256, features)))],
    )
    return (grad_input, *new)


def solution(mesh):
    rows = P(("dp", "fsdp"), None)
    labels = P(("dp", "fsdp"))
    first = P("fsdp", "dp")
    return jax.shard_map(
        per_device,
        mesh=mesh,
        in_specs=(rows, rows, labels, labels, P("fsdp", None), first, first, first, rows, rows, rows),
        out_specs=(rows, first, first, first, rows, rows, rows),
        check_vma=False,
    )
```

```python
import functools

import jax
import jax.numpy as jnp
from jax import lax
from jax.experimental import pallas as pl
from jax.experimental.pallas import tpu as pltpu
from jax.sharding import PartitionSpec as P

MODEL_WIDTH = 4096
ADAPTER_RANK = 32
TEN_DEV = 8
LANES = 128
ROW_STEP = 512
MID_STEP = 256
LABEL_ROWS = 16
FULL = (64 << 20) - (64 << 10)

adapter_scale = 2.0
learn_rate = 0.02
beta_one = 0.9
beta_two = 0.999
adam_eps = 1e-08
bias_one = 1.0 - 0.9**10
bias_two = 1.0 - 0.999**10

SOME = 16 << 20

f32 = jnp.float32
bf16 = jnp.bfloat16
HBM = pl.BlockSpec(memory_space=pltpu.HBM)
VMEM = pl.BlockSpec(memory_space=pltpu.VMEM)
DMA = pltpu.SemaphoreType.DMA

def shape(dims, kind=bf16):
    return jax.ShapeDtypeStruct(tuple(dims), kind)

class Staging:
    def __init__(self, loads, stores):
        self.loads, self.stores, self.gone = loads, stores, set()

    def ready(self):
        for copy in self.loads:
            copy.wait()

    def store(self, n):
        self.stores[n].start()
        self.gone.add(n)

    def finish(self):
        for n in self.stores:
            if n not in self.gone:
                self.store(n)
        for copy in self.stores.values():
            copy.wait()


def call(body, outs, ins, kinds, out_kinds, scratch=(), room=FULL):
    single = not isinstance(outs, (list, tuple))
    outs = [outs] if single else list(outs)
    staged = [x for x, kind in zip(ins, kinds) if kind == "h"]
    staged_outs = [x for x, kind in zip(outs, out_kinds) if kind == "h"]
    count = len(staged) + len(staged_outs)
    buffers = [pltpu.VMEM(x.shape, x.dtype) for x in staged + staged_outs]

    def kernel(*refs):
        refs = list(refs)
        given, made = refs[: len(ins)], refs[len(ins) : len(ins) + len(outs)]
        rest = refs[len(ins) + len(outs) :]
        held, own, sems = rest[:count], rest[count:-1], rest[-1]
        loads, stores = [], {}
        for n, kind in enumerate(kinds):
            if kind == "h":
                at = len(loads)
                loads.append(pltpu.make_async_copy(given[n], held[at], sems.at[at]))
                given[n] = held[at]
        for n, kind in enumerate(out_kinds):
            if kind == "h":
                at = len(loads) + len(stores)
                stores[n] = pltpu.make_async_copy(held[at], made[n], sems.at[at])
                made[n] = held[at]
        for copy in loads:
            copy.start()
        io = Staging(loads, stores)
        body(io, *given, *made, *own)
        io.finish()

    result = pl.pallas_call(
        kernel,
        out_shape=outs,
        in_specs=[VMEM if kind == "v" else HBM for kind in kinds],
        out_specs=[HBM] * len(outs),
        scratch_shapes=buffers + list(scratch) + [DMA((count,))],
        compiler_params=pltpu.CompilerParams(vmem_limit_bytes=room),
        cost_estimate=pl.CostEstimate(flops=0, bytes_accessed=0, transcendentals=0),
    )(*ins)
    return result[0] if single else result


def adam_step(param, moment, second, gradient):
    moment = beta_one * moment + (1.0 - beta_one) * gradient
    second = beta_two * second + (1.0 - beta_two) * gradient * gradient
    step = (learn_rate / bias_one) * moment
    param = param - step / (jnp.sqrt((1.0 / bias_two) * second) + adam_eps)
    return (param, moment, second)

def dot(left, right, left_dim=1, right_dim=0):
    return lax.dot_general(
        left, right, (((left_dim,), (right_dim,)), ((), ())), preferred_element_type=f32
    )

def halvings(n):
    return n.bit_length() - 1


def over(x, n):
    return lax.shift_right_logical(x, jnp.full(x.shape, halvings(n), jnp.int32))


def past(x, n):
    return x & (n - 1)


def iota(dims, axis):
    return lax.broadcasted_iota(jnp.int32, dims, axis)

def column_of(row, lanes=LANES):
    n = row.shape[1]
    wide = jnp.broadcast_to(row.astype(f32), (lanes, n))
    return jnp.transpose(wide)

def prep_kernel(io, acts, cot, tenant, advantage, a_param, b_param, packed, low):
    io.ready()
    rows, keys = cot.shape
    shards, _, unit = packed.shape
    features, columns = a_param.shape
    factor = column_of(advantage[...]) * 0.25
    factor = jnp.concatenate([factor] * (keys // LANES), axis=1)
    scaled = (cot[...].astype(f32) * factor).astype(bf16)
    t = tenant[...]
    line = iota((LABEL_ROWS, rows), 0)
    owner = jnp.broadcast_to(lax.div(t, TEN_DEV), (LABEL_ROWS, rows))
    local = jnp.broadcast_to(lax.rem(t, TEN_DEV), (LABEL_ROWS, rows))
    labels = jnp.where(line == 0, owner, jnp.where(line == 1, local, 0)).astype(f32)
    labels = labels.astype(bf16)
    for j in range(shards):
        for q in range(features // unit):
            at = j * features + q * unit
            packed[j, q * rows : (q + 1) * rows] = acts[:, at : at + unit]
        first = features // unit * rows
        for q in range(keys // unit):
            packed[j, first + q * rows : first + (q + 1) * rows] = scaled[:, q * unit : (q + 1) * unit]
        first += keys // unit * rows
        packed[j, first:, :rows] = labels
        packed[j, first:, rows:] = jnp.zeros((LABEL_ROWS, unit - rows), bf16)
    io.store(0)
    low[:features] = (a_param[...] * MODEL_WIDTH ** (-0.5)).astype(bf16)
    own_rows = b_param.shape[0]
    for q in range(keys // columns):
        part = b_param[:, q * columns : (q + 1) * columns] * ADAPTER_RANK ** (-0.5)
        low[features + q * own_rows : features + (q + 1) * own_rows] = part.astype(bf16)


def second_ids(count, own_rows, rows):
    line = iota((count * own_rows, rows), 0)
    inner = past(line, own_rows) + lax.axis_index("fsdp") * own_rows
    return over(line, own_rows) * TEN_DEV + over(inner, ADAPTER_RANK)


def load_factors(a_blocks, a_all, sems):
    columns = a_blocks[0].shape[1]
    copies = [
        pltpu.make_async_copy(
            block.at[pl.ds(0, a_all.shape[0])],
            a_all.at[:, pl.ds(k * columns, columns)],
            sems.at[k],
        )
        for k, block in enumerate(a_blocks)
    ]
    for copy in copies:
        copy.start()
    return copies


def open_kernel(owners, own_rows, io, packed, *refs):
    blocks = refs[:owners]
    acts, scaled, label, both, marks, b_all, a_all, in_sems, b_sems, sems = refs[owners:]
    rows, features = acts.shape
    keys = scaled.shape[1]
    columns = blocks[0].shape[1]
    shards, _, unit = packed.shape
    rd = rows // shards
    first = (features + keys) // unit * rd
    act_copies, row_copies, b_copies = [], [], []
    for j in range(shards):
        at = pl.ds(j * rd, rd)
        for q in range((features + keys) // unit):
            piece = packed.at[j, pl.ds(q * rd, rd)]
            c = q * unit
            if c < features:
                copy = pltpu.make_async_copy(piece, acts.at[at, pl.ds(c, unit)], in_sems.at[j, q])
                act_copies.append(copy)
            else:
                to = scaled.at[at, pl.ds(c - features, unit)]
                row_copies.append(pltpu.make_async_copy(piece, to, in_sems.at[j, q]))
        row_copies.append(
            pltpu.make_async_copy(
                packed.at[j, pl.ds(first, LABEL_ROWS)], marks.at[j], in_sems.at[j, first // rd]
            )
        )
    for k in range(owners):
        for q in range(keys // columns):
            b_copies.append(
                pltpu.make_async_copy(
                    blocks[k].at[pl.ds(features + q * own_rows, own_rows)],
                    b_all.at[pl.ds(k * own_rows, own_rows), pl.ds(q * columns, columns)],
                    b_sems.at[k, q],
                )
            )
    for copy in row_copies + b_copies + act_copies:
        copy.start()
    copies = load_factors(blocks, a_all, sems)
    me = lax.axis_index("dp")
    for copy in row_copies:
        copy.wait()
    for j in range(shards):
        ids = marks[j, :, :rd].astype(f32).astype(jnp.int32)
        tid = (ids[0:1] ^ me) * TEN_DEV + ids[1:2]
        label[:, j * rd : (j + 1) * rd] = jnp.broadcast_to(tid, (8, rd))
    io.store(1)
    io.store(2)
    step = min(ROW_STEP, rows)
    ids = second_ids(owners, own_rows, step)
    for copy in b_copies:
        copy.wait()
    for r in range(0, rows, step):
        at = slice(r, r + step)
        wide = dot(b_all[...], scaled[at], 1, 1)
        wide = jnp.where(ids == label[0:1, at], wide, 0.0)
        if own_rows >= ADAPTER_RANK:
            low = jnp.sum(wide.reshape(-1, ADAPTER_RANK, step), axis=0)
        else:
            low = jnp.sum(wide.reshape(-1, own_rows, step), axis=0)
            low = jnp.concatenate([low] * (ADAPTER_RANK // own_rows), axis=0)
            part = over(iota(low.shape, 0), own_rows)
            place = lax.rem(lax.axis_index("fsdp"), ADAPTER_RANK // own_rows)
            low = jnp.where(part == place, low, 0.0)
        both[:ADAPTER_RANK, at] = low.astype(bf16)
    for copy in act_copies:
        copy.wait()
    io.store(0)
    step = min(MID_STEP, rows)
    for r in range(0, rows, step):
        at = slice(r, r + step)
        where = column_of(label[0:1, at]).astype(jnp.int32) - over(
            iota((step, LANES), 1), ADAPTER_RANK
        )
        low = jnp.zeros((step, LANES), f32)
        for k in range(owners):
            if r == 0:
                copies[k].wait()
            wide = dot(acts[at], a_all[:, k * columns : (k + 1) * columns])
            for q in range(columns // LANES):
                hit = where == k * TEN_DEV + q * (LANES // ADAPTER_RANK)
                low = low + jnp.where(hit, wide[:, q * LANES : (q + 1) * LANES], 0.0)
        low = jnp.transpose(low).reshape(LANES // ADAPTER_RANK, ADAPTER_RANK, step)
        both[ADAPTER_RANK:, at] = jnp.sum(low, axis=0).astype(bf16)


def total(parts, lines, at):
    value = parts[0][lines, at].astype(f32)
    for part in parts[1:]:
        value = value + part[lines, at].astype(f32)
    return value


BACK = slice(0, ADAPTER_RANK)
MID = slice(ADAPTER_RANK, 2 * ADAPTER_RANK)


def spread(tall, ids, label, k):
    return jnp.where(ids == label - k * TEN_DEV, tall, 0.0).astype(bf16)


def second_grads(owners, parity, own_rows, boths, label, scaled, held):
    rows = scaled.shape[0]
    count = owners // 2
    step = min(ROW_STEP, rows)
    second = None
    line = iota((count * own_rows, step), 0)
    ids = second_ids(count, own_rows, step)
    ids = ids + (over(line, own_rows) + parity) * TEN_DEV
    for r in range(0, rows, step):
        at = slice(r, r + step)
        held[...] = total(boths, MID, at)
        if own_rows >= ADAPTER_RANK:
            low = jnp.concatenate([held[...]] * (count * own_rows // ADAPTER_RANK), axis=0)
        else:
            first = lax.rem(lax.axis_index("fsdp") * own_rows, ADAPTER_RANK)
            low = held[pl.ds(pl.multiple_of(first, own_rows), own_rows)]
            low = jnp.concatenate([low] * count, axis=0)
        low = jnp.where(ids == label[0:1, at], low, 0.0).astype(bf16)
        term = dot(low, scaled[at])
        second = term if second is None else second + term
    return adapter_scale * ADAPTER_RANK ** (-0.5) * second


def grads_step(owners, parity, own_rows, boths, label, acts, scaled, held, out, arrived, send, wait=None):
    features = acts.shape[1]
    keys = scaled.shape[1]
    columns = out.shape[1]
    down = adapter_scale * MODEL_WIDTH ** (-0.5)
    second = second_grads(owners, parity, own_rows, boths, label, scaled, held)
    tall = down * total(boths, BACK, slice(None))
    ids = over(iota((columns, tall.shape[1]), 0), ADAPTER_RANK)
    tall = jnp.concatenate([tall] * (columns // ADAPTER_RANK), axis=0)
    for n in range(owners // 2):
        grad = dot(spread(tall, ids, label[0:1], 2 * n + parity), acts[...])
        if n == 0 and wait is not None:
            wait()
        if arrived is not None:
            grad = grad + arrived[n, :, :features].astype(f32)
        out[n, :, :features] = grad.astype(bf16)
        for q in range(keys // LANES):
            lines = slice(q * own_rows, (q + 1) * own_rows)
            part = second[n * own_rows : (n + 1) * own_rows, q * LANES : (q + 1) * LANES]
            if arrived is not None:
                part = part + arrived[n, lines, features:].astype(f32)
            out[n, lines, features:] = part.astype(bf16)
        used = keys // LANES * own_rows
        if used < columns:
            out[n, used:, features:] = jnp.zeros((columns - used, LANES), bf16)
        send[n].start()


def even_kernel(shards, owners, own_rows, io, *refs):
    boths, (label, acts, scaled, arrived) = refs[:shards], refs[shards : shards + 4]
    outs = refs[shards + 4 : shards + 4 + owners // 2]
    held, made, got, sems, got_sem = refs[shards + 4 + owners // 2 :]
    late = pltpu.make_async_copy(arrived, got, got_sem)
    late.start()
    send = [pltpu.make_async_copy(made.at[n], outs[n], sems.at[n]) for n in range(owners // 2)]
    io.ready()
    grads_step(
        owners, 0, own_rows, boths, label, acts, scaled, held, made, got, send, late.wait
    )
    for copy in send:
        copy.wait()


def main_kernel(shards, owners, own_rows, io, *refs):
    boths, (label, acts, scaled, weight) = refs[:shards], refs[shards : shards + 4]
    a_blocks = refs[shards + 4 : shards + 4 + owners]
    odd, out, held, made, part, a_all, back_wide, sems, odd_sems, part_sems = refs[
        shards + 4 + owners :
    ]
    copies = load_factors(a_blocks, a_all, sems)
    send = [pltpu.make_async_copy(made.at[n], odd.at[n], odd_sems.at[n]) for n in range(owners // 2)]
    io.ready()
    grads_step(owners, 1, own_rows, boths, label, acts, scaled, held, made, None, send)
    rows, features = part.shape
    step = min(ROW_STEP, rows)
    width = a_all.shape[1]
    chunk = min(256, features)
    for r in range(0, rows, step):
        at = slice(r, r + step)
        low = adapter_scale * jnp.transpose(total(boths, BACK, at))
        low = jnp.concatenate([low] * (LANES // ADAPTER_RANK), axis=1)
        where = column_of(label[0:1, at]).astype(jnp.int32) - over(
            iota((step, LANES), 1), ADAPTER_RANK
        )
        for q in range(width // LANES):
            hit = where == q * (LANES // ADAPTER_RANK)
            back_wide[:, q * LANES : (q + 1) * LANES] = jnp.where(hit, low, 0.0).astype(bf16)
        if r == 0:
            for copy in copies:
                copy.wait()
        for c in range(0, features, chunk):
            base = dot(scaled[at], weight[c : c + chunk], 1, 1).astype(bf16)
            side = dot(back_wide[...], a_all[c : c + chunk], 1, 1).astype(bf16)
            part[at, c : c + chunk] = (base.astype(f32) + side.astype(f32)).astype(bf16)
            copy = pltpu.make_async_copy(
                part.at[pl.ds(r, step), pl.ds(c, chunk)],
                out.at[pl.ds(r, step), pl.ds(c, chunk)],
                part_sems.at[r // step, c // chunk],
            )
            copy.start()
            send.append(copy)
    for copy in send:
        copy.wait()


def adam_kernel(count, own_rows, io, *refs):
    grads, firsts = refs[:count], refs[count : count + 3]
    seconds, outs = refs[count + 3 : count + 6], refs[count + 6 : count + 12]
    made, sems = refs[count + 12 : count + 15], refs[count + 15]
    features, _ = firsts[0].shape
    keys = seconds[0].shape[1]
    io.ready()

    def summed(at):
        value = grads[0][:, at].astype(f32)
        for part in grads[1:]:
            value = value + part[:, at].astype(f32)
        return value

    copies = []
    block = min(256, features)
    for n, c in enumerate(range(0, features, block)):
        at = slice(c, c + block)
        grad = jnp.transpose(summed(at))
        for m, value in enumerate(adam_step(*[x[at] for x in firsts], grad)):
            made[m][at] = value
            rows = pl.ds(c, block)
            copies.append(
                pltpu.make_async_copy(made[m].at[rows], outs[m].at[rows], sems.at[m, n])
            )
            copies[-1].start()
    grad = summed(slice(features, features + LANES))
    for q in range(keys // LANES):
        at = slice(q * LANES, (q + 1) * LANES)
        part = grad[q * own_rows : (q + 1) * own_rows]
        for out, value in zip(outs[3:], adam_step(*[x[:, at] for x in seconds], part)):
            out[:, at] = value
    for copy in copies:
        copy.wait()


def lay_kernel(io, blocks, out):
    io.ready()
    shards, _, width = blocks.shape
    for j in range(shards):
        out[:, j * width : (j + 1) * width] = blocks[j]


def swap(block, axis, bits):
    size = lax.axis_size(axis)
    return lax.ppermute(block, axis, [(i, i ^ bits) for i in range(size)])


def exchange(blocks, axis, groups=None):
    return lax.all_to_all(
        blocks, axis, split_axis=0, concat_axis=0, tiled=True, axis_index_groups=groups
    )

def per_device(
    acts,
    cotangent,
    tenant,
    advantage,
    base_weight,
    a_param,
    a_moment,
    a_second,
    b_param,
    b_moment,
    b_second,
):
    owners = lax.axis_size("dp")
    shards = lax.axis_size("fsdp")
    row_count, keys = cotangent.shape
    features, columns = a_param.shape
    own_rows = b_param.shape[0]
    rows = row_count * shards

    unit = min(features, keys)
    b_lines = own_rows * keys // columns
    lines = (features + keys) // unit * row_count + LABEL_ROWS

    packed, low = call(
        prep_kernel,
        [shape((shards, lines, unit)), shape((features + b_lines, columns))],
        (acts, cotangent, tenant[None], advantage[None], a_param, b_param),
        "h" * 6,
        "hh",
    )
    packed = exchange(packed, "fsdp")
    chips = [low] + [swap(low, "dp", k) for k in range(2, owners, 2)]
    blocks = []
    for block in chips:
        blocks += [block, swap(block, "dp", 1)]

    step = min(ROW_STEP, rows)
    factors = pltpu.VMEM((features, owners * columns), bf16)
    acts_part, scaled, label, both = call(
        functools.partial(open_kernel, owners, own_rows),
        [
            shape((rows, features)),
            shape((rows, keys)),
            shape((8, rows), jnp.int32),
            shape((2 * ADAPTER_RANK, rows)),
        ],
        (packed, *blocks),
        "r" + "r" * owners,
        "hhhh",
        [
            pltpu.VMEM((shards, LABEL_ROWS, unit), bf16),
            pltpu.VMEM((owners * own_rows, keys), bf16),
            factors,
            DMA((shards, (features + keys) // unit + 1)),
            DMA((owners, keys // columns)),
            DMA((owners,)),
        ],
    )
    boths = [both] + [swap(both, "fsdp", j) for j in range(1, shards)]

    grads = shape((owners // 2, columns, features + LANES))
    held = [pltpu.VMEM((ADAPTER_RANK, step), f32), pltpu.VMEM(grads.shape, bf16)]
    odd, grad_part = call(
        functools.partial(main_kernel, shards, owners, own_rows),
        [grads, shape((rows, features))],
        (*boths, label, acts_part, scaled, base_weight, *blocks),
        "h" * (shards + 4) + "r" * owners,
        "rr",
        held
        + [
            pltpu.VMEM((rows, features), bf16),
            factors,
            pltpu.VMEM((step, owners * columns), bf16),
            DMA((owners,)),
            DMA((owners // 2,)),
            DMA((rows // step, features // min(256, features))),
        ],
    )
    returned = exchange(grad_part.reshape(shards, row_count, features), "fsdp")
    grad_input = call(
        lay_kernel, shape((row_count, shards * features)), (returned,), "h", "h", room=SOME
    )
    even = call(
        functools.partial(even_kernel, shards, owners, own_rows),
        [shape((columns, features + LANES))] * (owners // 2),
        (*boths, label, acts_part, scaled, swap(odd, "dp", 1)),
        "h" * (shards + 3) + "r",
        "r" * (owners // 2),
        held + [pltpu.VMEM(grads.shape, bf16), DMA((owners // 2,)), DMA],
    )
    sums = [even[0]] + [swap(even[n], "dp", 2 * n) for n in range(1, owners // 2)]

    new = call(
        functools.partial(adam_kernel, owners // 2, own_rows),
        [shape(a_param.shape, f32)] * 3 + [shape(b_param.shape, f32)] * 3,
        (*sums, a_param, a_moment, a_second, b_param, b_moment, b_second),
        "v" * (owners // 2 + 6),
        "rrrhhh",
        [pltpu.VMEM(a_param.shape, f32)] * 3 + [DMA((3, features // min(256, features)))],
        room=SOME,
    )
    return (grad_input, *new)


def solution(mesh):
    rows = P(("dp", "fsdp"), None)
    labels = P(("dp", "fsdp"))
    first = P("fsdp", "dp")
    return jax.shard_map(
        per_device,
        mesh=mesh,
        in_specs=(rows, rows, labels, labels, P("fsdp", None), first, first, first, rows, rows, rows),
        out_specs=(rows, first, first, first, rows, rows, rows),
        check_vma=False,
    )
```

```python
import functools

import jax
import jax.numpy as jnp
from jax import lax
from jax.experimental import pallas as pl
from jax.experimental.pallas import tpu as pltpu
from jax.sharding import PartitionSpec as P

MODEL_WIDTH = 4096
ADAPTER_RANK = 32
TEN_DEV = 8
LANES = 128
ROW_STEP = 512
MID_STEP = 256
LABEL_ROWS = 16
FULL = (64 << 20) - (64 << 10)

adapter_scale = 2.0
learn_rate = 0.02
beta_one = 0.9
beta_two = 0.999
adam_eps = 1e-08
bias_one = 1.0 - 0.9**10
bias_two = 1.0 - 0.999**10

f32 = jnp.float32
bf16 = jnp.bfloat16
HBM = pl.BlockSpec(memory_space=pltpu.HBM)
DMA = pltpu.SemaphoreType.DMA

def shape(dims, kind=bf16):
    return jax.ShapeDtypeStruct(tuple(dims), kind)

class Staging:
    def __init__(self, loads, stores):
        self.loads, self.stores, self.gone = loads, stores, set()

    def ready(self):
        for copy in self.loads:
            copy.wait()

    def store(self, n):
        self.stores[n].start()
        self.gone.add(n)

    def finish(self):
        for n in self.stores:
            if n not in self.gone:
                self.store(n)
        for copy in self.stores.values():
            copy.wait()


def call(body, outs, ins, kinds, out_kinds, scratch=()):
    single = not isinstance(outs, (list, tuple))
    outs = [outs] if single else list(outs)
    staged = [x for x, kind in zip(ins, kinds) if kind == "h"]
    staged_outs = [x for x, kind in zip(outs, out_kinds) if kind == "h"]
    count = len(staged) + len(staged_outs)
    buffers = [pltpu.VMEM(x.shape, x.dtype) for x in staged + staged_outs]

    def kernel(*refs):
        refs = list(refs)
        given, made = refs[: len(ins)], refs[len(ins) : len(ins) + len(outs)]
        rest = refs[len(ins) + len(outs) :]
        held, own, sems = rest[:count], rest[count:-1], rest[-1]
        loads, stores = [], {}
        for n, kind in enumerate(kinds):
            if kind == "h":
                at = len(loads)
                loads.append(pltpu.make_async_copy(given[n], held[at], sems.at[at]))
                given[n] = held[at]
        for n, kind in enumerate(out_kinds):
            if kind == "h":
                at = len(loads) + len(stores)
                stores[n] = pltpu.make_async_copy(held[at], made[n], sems.at[at])
                made[n] = held[at]
        for copy in loads:
            copy.start()
        io = Staging(loads, stores)
        body(io, *given, *made, *own)
        io.finish()

    result = pl.pallas_call(
        kernel,
        out_shape=outs,
        in_specs=[HBM] * len(ins),
        out_specs=[HBM] * len(outs),
        scratch_shapes=buffers + list(scratch) + [DMA((count,))],
        compiler_params=pltpu.CompilerParams(vmem_limit_bytes=FULL),
        cost_estimate=pl.CostEstimate(flops=0, bytes_accessed=0, transcendentals=0),
    )(*ins)
    return result[0] if single else result


def adam_step(param, moment, second, gradient):
    moment = beta_one * moment + (1.0 - beta_one) * gradient
    second = beta_two * second + (1.0 - beta_two) * gradient * gradient
    step = (learn_rate / bias_one) * moment
    param = param - step / (jnp.sqrt((1.0 / bias_two) * second) + adam_eps)
    return (param, moment, second)

def dot(left, right, left_dim=1, right_dim=0):
    return lax.dot_general(
        left, right, (((left_dim,), (right_dim,)), ((), ())), preferred_element_type=f32
    )

def halvings(n):
    return n.bit_length() - 1


def over(x, n):
    return lax.shift_right_logical(x, jnp.full(x.shape, halvings(n), jnp.int32))


def past(x, n):
    return x & (n - 1)


def iota(dims, axis):
    return lax.broadcasted_iota(jnp.int32, dims, axis)

def column_of(row, lanes=LANES):
    n = row.shape[1]
    wide = jnp.broadcast_to(row.astype(f32), (lanes, n))
    return jnp.transpose(wide)

def prep_kernel(features, io, acts, cot, tenant, advantage, packed):
    io.ready()
    rows, keys = cot.shape
    shards, _, unit = packed.shape
    factor = column_of(advantage[...]) * 0.25
    factor = jnp.concatenate([factor] * (keys // LANES), axis=1)
    scaled = (cot[...].astype(f32) * factor).astype(bf16)
    t = tenant[...]
    line = iota((LABEL_ROWS, rows), 0)
    owner = jnp.broadcast_to(lax.div(t, TEN_DEV), (LABEL_ROWS, rows))
    local = jnp.broadcast_to(lax.rem(t, TEN_DEV), (LABEL_ROWS, rows))
    labels = jnp.where(line == 0, owner, jnp.where(line == 1, local, 0)).astype(f32)
    labels = labels.astype(bf16)
    for j in range(shards):
        for q in range(features // unit):
            at = j * features + q * unit
            packed[j, q * rows : (q + 1) * rows] = acts[:, at : at + unit]
        first = features // unit * rows
        for q in range(keys // unit):
            packed[j, first + q * rows : first + (q + 1) * rows] = scaled[:, q * unit : (q + 1) * unit]
        first += keys // unit * rows
        packed[j, first:, :rows] = labels
        packed[j, first:, rows:] = jnp.zeros((LABEL_ROWS, unit - rows), bf16)


def low_kernel(io, a_param, b_param, low):
    io.ready()
    features, columns = a_param.shape
    keys = b_param.shape[1]
    low[:features] = (a_param[...] * MODEL_WIDTH ** (-0.5)).astype(bf16)
    own_rows = b_param.shape[0]
    for q in range(keys // columns):
        part = b_param[:, q * columns : (q + 1) * columns] * ADAPTER_RANK ** (-0.5)
        low[features + q * own_rows : features + (q + 1) * own_rows] = part.astype(bf16)


def second_ids(count, own_rows, rows):
    line = iota((count * own_rows, rows), 0)
    inner = past(line, own_rows) + lax.axis_index("fsdp") * own_rows
    return over(line, own_rows) * TEN_DEV + over(inner, ADAPTER_RANK)


def load_factors(a_blocks, a_all, sems):
    columns = a_blocks[0].shape[1]
    copies = [
        pltpu.make_async_copy(
            block.at[pl.ds(0, a_all.shape[0])],
            a_all.at[:, pl.ds(k * columns, columns)],
            sems.at[k],
        )
        for k, block in enumerate(a_blocks)
    ]
    for copy in copies:
        copy.start()
    return copies


def open_kernel(owners, own_rows, io, packed, *refs):
    blocks = refs[:owners]
    acts, scaled, label, both, marks, b_all, a_all, in_sems, b_sems, sems = refs[owners:]
    rows, features = acts.shape
    keys = scaled.shape[1]
    columns = blocks[0].shape[1]
    shards, _, unit = packed.shape
    rd = rows // shards
    first = (features + keys) // unit * rd
    act_copies, row_copies, b_copies = [], [], []
    for j in range(shards):
        at = pl.ds(j * rd, rd)
        for q in range((features + keys) // unit):
            piece = packed.at[j, pl.ds(q * rd, rd)]
            c = q * unit
            if c < features:
                copy = pltpu.make_async_copy(piece, acts.at[at, pl.ds(c, unit)], in_sems.at[j, q])
                act_copies.append(copy)
            else:
                to = scaled.at[at, pl.ds(c - features, unit)]
                row_copies.append(pltpu.make_async_copy(piece, to, in_sems.at[j, q]))
        row_copies.append(
            pltpu.make_async_copy(
                packed.at[j, pl.ds(first, LABEL_ROWS)], marks.at[j], in_sems.at[j, first // rd]
            )
        )
    for k in range(owners):
        for q in range(keys // columns):
            b_copies.append(
                pltpu.make_async_copy(
                    blocks[k].at[pl.ds(features + q * own_rows, own_rows)],
                    b_all.at[pl.ds(k * own_rows, own_rows), pl.ds(q * columns, columns)],
                    b_sems.at[k, q],
                )
            )
    for copy in row_copies + b_copies + act_copies:
        copy.start()
    copies = load_factors(blocks, a_all, sems)
    me = lax.axis_index("dp")
    for copy in row_copies:
        copy.wait()
    for j in range(shards):
        ids = marks[j, :, :rd].astype(f32).astype(jnp.int32)
        tid = (ids[0:1] ^ me) * TEN_DEV + ids[1:2]
        label[:, j * rd : (j + 1) * rd] = jnp.broadcast_to(tid, (8, rd))
    io.store(1)
    io.store(2)
    step = min(ROW_STEP, rows)
    ids = second_ids(owners, own_rows, step)
    for copy in b_copies:
        copy.wait()
    for r in range(0, rows, step):
        at = slice(r, r + step)
        wide = dot(b_all[...], scaled[at], 1, 1)
        wide = jnp.where(ids == label[0:1, at], wide, 0.0)
        if own_rows >= ADAPTER_RANK:
            low = jnp.sum(wide.reshape(-1, ADAPTER_RANK, step), axis=0)
        else:
            low = jnp.sum(wide.reshape(-1, own_rows, step), axis=0)
            low = jnp.concatenate([low] * (ADAPTER_RANK // own_rows), axis=0)
            part = over(iota(low.shape, 0), own_rows)
            place = lax.rem(lax.axis_index("fsdp"), ADAPTER_RANK // own_rows)
            low = jnp.where(part == place, low, 0.0)
        both[:ADAPTER_RANK, at] = low.astype(bf16)
    for copy in act_copies:
        copy.wait()
    io.store(0)
    step = min(MID_STEP, rows)
    for r in range(0, rows, step):
        at = slice(r, r + step)
        where = column_of(label[0:1, at]).astype(jnp.int32) - over(
            iota((step, LANES), 1), ADAPTER_RANK
        )
        low = jnp.zeros((step, LANES), f32)
        for k in range(owners):
            if r == 0:
                copies[k].wait()
            wide = dot(acts[at], a_all[:, k * columns : (k + 1) * columns])
            for q in range(columns // LANES):
                hit = where == k * TEN_DEV + q * (LANES // ADAPTER_RANK)
                low = low + jnp.where(hit, wide[:, q * LANES : (q + 1) * LANES], 0.0)
        low = jnp.transpose(low).reshape(LANES // ADAPTER_RANK, ADAPTER_RANK, step)
        both[ADAPTER_RANK:, at] = jnp.sum(low, axis=0).astype(bf16)


def total(parts, lines, at):
    value = parts[0][lines, at].astype(f32)
    for part in parts[1:]:
        value = value + part[lines, at].astype(f32)
    return value


BACK = slice(0, ADAPTER_RANK)
MID = slice(ADAPTER_RANK, 2 * ADAPTER_RANK)


def spread(tall, ids, label, k):
    return jnp.where(ids == label - k * TEN_DEV, tall, 0.0).astype(bf16)


def second_grads(owners, parity, own_rows, boths, label, scaled, held):
    rows = scaled.shape[0]
    count = owners // 2
    step = min(ROW_STEP, rows)
    second = None
    line = iota((count * own_rows, step), 0)
    ids = second_ids(count, own_rows, step)
    ids = ids + (over(line, own_rows) + parity) * TEN_DEV
    for r in range(0, rows, step):
        at = slice(r, r + step)
        held[...] = total(boths, MID, at)
        if own_rows >= ADAPTER_RANK:
            low = jnp.concatenate([held[...]] * (count * own_rows // ADAPTER_RANK), axis=0)
        else:
            first = lax.rem(lax.axis_index("fsdp") * own_rows, ADAPTER_RANK)
            low = held[pl.ds(pl.multiple_of(first, own_rows), own_rows)]
            low = jnp.concatenate([low] * count, axis=0)
        low = jnp.where(ids == label[0:1, at], low, 0.0).astype(bf16)
        term = dot(low, scaled[at])
        second = term if second is None else second + term
    return adapter_scale * ADAPTER_RANK ** (-0.5) * second


def grads_step(owners, parity, own_rows, boths, label, acts, scaled, held, out, arrived, send, wait=None):
    features = acts.shape[1]
    keys = scaled.shape[1]
    columns = out.shape[1]
    down = adapter_scale * MODEL_WIDTH ** (-0.5)
    second = second_grads(owners, parity, own_rows, boths, label, scaled, held)
    tall = down * total(boths, BACK, slice(None))
    ids = over(iota((columns, tall.shape[1]), 0), ADAPTER_RANK)
    tall = jnp.concatenate([tall] * (columns // ADAPTER_RANK), axis=0)
    for n in range(owners // 2):
        grad = dot(spread(tall, ids, label[0:1], 2 * n + parity), acts[...])
        if n == 0 and wait is not None:
            wait()
        if arrived is not None:
            grad = grad + arrived[n, :, :features].astype(f32)
        out[n, :, :features] = grad.astype(bf16)
        for q in range(keys // LANES):
            lines = slice(q * own_rows, (q + 1) * own_rows)
            part = second[n * own_rows : (n + 1) * own_rows, q * LANES : (q + 1) * LANES]
            if arrived is not None:
                part = part + arrived[n, lines, features:].astype(f32)
            out[n, lines, features:] = part.astype(bf16)
        used = keys // LANES * own_rows
        if used < columns:
            out[n, used:, features:] = jnp.zeros((columns - used, LANES), bf16)
        send[n].start()


def even_kernel(shards, owners, own_rows, io, *refs):
    boths, (label, acts, scaled, arrived) = refs[:shards], refs[shards : shards + 4]
    outs = refs[shards + 4 : shards + 4 + owners // 2]
    held, made, got, sems, got_sem = refs[shards + 4 + owners // 2 :]
    late = pltpu.make_async_copy(arrived, got, got_sem)
    late.start()
    send = [pltpu.make_async_copy(made.at[n], outs[n], sems.at[n]) for n in range(owners // 2)]
    io.ready()
    grads_step(
        owners, 0, own_rows, boths, label, acts, scaled, held, made, got, send, late.wait
    )
    for copy in send:
        copy.wait()


def main_kernel(shards, owners, own_rows, io, *refs):
    boths, (label, acts, scaled, weight) = refs[:shards], refs[shards : shards + 4]
    a_blocks = refs[shards + 4 : shards + 4 + owners]
    odd, out, held, made, part, a_all, back_wide, sems, odd_sems, part_sems = refs[
        shards + 4 + owners :
    ]
    copies = load_factors(a_blocks, a_all, sems)
    send = [pltpu.make_async_copy(made.at[n], odd.at[n], odd_sems.at[n]) for n in range(owners // 2)]
    io.ready()
    grads_step(owners, 1, own_rows, boths, label, acts, scaled, held, made, None, send)
    rows, features = part.shape
    step = min(ROW_STEP, rows)
    width = a_all.shape[1]
    chunk = min(256, features)
    for r in range(0, rows, step):
        at = slice(r, r + step)
        low = adapter_scale * jnp.transpose(total(boths, BACK, at))
        low = jnp.concatenate([low] * (LANES // ADAPTER_RANK), axis=1)
        where = column_of(label[0:1, at]).astype(jnp.int32) - over(
            iota((step, LANES), 1), ADAPTER_RANK
        )
        for q in range(width // LANES):
            hit = where == q * (LANES // ADAPTER_RANK)
            back_wide[:, q * LANES : (q + 1) * LANES] = jnp.where(hit, low, 0.0).astype(bf16)
        if r == 0:
            for copy in copies:
                copy.wait()
        for c in range(0, features, chunk):
            base = dot(scaled[at], weight[c : c + chunk], 1, 1).astype(bf16)
            side = dot(back_wide[...], a_all[c : c + chunk], 1, 1).astype(bf16)
            part[at, c : c + chunk] = (base.astype(f32) + side.astype(f32)).astype(bf16)
            copy = pltpu.make_async_copy(
                part.at[pl.ds(r, step), pl.ds(c, chunk)],
                out.at[pl.ds(r, step), pl.ds(c, chunk)],
                part_sems.at[r // step, c // chunk],
            )
            copy.start()
            send.append(copy)
    for copy in send:
        copy.wait()


def adam_kernel(count, own_rows, io, *refs):
    grads, firsts = refs[:count], refs[count : count + 3]
    seconds, outs = refs[count + 3 : count + 6], refs[count + 6 : count + 12]
    made, sems = refs[count + 12 : count + 15], refs[count + 15]
    features, _ = firsts[0].shape
    keys = seconds[0].shape[1]
    io.ready()

    def summed(at):
        value = grads[0][:, at].astype(f32)
        for part in grads[1:]:
            value = value + part[:, at].astype(f32)
        return value

    copies = []
    block = min(256, features)
    for n, c in enumerate(range(0, features, block)):
        at = slice(c, c + block)
        grad = jnp.transpose(summed(at))
        for m, value in enumerate(adam_step(*[x[at] for x in firsts], grad)):
            made[m][at] = value
            rows = pl.ds(c, block)
            copies.append(
                pltpu.make_async_copy(made[m].at[rows], outs[m].at[rows], sems.at[m, n])
            )
            copies[-1].start()
    grad = summed(slice(features, features + LANES))
    for q in range(keys // LANES):
        at = slice(q * LANES, (q + 1) * LANES)
        part = grad[q * own_rows : (q + 1) * own_rows]
        for out, value in zip(outs[3:], adam_step(*[x[:, at] for x in seconds], part)):
            out[:, at] = value
    for copy in copies:
        copy.wait()


def lay_kernel(io, blocks, out):
    io.ready()
    shards, _, width = blocks.shape
    for j in range(shards):
        out[:, j * width : (j + 1) * width] = blocks[j]


def swap(block, axis, bits):
    size = lax.axis_size(axis)
    return lax.ppermute(block, axis, [(i, i ^ bits) for i in range(size)])


def exchange(blocks, axis, groups=None):
    return lax.all_to_all(
        blocks, axis, split_axis=0, concat_axis=0, tiled=True, axis_index_groups=groups
    )

def per_device(
    acts,
    cotangent,
    tenant,
    advantage,
    base_weight,
    a_param,
    a_moment,
    a_second,
    b_param,
    b_moment,
    b_second,
):
    owners = lax.axis_size("dp")
    shards = lax.axis_size("fsdp")
    row_count, keys = cotangent.shape
    features, columns = a_param.shape
    own_rows = b_param.shape[0]
    rows = row_count * shards

    unit = min(features, keys)
    b_lines = own_rows * keys // columns
    lines = (features + keys) // unit * row_count + LABEL_ROWS

    packed = call(
        functools.partial(prep_kernel, features),
        shape((shards, lines, unit)),
        (acts, cotangent, tenant[None], advantage[None]),
        "hhhh",
        "h",
    )
    packed, a_first, b_first = lax.optimization_barrier((packed, a_param, b_param))
    low = call(
        low_kernel, shape((features + b_lines, columns)), (a_first, b_first), "hh", "h"
    )
    packed = exchange(packed, "fsdp")
    chips = [low] + [swap(low, "dp", k) for k in range(2, owners, 2)]
    blocks = []
    for block in chips:
        blocks += [block, swap(block, "dp", 1)]

    step = min(ROW_STEP, rows)
    factors = pltpu.VMEM((features, owners * columns), bf16)
    acts_part, scaled, label, both = call(
        functools.partial(open_kernel, owners, own_rows),
        [
            shape((rows, features)),
            shape((rows, keys)),
            shape((8, rows), jnp.int32),
            shape((2 * ADAPTER_RANK, rows)),
        ],
        (packed, *blocks),
        "r" + "r" * owners,
        "hhhh",
        [
            pltpu.VMEM((shards, LABEL_ROWS, unit), bf16),
            pltpu.VMEM((owners * own_rows, keys), bf16),
            factors,
            DMA((shards, (features + keys) // unit + 1)),
            DMA((owners, keys // columns)),
            DMA((owners,)),
        ],
    )
    boths = [both] + [swap(both, "fsdp", j) for j in range(1, shards)]

    grads = shape((owners // 2, columns, features + LANES))
    held = [pltpu.VMEM((ADAPTER_RANK, step), f32), pltpu.VMEM(grads.shape, bf16)]
    odd, grad_part = call(
        functools.partial(main_kernel, shards, owners, own_rows),
        [grads, shape((rows, features))],
        (*boths, label, acts_part, scaled, base_weight, *blocks),
        "h" * (shards + 4) + "r" * owners,
        "rr",
        held
        + [
            pltpu.VMEM((rows, features), bf16),
            factors,
            pltpu.VMEM((step, owners * columns), bf16),
            DMA((owners,)),
            DMA((owners // 2,)),
            DMA((rows // step, features // min(256, features))),
        ],
    )
    returned = exchange(grad_part.reshape(shards, row_count, features), "fsdp")
    grad_input = call(
        lay_kernel, shape((row_count, shards * features)), (returned,), "h", "h"
    )
    even = call(
        functools.partial(even_kernel, shards, owners, own_rows),
        [shape((columns, features + LANES))] * (owners // 2),
        (*boths, label, acts_part, scaled, swap(odd, "dp", 1)),
        "h" * (shards + 3) + "r",
        "r" * (owners // 2),
        held + [pltpu.VMEM(grads.shape, bf16), DMA((owners // 2,)), DMA],
    )
    sums = [even[0]] + [swap(even[n], "dp", 2 * n) for n in range(1, owners // 2)]

    new = call(
        functools.partial(adam_kernel, owners // 2, own_rows),
        [shape(a_param.shape, f32)] * 3 + [shape(b_param.shape, f32)] * 3,
        (*sums, a_param, a_moment, a_second, b_param, b_moment, b_second),
        "h" * (owners // 2 + 6),
        "rrrhhh",
        [pltpu.VMEM(a_param.shape, f32)] * 3 + [DMA((3, features // min(256, features)))],
    )
    return (grad_input, *new)


def solution(mesh):
    rows = P(("dp", "fsdp"), None)
    labels = P(("dp", "fsdp"))
    first = P("fsdp", "dp")
    return jax.shard_map(
        per_device,
        mesh=mesh,
        in_specs=(rows, rows, labels, labels, P("fsdp", None), first, first, first, rows, rows, rows),
        out_specs=(rows, first, first, first, rows, rows, rows),
        check_vma=False,
    )
```
